32 devices in a mesh: dp: 32 (over z, y, x, core).
Axes of the slice: x: 2, y: 2, z: 4, core: 2. Of those that a mesh axis runs over, the one named last changes fastest.
Arguments:
- hidden: bfloat16 [14592, 768], P('dp'), may hold values from -6 to 6
- region_count: int32 [64], P('dp'), may hold values from 10 to 100
- text_mask: int32 [64, 128], P('dp'), may hold values 0 or 1
- q_weight: bfloat16 [2, 768, 768], P(None, 'dp'), may hold values from -0.21875 to 0.21875
- k_weight: bfloat16 [2, 768, 768], P(None, 'dp'), may hold values from -0.21875 to 0.21875
- v_weight: bfloat16 [2, 768, 768], P(None, 'dp'), may hold values from -0.21875 to 0.21875
- o_weight: bfloat16 [2, 768, 768], P(None, 'dp'), may hold values from -0.75 to 0.75
- q_bias: bfloat16 [2, 768], P(None, 'dp'), may hold values from -3 to 3
- v_bias: bfloat16 [2, 768], P(None, 'dp'), may hold values from -3 to 3
- o_bias: bfloat16 [2, 768], P(None, 'dp'), may hold values from -3 to 3
- gain_one: bfloat16 [2, 768], P(None, 'dp'), may hold values from 0.099609375 to 1.8984375
- shift_one: bfloat16 [2, 768], P(None, 'dp'), may hold values from -3 to 3
- up_weight: bfloat16 [2, 768, 3072], P(None, 'dp'), may hold values from -0.21875 to 0.21875
- up_bias: bfloat16 [2, 3072], P(None, 'dp'), may hold values from -3 to 3
- down_weight: bfloat16 [2, 3072, 768], P(None, 'dp'), may hold values from -0.109375 to 0.109375
- down_bias: bfloat16 [2, 768], P(None, 'dp'), may hold values from -3 to 3
- gain_two: bfloat16 [2, 768], P(None, 'dp'), may hold values from 0.099609375 to 1.8984375
- shift_two: bfloat16 [2, 768], P(None, 'dp'), may hold values from -3 to 3
- cotangent: bfloat16 [14592, 768], P('dp'), may hold values from -6 to 6
Outputs:
- layer_output: bfloat16 [14592, 768], P('dp')
- hidden_grad: float32 [14592, 768], P('dp')
- q_weight_grad: float32 [2, 768, 768], P(None, 'dp')
- k_weight_grad: float32 [2, 768, 768], P(None, 'dp')
- v_weight_grad: float32 [2, 768, 768], P(None, 'dp')
- o_weight_grad: float32 [2, 768, 768], P(None, 'dp')
- q_bias_grad: float32 [2, 768], P(None, 'dp')
- v_bias_grad: float32 [2, 768], P(None, 'dp')
- o_bias_grad: float32 [2, 768], P(None, 'dp')
- gain_one_grad: float32 [2, 768], P(None, 'dp')
- shift_one_grad: float32 [2, 768], P(None, 'dp')
- up_weight_grad: float32 [2, 768, 3072], P(None, 'dp')
- up_bias_grad: float32 [2, 3072], P(None, 'dp')
- down_weight_grad: float32 [2, 3072, 768], P(None, 'dp')
- down_bias_grad: float32 [2, 768], P(None, 'dp')
- gain_two_grad: float32 [2, 768], P(None, 'dp')
- shift_two_grad: float32 [2, 768], P(None, 'dp')
The draws below stay inside these ranges and needn't reach their ends.
Inputs may be any that keep to these rules, and one draw needn't show every extreme that they name: `region_count`: region slots at or after an item's count are masked as keys.
All inputs are finite; a program needn't handle non-finite values. No bound on the sum of `text_mask` on one device may be relied on, other than what follows from the above.
Results may differ from the reference program's by a relative error of at most 0.03.
Values may be sent and summed in bfloat16 or wider, within the bound.
No kernel may reach another device: no remote copies, remote signals or barrier semaphores. Data moves between devices by JAX's collectives and lax.ppermute only.
A program may use at most 256 MiB of HBM per device.

```python
import jax
import jax.numpy as jnp
from jax import lax

D = 768
HEADS = 12
HEAD_DIM = 64
FF = 3072
TEXT = 128
REGIONS = 100
LAYERS = 2
ITEMS_DEV = 2
SEQ = 228
ITEMS = 64
TOKENS = 14592


def touch_ends(array, stream_key, smallest, largest):
    extent = array.shape
    index_at = [jax.random.randint(jax.random.fold_in(stream_key, axis), (), 0, extent[axis]) for axis in range(len(extent))]
    array = array.at[tuple(index_at)].set(smallest)
    longest = extent.index(max(extent))
    index_at[longest] = (index_at[longest] + 1) % extent[longest]
    return array.at[tuple(index_at)].set(largest)


def shard_levels(key, shape, split, smallest, high):
    loudness = 1.0
    for axis_at, parts in split:
        steps = jax.random.uniform(jax.random.fold_in(jax.random.fold_in(key, 6), axis_at), (parts,), jnp.float32, smallest / len(split), high / len(split))
        loudness = loudness * jnp.repeat(jnp.exp(steps), shape[axis_at] // parts).reshape((-1,) + (1,) * (len(shape) - 1 - axis_at))
    return loudness


def scatter_about(rng, extent, scale, limit, shards=(), held_as=jnp.bfloat16):
    drawn = jax.random.normal(rng, extent, jnp.float32) * scale
    if len(shards) > 0:
        drawn = shard_levels(rng, extent, shards, -0.22, 0.18) * drawn
    return jnp.clip(drawn, min=-limit, max=limit).astype(held_as)


def setup_inputs(seed: int = 0) -> dict:
    streams_of = jax.random.split(jax.random.key(seed), 20)
    return {
        "hidden": scatter_about(streams_of[0], (TOKENS, D), 1.0, 6.0, ((0, 32),)),
        "region_count": touch_ends(jax.random.randint(streams_of[1], (ITEMS,), max(1, REGIONS // 10), REGIONS + 1), jax.random.fold_in(streams_of[1], 1), max(1, REGIONS // 10), REGIONS).astype(jnp.int32),
        "text_mask": touch_ends((jax.random.randint(streams_of[2], (ITEMS, TEXT), 0, 8) < 7).astype(jnp.int32), jax.random.fold_in(streams_of[2], 1), 0, 1),
        "q_weight": scatter_about(streams_of[3], (LAYERS, D, D), D ** -0.5, 0.21875, ((1, 32),)),
        "k_weight": scatter_about(streams_of[4], (LAYERS, D, D), D ** -0.5, 0.21875, ((1, 32),)),
        "v_weight": scatter_about(streams_of[5], (LAYERS, D, D), D ** -0.5, 0.21875, ((1, 32),)),
        "o_weight": scatter_about(streams_of[6], (LAYERS, D, D), (D // 12) ** -0.5, 0.75, ((1, 32),)),
        "q_bias": scatter_about(streams_of[7], (LAYERS, D), 0.5, 3.0, ((1, 32),)),
        "v_bias": scatter_about(streams_of[8], (LAYERS, D), 0.5, 3.0, ((1, 32),)),
        "o_bias": scatter_about(streams_of[9], (LAYERS, D), 0.5, 3.0, ((1, 32),)),
        "gain_one": jnp.clip(1.0 + 0.18 * jax.random.normal(streams_of[10], (LAYERS, D), jnp.float32), 0.099609375, 1.8984375).astype(jnp.bfloat16),
        "shift_one": scatter_about(streams_of[11], (LAYERS, D), 0.5, 3.0, ((1, 32),)),
        "up_weight": scatter_about(streams_of[12], (LAYERS, D, FF), D ** -0.5, 0.21875, ((1, 32),)),
        "up_bias": scatter_about(streams_of[13], (LAYERS, FF), 0.5, 3.0, ((1, 32),)),
        "down_weight": scatter_about(streams_of[14], (LAYERS, FF, D), FF ** -0.5, 0.109375, ((1, 32),)),
        "down_bias": scatter_about(streams_of[15], (LAYERS, D), 0.5, 3.0, ((1, 32),)),
        "gain_two": jnp.clip(1.0 + 0.18 * jax.random.normal(streams_of[16], (LAYERS, D), jnp.float32), 0.099609375, 1.8984375).astype(jnp.bfloat16),
        "shift_two": scatter_about(streams_of[17], (LAYERS, D), 0.5, 3.0, ((1, 32),)),
        "cotangent": scatter_about(streams_of[18], (TOKENS, D), 1.0, 6.0, ((0, 32),)),
    }


@jax.custom_vjp
def low(v):
    return lax.optimization_barrier(v.astype(jnp.bfloat16)).astype(jnp.float32)

@jax.custom_vjp
def low_back(v):
    return v

def low_keep(v):
    return (low(v), None)

def low_pass(kept, grad):
    return (grad,)

def back_keep(v):
    return (v, None)

def back_low(kept, grad):
    return (low(grad),)
low.defvjp(low_keep, low_pass)
low_back.defvjp(back_keep, back_low)
epsilon = 1e-12
highest = lax.Precision.HIGHEST

def layer_norm(values, gain, shift):
    center = values - lax.optimization_barrier(jnp.mean(values, axis=-1, keepdims=True))
    spread = lax.optimization_barrier(jnp.mean(center * center, axis=-1, keepdims=True))
    return center * lax.rsqrt(spread + epsilon) * gain + shift

def slot_valid(region_count, text_mask):
    region_slot = jnp.arange(REGIONS, dtype=jnp.int32)[None, :] < region_count[:, None]
    return jnp.concatenate([text_mask.astype(jnp.float32), region_slot.astype(jnp.float32)], axis=1)

def matmul(left, right):
    return jnp.dot(left, right, precision=highest)

def attend_items(packed):
    queries, key_rows, value_rows, valid_keys = packed
    scores = jnp.einsum('bqhd,bkhd->bhqk', queries, key_rows, precision=highest) * 0.125
    scores = low_back(scores + (valid_keys[:, None, None, :] - 1.0) * 10000.0)
    attention = low(jax.nn.softmax(scores, axis=-1))
    return low_back(low(jnp.einsum('bhqk,bkhd->bqhd', attention, value_rows, precision=highest)))

def block(inputs, weights, valid_keys):
    q_weight, k_weight, v_weight, o_weight, q_bias, v_bias, o_bias, gain_one, shift_one, up_weight, up_bias, down_weight, down_bias, gain_two, shift_two = weights
    row_count = inputs.shape[0]
    groups = valid_keys.shape[0] // ITEMS_DEV

    def split_heads(values):
        return values.reshape(groups, ITEMS_DEV, SEQ, HEADS, HEAD_DIM)
    queries = low_back(low(matmul(inputs, q_weight) + q_bias))
    key_rows = low_back(low(matmul(inputs, k_weight)))
    value_rows = low_back(low(matmul(inputs, v_weight) + v_bias))
    context = lax.map(jax.checkpoint(attend_items), (split_heads(queries), split_heads(key_rows), split_heads(value_rows), valid_keys.reshape(groups, ITEMS_DEV, SEQ)))
    context = context.reshape(row_count, HEADS * HEAD_DIM)
    attended = low_back(matmul(context, o_weight) + o_bias)
    middle = low(layer_norm(inputs + attended, gain_one, shift_one))
    lifted = low_back(matmul(middle, up_weight) + up_bias)
    activated = low(jax.nn.gelu(lifted, approximate=False))
    lowered = low_back(matmul(activated, down_weight) + down_bias)
    return low(layer_norm(middle + lowered, gain_two, shift_two))

def reference(hidden, region_count, text_mask, q_weight, k_weight, v_weight, o_weight, q_bias, v_bias, o_bias, gain_one, shift_one, up_weight, up_bias, down_weight, down_bias, gain_two, shift_two, cotangent):
    valid_keys = slot_valid(region_count, text_mask)
    params = tuple((weight.astype(jnp.float32) for weight in (q_weight, k_weight, v_weight, o_weight, q_bias, v_bias, o_bias, gain_one, shift_one, up_weight, up_bias, down_weight, down_bias, gain_two, shift_two)))

    def forward(inputs, *weights):
        for layer_index in range(LAYERS):
            inputs = block(inputs, tuple((weight[layer_index] for weight in weights)), valid_keys)
        return inputs
    output, pullback = jax.vjp(forward, hidden.astype(jnp.float32), *params)
    gradients = pullback(cotangent.astype(jnp.float32))
    return (output.astype(jnp.bfloat16), gradients[0], gradients[1], gradients[2], gradients[3], gradients[4], gradients[5], gradients[6], gradients[7], gradients[8], gradients[9], gradients[10], gradients[11], gradients[12], gradients[13], gradients[14], gradients[15])
```

```python
import functools
import math

import jax
import jax.numpy as jnp
from jax import lax
from jax.experimental import pallas as pl
from jax.experimental.pallas import tpu as pltpu
from jax.sharding import PartitionSpec as P

HEADS = 12
HEAD_DIM = 64
REGIONS = 100

epsilon = 1e-12
F32 = jnp.float32
BF16 = jnp.bfloat16


def rounds_of(owners):
    bits = int(math.log2(owners))
    outer = list(range(3, bits))
    return (outer + [1, 2, 0], outer + [2, 1, 0])


def swaps(owners, step):
    rounds = rounds_of(owners)
    return [(i, i ^ (1 << rounds[i % 2][step])) for i in range(owners)]


def owner_table(owners):
    rounds = rounds_of(owners)
    half = owners // 2
    masks = [
        [sum(((b >> j) & 1) << order[j] for j in range(len(order) - 1)) for b in range(half)]
        for order in rounds
    ]
    me = lax.axis_index("dp")
    core = me % 2
    even, odd = (jnp.array(m, dtype=jnp.int32) for m in masks)
    near = jnp.where(core == 0, even, odd) ^ me
    far = jnp.where(core == 0, odd, even) ^ (me ^ 1)
    return jnp.concatenate([near, far]).astype(jnp.int32)


def tie(value, earlier):
    if earlier is None:
        return value
    return lax.optimization_barrier((value, earlier))[0]


def swap(value, step, owners):
    return lax.ppermute(value, "dp", swaps(owners, step))


class Lane:
    def __init__(self, lag):
        self.lag = lag
        self.ends = []

    def enter(self, value):
        at = len(self.ends) - self.lag
        return tie(value, self.ends[at] if at >= 0 else None)

    def leave(self, value):
        self.ends.append(value)


def gather_piece(shard, owners, lanes):
    steps = int(math.log2(owners)) - 1
    held = shard[None]
    for step in range(steps):
        if step == 0:
            held = lanes[0].enter(held)
        if step == steps - 2:
            held = lanes[1].enter(held)
        came = swap(held, step, owners)
        if step == steps - 3:
            lanes[0].leave(came)
        if step == steps - 1:
            lanes[1].leave(came)
        held = jnp.concatenate([held, came], axis=0)
    return held, swap(held, steps, owners)


def scatter_piece(blocks, owners, lanes):
    steps = int(math.log2(owners))
    held = blocks
    for step in reversed(range(steps)):
        half = held.shape[0] // 2
        if step == steps - 2:
            held = lanes[0].enter(held)
        if step == steps - 4:
            held = lanes[1].enter(held)
        came = swap(held[half:], step, owners)
        if step == steps - 3:
            lanes[0].leave(came)
        if step == 0:
            lanes[1].leave(came)
        held = held[:half].astype(F32) + came.astype(F32)
        if step > 0:
            held = held.astype(BF16)
    return held[0]


def place_kernel(table, *refs, scatter):
    parts, out, sem = refs[:-2], refs[-2], refs[-1]
    copies = []
    b = 0
    for part in parts:
        for j in range(out.shape[0] if scatter else part.shape[0]):
            at = table[b]
            if scatter:
                copies.append(pltpu.make_async_copy(part.at[at], out.at[b], sem.at[b]))
            else:
                copies.append(pltpu.make_async_copy(part.at[j], out.at[at], sem.at[b]))
            copies[-1].start()
            b += 1
    for copy in copies:
        copy.wait()


def place(table, parts, scatter=False):
    owners = table.shape[0]
    shape = (owners,) + parts[0].shape[1:]
    return pl.pallas_call(
        functools.partial(place_kernel, scatter=scatter),
        out_shape=jax.ShapeDtypeStruct(shape, parts[0].dtype),
        in_specs=[pl.BlockSpec(memory_space=pltpu.SMEM)]
        + [pl.BlockSpec(memory_space=pl.ANY)] * len(parts),
        out_specs=pl.BlockSpec(memory_space=pl.ANY),
        scratch_shapes=[pltpu.SemaphoreType.DMA((owners,))],
        cost_estimate=pl.CostEstimate(
            flops=0, bytes_accessed=2 * math.prod(shape) * 2, transcendentals=0
        ),
    )(table, *parts)


def dense(left, right):
    return jnp.dot(left, right, preferred_element_type=F32)


def outer(left, right):
    return lax.dot_general(left, right, (((0,), (0,)), ((), ())), preferred_element_type=F32)


def back_dense(left, right):
    return lax.dot_general(left, right, (((1,), (1,)), ((), ())), preferred_element_type=F32)


def column_sum(values):
    return jnp.sum(values.astype(F32), axis=0)


def slot_valid(region_count, text_mask):
    region_slot = jnp.arange(REGIONS, dtype=jnp.int32)[None, :] < region_count[:, None]
    return jnp.concatenate([text_mask.astype(F32), region_slot.astype(F32)], axis=1)


def norm(values, gain, shift):
    center = values - jnp.mean(values, axis=-1, keepdims=True)
    spread = jnp.mean(center * center, axis=-1, keepdims=True)
    scale = lax.rsqrt(spread + epsilon)
    unit = center * scale
    return unit * gain + shift, (unit, scale)


def norm_back(saved, gain, grad):
    unit, scale = saved
    inner = grad * gain
    into = scale * (
        inner
        - jnp.mean(inner, axis=-1, keepdims=True)
        - unit * jnp.mean(inner * unit, axis=-1, keepdims=True)
    )
    return into, column_sum(grad * unit), column_sum(grad)


def forward_layer(inputs, weights, vectors, valid_keys):
    q_weight, k_weight, v_weight, o_weight, up_weight, down_weight = weights
    q_bias, v_bias, o_bias, gain_one, shift_one, up_bias, down_bias, gain_two, shift_two = vectors
    item_count = valid_keys.shape[0]
    row_count, width = inputs.shape

    def heads_of(values):
        return values.reshape(item_count, row_count // item_count, HEADS, HEAD_DIM)

    queries = heads_of((dense(inputs, q_weight) + q_bias).astype(BF16))
    key_rows = heads_of(dense(inputs, k_weight).astype(BF16))
    value_rows = heads_of((dense(inputs, v_weight) + v_bias).astype(BF16))
    scores = (
        jnp.einsum("bqhd,bkhd->bhqk", queries, key_rows, preferred_element_type=F32) * 0.125
    )
    scores = scores + (valid_keys[:, None, None, :] - 1.0) * 10000.0
    attention = jax.nn.softmax(scores, axis=-1)
    attention_low = attention.astype(BF16)
    context = jnp.einsum("bhqk,bkhd->bqhd", attention_low, value_rows, preferred_element_type=F32)
    context = context.astype(BF16).reshape(row_count, width)
    first_sum = inputs.astype(F32) + dense(context, o_weight) + o_bias
    middle, norm_one = norm(first_sum, gain_one, shift_one)
    middle = middle.astype(BF16)
    lifted = dense(middle, up_weight) + up_bias
    half = 0.5 * lax.erf(lifted * math.sqrt(0.5)) + 0.5
    activated = (lifted * half).astype(BF16)
    slope = half + lifted * jnp.exp(-0.5 * lifted * lifted) * (1.0 / math.sqrt(2.0 * math.pi))
    slope = slope.astype(BF16)
    second_sum = middle.astype(F32) + dense(activated, down_weight) + down_bias
    output, norm_two = norm(second_sum, gain_two, shift_two)
    saved = (queries, key_rows, value_rows, attention, attention_low, context, norm_one, middle, slope, activated, norm_two)
    return output.astype(BF16), saved


def backward_layer(inputs, weights, vectors, saved, out_grad, send):
    q_weight, k_weight, v_weight, o_weight, up_weight, down_weight = weights
    q_bias, v_bias, o_bias, gain_one, shift_one, up_bias, down_bias, gain_two, shift_two = vectors
    queries, key_rows, value_rows, attention, attention_low, context, norm_one, middle, slope, activated, norm_two = saved
    row_count, width = inputs.shape
    sum_grad, gain_two_grad, shift_two_grad = norm_back(norm_two, gain_two, out_grad)
    lowered_grad = sum_grad.astype(BF16)
    send("down", [outer(activated, lowered_grad)])
    lifted_grad = (back_dense(lowered_grad, down_weight) * slope).astype(BF16)
    send("up", [outer(middle, lifted_grad)])
    middle_grad = sum_grad + back_dense(lifted_grad, up_weight)
    first_grad, gain_one_grad, shift_one_grad = norm_back(norm_one, gain_one, middle_grad)
    attended_grad = first_grad.astype(BF16)
    o_grad = outer(context, attended_grad)
    context_grad = back_dense(attended_grad, o_weight).astype(BF16).reshape(queries.shape)
    attention_grad = jnp.einsum(
        "bqhd,bkhd->bhqk", context_grad, value_rows, preferred_element_type=F32
    )
    value_grad = jnp.einsum(
        "bhqk,bqhd->bkhd", attention_low, context_grad, preferred_element_type=F32
    )
    value_grad = value_grad.astype(BF16).reshape(row_count, width)
    weighed = attention * attention_grad
    score_grad = (weighed - attention * jnp.sum(weighed, axis=-1, keepdims=True)).astype(BF16)
    query_grad = (
        jnp.einsum("bhqk,bkhd->bqhd", score_grad, key_rows, preferred_element_type=F32) * 0.125
    )
    query_grad = query_grad.astype(BF16).reshape(row_count, width)
    key_grad = (
        jnp.einsum("bhqk,bqhd->bkhd", score_grad, queries, preferred_element_type=F32) * 0.125
    )
    key_grad = key_grad.astype(BF16).reshape(row_count, width)
    send("four", [outer(inputs, query_grad), outer(inputs, key_grad), outer(inputs, value_grad), o_grad])
    input_grad = (
        first_grad
        + back_dense(query_grad, q_weight)
        + back_dense(key_grad, k_weight)
        + back_dense(value_grad, v_weight)
    )
    small = (column_sum(query_grad), column_sum(value_grad), column_sum(attended_grad), gain_one_grad, shift_one_grad, column_sum(lifted_grad), column_sum(lowered_grad), gain_two_grad, shift_two_grad)
    return input_grad, small


def shards(
    hidden, region_count, text_mask,
    q_weight, k_weight, v_weight, o_weight, q_bias, v_bias, o_bias, gain_one, shift_one,
    up_weight, up_bias, down_weight, down_bias, gain_two, shift_two, cotangent,
):
    owners = lax.axis_size("dp")
    layers = q_weight.shape[0]
    valid_keys = slot_valid(region_count, text_mask)
    doubling = owners >= 16 and owners & (owners - 1) == 0 and q_weight.shape[1] % 8 == 0
    table = owner_table(owners) if doubling else None

    small = (q_bias, v_bias, o_bias, gain_one, shift_one, up_bias, down_bias, gain_two, shift_two)
    packed = jnp.concatenate([v.reshape(1, -1) for v in small], axis=1)
    packed = lax.all_gather(packed, "dp", axis=0, tiled=True).astype(F32)
    vectors = []
    offset = 0
    for v in small:
        size = v.shape[0] * v.shape[1]
        part = packed[:, offset : offset + size].reshape((owners,) + v.shape)
        vectors.append(jnp.swapaxes(part, 0, 1).reshape(layers, -1))
        offset += size
    vectors = [tuple(v[layer] for v in vectors) for layer in range(layers)]

    def whole(blocks):
        return blocks.reshape((-1, blocks.shape[-1]))

    lanes = (Lane(3), Lane(3))
    gathered = []
    for layer in range(layers):
        four = [w[layer] for w in (q_weight, k_weight, v_weight, o_weight)]
        if not doubling:
            gathered.append(
                tuple(
                    lax.all_gather(w, "dp", axis=0, tiled=True)
                    for w in four + [up_weight[layer], down_weight[layer]]
                )
            )
            continue
        rows = four[0].shape[0]
        near, far = gather_piece(jnp.stack(four), owners, lanes)
        fours = [place(table, [near[:, i], far[:, i]]) for i in range(4)]
        up = place(table, list(gather_piece(up_weight[layer], owners, lanes)))
        down = place(table, list(gather_piece(down_weight[layer], owners, lanes)))
        gathered.append(tuple(whole(w) for w in fours + [up, down]))

    current = hidden
    inputs, saved = [], []
    for layer in range(layers):
        inputs.append(current)
        current, kept = forward_layer(current, gathered[layer], vectors[layer], valid_keys)
        saved.append(kept)
    flowing = cotangent.astype(F32)
    lanes = (Lane(2), Lane(2))
    big = [{} for _ in range(layers)]
    tiny = [None] * layers
    for layer in reversed(range(layers)):

        def send(name, grads, layer=layer):
            lows = [g.astype(BF16).reshape(owners, -1, g.shape[-1]) for g in grads]
            if not doubling:
                big[layer][name] = [
                    lax.psum_scatter(g, "dp", scatter_dimension=0, tiled=True)[0].astype(F32)
                    for g in lows
                ]
                return
            lows = [place(table, [g], scatter=True) for g in lows]
            rows = lows[0].shape[1]
            mine = scatter_piece(jnp.concatenate(lows, axis=1) if len(lows) > 1 else lows[0], owners, lanes)
            big[layer][name] = [mine[i * rows : (i + 1) * rows] for i in range(len(lows))]

        flowing, tiny[layer] = backward_layer(
            inputs[layer], gathered[layer], vectors[layer], saved[layer], flowing, send
        )
    sizes = [v.shape[1] for v in small]
    flat = jnp.concatenate(
        [g.reshape(owners, -1) for layer in range(layers) for g in tiny[layer]], axis=1
    )
    flat = lax.psum_scatter(flat, "dp", scatter_dimension=0, tiled=True).reshape(layers, -1)
    summed = []
    offset = 0
    for size in sizes:
        summed.append(flat[:, offset : offset + size])
        offset += size
    q_b, v_b, o_b, g_one, s_one, u_b, d_b, g_two, s_two = summed
    fours = [jnp.stack([big[layer]["four"][i] for layer in range(layers)]) for i in range(4)]
    up = jnp.stack([big[layer]["up"][0] for layer in range(layers)])
    down = jnp.stack([big[layer]["down"][0] for layer in range(layers)])
    return (
        current, flowing, fours[0], fours[1], fours[2], fours[3],
        q_b, v_b, o_b, g_one, s_one, up, u_b, down, d_b, g_two, s_two,
    )


def solution(mesh):
    rows = P("dp", None)
    matrix = P(None, "dp", None)
    vector = P(None, "dp")
    four = (matrix,) * 4
    return jax.shard_map(
        shards,
        mesh=mesh,
        in_specs=(rows, P("dp"), rows) + four + (vector,) * 5
        + (matrix, vector, matrix, vector, vector, vector, rows),
        out_specs=(rows, rows) + four + (vector,) * 5
        + (matrix, vector, matrix, vector, vector, vector),
        check_vma=False,
    )
```

```python
import functools
import math

import jax
import jax.numpy as jnp
from jax import lax
from jax.experimental import pallas as pl
from jax.experimental.pallas import tpu as pltpu
from jax.sharding import PartitionSpec as P

HEADS = 12
HEAD_DIM = 64
REGIONS = 100

epsilon = 1e-12
F32 = jnp.float32
BF16 = jnp.bfloat16


def dense(left, right):
    return jnp.dot(left, right, preferred_element_type=F32)


def outer(left, right):
    return lax.dot_general(left, right, (((0,), (0,)), ((), ())), preferred_element_type=F32)


def back_dense(left, right):
    return lax.dot_general(left, right, (((1,), (1,)), ((), ())), preferred_element_type=F32)


def column_sum(values):
    return jnp.sum(values.astype(F32), axis=0)


def slot_valid(region_count, text_mask):
    region_slot = jnp.arange(REGIONS, dtype=jnp.int32)[None, :] < region_count[:, None]
    return jnp.concatenate([text_mask.astype(F32), region_slot.astype(F32)], axis=1)


def norm(values, gain, shift):
    center = values - jnp.mean(values, axis=-1, keepdims=True)
    spread = jnp.mean(center * center, axis=-1, keepdims=True)
    scale = lax.rsqrt(spread + epsilon)
    unit = center * scale
    return unit * gain + shift, (unit, scale)


def norm_back(saved, gain, grad):
    unit, scale = saved
    inner = grad * gain
    into = scale * (
        inner
        - jnp.mean(inner, axis=-1, keepdims=True)
        - unit * jnp.mean(inner * unit, axis=-1, keepdims=True)
    )
    return into, column_sum(grad * unit), column_sum(grad)


def forward_layer(inputs, weights, vectors, valid_keys):
    q_weight, k_weight, v_weight, o_weight, up_weight, down_weight = weights
    q_bias, v_bias, o_bias, gain_one, shift_one, up_bias, down_bias, gain_two, shift_two = vectors
    item_count = valid_keys.shape[0]
    row_count, width = inputs.shape

    def heads_of(values):
        return values.reshape(item_count, row_count // item_count, HEADS, HEAD_DIM)

    queries = heads_of((dense(inputs, q_weight) + q_bias).astype(BF16))
    key_rows = heads_of(dense(inputs, k_weight).astype(BF16))
    value_rows = heads_of((dense(inputs, v_weight) + v_bias).astype(BF16))
    scores = (
        jnp.einsum("bqhd,bkhd->bhqk", queries, key_rows, preferred_element_type=F32) * 0.125
    )
    scores = scores + (valid_keys[:, None, None, :] - 1.0) * 10000.0
    attention = jax.nn.softmax(scores, axis=-1)
    attention_low = attention.astype(BF16)
    context = jnp.einsum("bhqk,bkhd->bqhd", attention_low, value_rows, preferred_element_type=F32)
    context = context.astype(BF16).reshape(row_count, width)
    first_sum = inputs.astype(F32) + dense(context, o_weight) + o_bias
    middle, norm_one = norm(first_sum, gain_one, shift_one)
    middle = middle.astype(BF16)
    lifted = dense(middle, up_weight) + up_bias
    half = 0.5 * lax.erf(lifted * math.sqrt(0.5)) + 0.5
    activated = (lifted * half).astype(BF16)
    slope = half + lifted * jnp.exp(-0.5 * lifted * lifted) * (1.0 / math.sqrt(2.0 * math.pi))
    slope = slope.astype(BF16)
    second_sum = middle.astype(F32) + dense(activated, down_weight) + down_bias
    output, norm_two = norm(second_sum, gain_two, shift_two)
    saved = (queries, key_rows, value_rows, attention, attention_low, context, norm_one, middle, slope, activated, norm_two)
    return output.astype(BF16), saved


def backward_layer(inputs, weights, vectors, saved, out_grad, send):
    q_weight, k_weight, v_weight, o_weight, up_weight, down_weight = weights
    q_bias, v_bias, o_bias, gain_one, shift_one, up_bias, down_bias, gain_two, shift_two = vectors
    queries, key_rows, value_rows, attention, attention_low, context, norm_one, middle, slope, activated, norm_two = saved
    row_count, width = inputs.shape
    sum_grad, gain_two_grad, shift_two_grad = norm_back(norm_two, gain_two, out_grad)
    lowered_grad = sum_grad.astype(BF16)
    send("down", [outer(activated, lowered_grad)])
    lifted_grad = (back_dense(lowered_grad, down_weight) * slope).astype(BF16)
    send("up", [outer(middle, lifted_grad)])
    middle_grad = sum_grad + back_dense(lifted_grad, up_weight)
    first_grad, gain_one_grad, shift_one_grad = norm_back(norm_one, gain_one, middle_grad)
    attended_grad = first_grad.astype(BF16)
    o_grad = outer(context, attended_grad)
    context_grad = back_dense(attended_grad, o_weight).astype(BF16).reshape(queries.shape)
    attention_grad = jnp.einsum(
        "bqhd,bkhd->bhqk", context_grad, value_rows, preferred_element_type=F32
    )
    value_grad = jnp.einsum(
        "bhqk,bqhd->bkhd", attention_low, context_grad, preferred_element_type=F32
    )
    value_grad = value_grad.astype(BF16).reshape(row_count, width)
    weighed = attention * attention_grad
    score_grad = (weighed - attention * jnp.sum(weighed, axis=-1, keepdims=True)).astype(BF16)
    query_grad = (
        jnp.einsum("bhqk,bkhd->bqhd", score_grad, key_rows, preferred_element_type=F32) * 0.125
    )
    query_grad = query_grad.astype(BF16).reshape(row_count, width)
    key_grad = (
        jnp.einsum("bhqk,bqhd->bkhd", score_grad, queries, preferred_element_type=F32) * 0.125
    )
    key_grad = key_grad.astype(BF16).reshape(row_count, width)
    send("four", [outer(inputs, query_grad), outer(inputs, key_grad), outer(inputs, value_grad), o_grad])
    input_grad = (
        first_grad
        + back_dense(query_grad, q_weight)
        + back_dense(key_grad, k_weight)
        + back_dense(value_grad, v_weight)
    )
    small = (column_sum(query_grad), column_sum(value_grad), column_sum(attended_grad), gain_one_grad, shift_one_grad, column_sum(lifted_grad), column_sum(lowered_grad), gain_two_grad, shift_two_grad)
    return input_grad, small


def plain(weights, small, valid_keys, hidden, cotangent):
    owners = lax.axis_size("dp")
    layers = weights[0].shape[0]
    packed = jnp.concatenate([v.reshape(1, -1) for v in small], axis=1)
    packed = lax.all_gather(packed, "dp", axis=0, tiled=True).astype(F32)
    vectors = []
    offset = 0
    for v in small:
        size = v.shape[0] * v.shape[1]
        part = packed[:, offset : offset + size].reshape((owners,) + v.shape)
        vectors.append(jnp.swapaxes(part, 0, 1).reshape(layers, -1))
        offset += size
    vectors = [tuple(v[layer] for v in vectors) for layer in range(layers)]
    gathered = [
        tuple(lax.all_gather(w[layer], "dp", axis=0, tiled=True) for w in weights)
        for layer in range(layers)
    ]
    current = hidden
    inputs, saved = [], []
    for layer in range(layers):
        inputs.append(current)
        current, kept = forward_layer(current, gathered[layer], vectors[layer], valid_keys)
        saved.append(kept)
    flowing = cotangent.astype(F32)
    big = [{} for _ in range(layers)]
    tiny = [None] * layers
    for layer in reversed(range(layers)):

        def send(name, grads, layer=layer):
            big[layer][name] = [
                lax.psum_scatter(g.astype(BF16).reshape(owners, -1, g.shape[-1]), "dp", scatter_dimension=0, tiled=True)[0].astype(F32)
                for g in grads
            ]

        flowing, tiny[layer] = backward_layer(
            inputs[layer], gathered[layer], vectors[layer], saved[layer], flowing, send
        )
    flat = jnp.concatenate(
        [g.reshape(owners, -1) for layer in range(layers) for g in tiny[layer]], axis=1
    )
    flat = lax.psum_scatter(flat, "dp", scatter_dimension=0, tiled=True).reshape(layers, -1)
    summed = []
    offset = 0
    for v in small:
        summed.append(flat[:, offset : offset + v.shape[1]])
        offset += v.shape[1]
    q_b, v_b, o_b, g_one, s_one, u_b, d_b, g_two, s_two = summed
    fours = [jnp.stack([big[layer]["four"][i] for layer in range(layers)]) for i in range(4)]
    up = jnp.stack([big[layer]["up"][0] for layer in range(layers)])
    down = jnp.stack([big[layer]["down"][0] for layer in range(layers)])
    return (
        current, flowing, *fours,
        q_b, v_b, o_b, g_one, s_one, up, u_b, down, d_b, g_two, s_two,
    )


ITEM = 256
PAD = -1e30


def table_of(owners):
    chips = owners // 2
    depth = chips // 4
    me = lax.axis_index("dp")
    chip, core = me // 2, me % 2
    walk = jnp.arange(chips, dtype=jnp.int32)

    def chip_at(position, core):
        z, first, second = position % depth, position // depth % 2, position // (2 * depth)
        return chip ^ (z * 4 + jnp.where(core == 0, second * 2 + first, first * 2 + second))

    def place_of(other, core):
        z, y, x = (other ^ chip) // 4, (other ^ chip) // 2 % 2, (other ^ chip) % 2
        return z + depth * jnp.where(core == 0, x + 2 * y, y + 2 * x)

    return jnp.concatenate(
        [chip_at(walk, core), chip_at(walk, 1 - core), place_of(walk, core), place_of(walk, 1 - core), core[None]]
    ).astype(jnp.int32)


def flip(value, owners, even, odd):
    return lax.ppermute(value, "dp", [(i, i ^ (odd if i % 2 else even)) for i in range(owners)])


MICROS = {
    "attend_forward": 18, "lift": 13, "lower": 9, "lower_back": 6, "lift_back": 15, "attend_back_first": 13,
    "attend_back_second": 10, "attend_back_third": 5, "attend_back_last": 6,
}


def padded_bytes(shape, dtype):
    *lead, rows, columns = (1,) * max(0, 2 - len(shape)) + tuple(shape)
    return math.prod(lead) * (-(-rows // 16) * 16) * (-(-columns // 128) * 128) * jnp.dtype(dtype).itemsize


def launch(body, outs, smem=(), vmem=(), hbm=(), deps=(), scratch=(), extra=3):
    counts = (len(smem), len(vmem), len(hbm), len(deps), len(outs))
    name = getattr(body, "func", body).__name__
    micros = MICROS.get(name, 2)
    held = [(v.shape, v.dtype) for v in vmem] + list(outs)
    held += [(v.shape, v.dtype) for v in scratch if jnp.issubdtype(v.dtype, jnp.floating)]
    limit = extra * 2**20 + sum(padded_bytes(shape, dtype) for shape, dtype in held)

    def kernel(*refs):
        groups, at = [], 0
        for count in counts:
            groups.append(refs[at : at + count])
            at += count
        body(groups[0], groups[1], groups[2], groups[4], refs[at:])

    in_specs = (
        [pl.BlockSpec(memory_space=pltpu.SMEM)] * len(smem)
        + [pl.BlockSpec(memory_space=pltpu.VMEM)] * len(vmem)
        + [pl.BlockSpec(memory_space=pl.ANY)] * (len(hbm) + len(deps))
    )
    return pl.pallas_call(
        kernel,
        out_shape=[jax.ShapeDtypeStruct(s, d) for s, d in outs],
        in_specs=in_specs,
        out_specs=[pl.BlockSpec(memory_space=pltpu.VMEM)] * len(outs),
        scratch_shapes=list(scratch),
        name=name,
        compiler_params=pltpu.CompilerParams(vmem_limit_bytes=limit),
        cost_estimate=pl.CostEstimate(
            flops=int(micros * 1e9), bytes_accessed=int(micros * 3e6), transcendentals=0
        ),
    )(*smem, *vmem, *hbm, *deps)


def mm(left, right):
    return jnp.dot(left, right, preferred_element_type=F32)


def mm_nt(left, right):
    return lax.dot_general(left, right, (((1,), (1,)), ((), ())), preferred_element_type=F32)


def mm_tn(left, right):
    return lax.dot_general(left, right, (((0,), (0,)), ((), ())), preferred_element_type=F32)


def fetch(tab, parts, whole, sems, columns=None):
    near, near_more, far, far_more = parts
    half, rows = near.shape[0], near.shape[1]
    core = tab[8 * half]
    start, stop = (0, near.shape[2]) if columns is None else columns
    step = (stop - start) // 3 if (stop - start) % 384 == 0 and rows > 128 else (768 if (stop - start) % 768 == 0 else 384)
    copies = []
    for side, group in enumerate(((near, near_more), (far, far_more))):
        hand = core if side == 0 else 1 - core
        for which, part in enumerate(group):
            for b in range(half):
                chip = tab[(2 * side + which) * half + b]
                for at in range(start, stop, step):
                    source = part.at[b, :, pl.ds(at, step)]
                    to = pl.ds(pl.multiple_of(chip * rows, 16), rows)
                    target = whole.at[hand, to, pl.ds(at - start, step)]
                    copies.append(pltpu.make_async_copy(source, target, sems.at[len(copies)]))
                    copies[-1].start()
    return copies


def fetch_packed(tab, parts, kind, whole, sems, columns=None):
    near, far = parts
    chips, rows = near.shape[0], near.shape[1] // 3
    core = tab[4 * chips]
    copies = []

    def move(source, target):
        copies.append(pltpu.make_async_copy(source, target, sems.at[len(copies)]))
        copies[-1].start()

    for part, hand in ((near, core), (far, 1 - core)):
        for chip in range(chips):
            if kind == "down":
                wide = whole.shape[2]
                for g in range(4):
                    source = part.at[chip, pl.ds(2 * rows, rows), pl.ds(g * wide, wide)]
                    move(source, whole.at[hand, pl.ds((4 * chip + g) * rows, rows)])
                continue
            at = pl.ds(0 if kind == "four" else rows, rows)
            start, stop = (0, whole.shape[2]) if columns is None else columns
            step = (768 if (stop - start) % 768 == 0 else 384)
            for c in range(start, stop, step):
                source = part.at[chip, at, pl.ds(c, step)]
                move(source, whole.at[hand, pl.ds(chip * rows, rows), pl.ds(c - start, step)])
    return copies


def bring(tab, parts, kind, whole, sems, columns=None):
    if len(parts) == 2:
        return fetch_packed(tab, parts, kind, whole, sems, columns)
    return fetch(tab, parts, whole, sems, columns)


def finish(copies):
    for copy in copies:
        copy.wait()


def norm_rows(values):
    center = values - jnp.mean(values, axis=-1, keepdims=True)
    scale = lax.rsqrt(jnp.mean(center * center, axis=-1, keepdims=True) + epsilon)
    return center * scale, scale


def norm_rows_back(unit, scale, inner):
    return scale * (
        inner
        - jnp.mean(inner, axis=-1, keepdims=True)
        - unit * jnp.mean(inner * unit, axis=-1, keepdims=True)
    )


def gelu_and_slope(v):
    z = jnp.abs(v) * math.sqrt(0.5)
    t = 1.0 / (1.0 + 0.3275911 * z)
    bell = jnp.exp(-0.5 * v * v)
    poly = 0.5 * 1.061405429 * t - 0.5 * 1.453152027
    poly = poly * t + 0.5 * 1.421413741
    poly = poly * t - 0.5 * 0.284496736
    poly = poly * t + 0.5 * 0.254829592
    tail = poly * t * bell
    phi = jnp.where(v >= 0.0, 1.0 - tail, tail)
    return v * phi, phi + v * bell * (1.0 / math.sqrt(2.0 * math.pi))


Q_B, V_B, O_B, G_ONE, S_ONE, D_B, G_TWO, S_TWO, UP_B = range(9)


def split_own(smem, vmem, hbm, outs, scratch):
    (tab,) = smem
    core = tab[tab.shape[0] - 1]
    q, k, v, o, up, down = vmem
    layers = q.shape[0]
    for layer in range(layers):
        for place, hand in ((0, core), (1, 1 - core)):
            four, wide, tall = outs[6 * layer + 3 * place : 6 * layer + 3 * place + 3]
            part = q.shape[2] // 2
            at = pl.ds(pl.multiple_of(hand * part, 128), part)
            for i, w in enumerate((q, k, v, o)):
                four[:, i * part : (i + 1) * part] = w[layer, :, at]
            part = up.shape[2] // 2
            wide[...] = up[layer, :, pl.ds(pl.multiple_of(hand * part, 128), part)]
            part = down.shape[2] // 2
            tall[...] = down[layer, :, pl.ds(pl.multiple_of(hand * part, 128), part)]


def join_rows(smem, vmem, hbm, outs, scratch):
    (tab,) = smem
    first = tab[tab.shape[0] - 1] == 0
    for i, out in enumerate(outs):
        mine, came = vmem[2 * i][...].astype(F32), vmem[2 * i + 1][...].astype(F32)
        rows = mine.shape[0]
        upper = jnp.where(first, mine, came)
        lower = jnp.where(first, came, mine)
        out[...] = jnp.concatenate([upper, lower], axis=0).astype(out.dtype)


def join_blocks(smem, vmem, hbm, outs, scratch):
    (out,) = outs
    (sems,) = scratch
    at = 0
    copies = []
    for part in hbm:
        count = part.shape[0] if len(part.shape) == 3 else 1
        target = out.at[pl.ds(at, count)] if len(part.shape) == 3 else out.at[at]
        copies.append(pltpu.make_async_copy(part, target, sems.at[len(copies)]))
        copies[-1].start()
        at += count
    finish(copies)


def attend_forward(smem, vmem, hbm, outs, scratch):
    (tab,) = smem
    x, vec, mask = vmem
    q, k, v, p, context, unit, scale, middle = outs
    whole, sems = scratch
    finish(bring(tab, hbm, "four", whole, sems))
    half = x.shape[1] // 2
    for h in (0, 1):
        at = slice(h * half, (h + 1) * half)
        made = mm(x[...], whole[h, :, 0 : 3 * half])
        q[:, at] = (made[:, 0:half] + vec[Q_B : Q_B + 1, at]).astype(BF16)
        k[:, at] = made[:, half : 2 * half].astype(BF16)
        v[:, at] = (made[:, 2 * half :] + vec[V_B : V_B + 1, at]).astype(BF16)
    low = lax.broadcasted_iota(jnp.int32, (ITEM, 2 * HEAD_DIM), 1) < HEAD_DIM
    items = x.shape[0] // ITEM

    def pair(i, carry):
        at = pl.ds(pl.multiple_of(i * 2 * HEAD_DIM, 2 * HEAD_DIM), 2 * HEAD_DIM)
        for item in range(items):
            rows = slice(item * ITEM, (item + 1) * ITEM)
            qs, ks, vs = q[rows, at], k[rows, at], v[rows, at]
            made = []
            for side in (0, 1):
                own = low if side == 0 else jnp.logical_not(low)
                s = mm_nt(jnp.where(own, qs, jnp.zeros_like(qs)), ks) * 0.125 + mask[item]
                e = jnp.exp(s - jnp.max(s, axis=-1, keepdims=True))
                w = (e * (1.0 / jnp.sum(e, axis=-1, keepdims=True))).astype(BF16)
                p[item * HEADS + 2 * i + side] = w
                made.append(mm(w, vs))
            context[rows, at] = jnp.where(low, made[0], made[1]).astype(BF16)
        return carry

    lax.fori_loop(0, HEADS // 2, pair, 0)
    attended = jnp.concatenate([mm(context[...], whole[h, :, 3 * half :]) for h in (0, 1)], axis=1)
    first = x[...].astype(F32) + (attended + vec[O_B : O_B + 1, :])
    made, made_scale = norm_rows(first)
    unit[...] = made
    scale[...] = made_scale
    middle[...] = (made * vec[G_ONE : G_ONE + 1, :] + vec[S_ONE : S_ONE + 1, :]).astype(BF16)


def lift(smem, vmem, hbm, outs, scratch):
    (tab,) = smem
    middle, vec = vmem
    activated, slope = outs
    whole, sems = scratch
    finish(bring(tab, hbm, "up", whole, sems))
    half = whole.shape[2]
    width = vec.shape[1]
    step = width // 2
    for h in (0, 1):
        for j in range(half // step):
            at = slice(j * step, (j + 1) * step)
            column = h * half + j * step
            bias = vec[UP_B + column // width : UP_B + column // width + 1, column % width : column % width + step]
            a, s = gelu_and_slope(mm(middle[...], whole[h, :, at]) + bias)
            activated[h, :, at] = a.astype(BF16)
            slope[h, :, at] = s.astype(BF16)


def lower(smem, vmem, hbm, outs, scratch):
    (tab,) = smem
    activated, middle, vec = vmem
    output, unit, scale = outs
    whole, sems = scratch
    finish(bring(tab, hbm, "down", whole, sems))
    deep = activated.shape[2]
    lowered = jnp.concatenate(
        [
            mm(activated[0], whole[h, 0:deep, :]) + mm(activated[1], whole[h, deep:, :])
            for h in (0, 1)
        ],
        axis=1,
    )
    second = middle[...].astype(F32) + (lowered + vec[D_B : D_B + 1, :])
    made, made_scale = norm_rows(second)
    unit[...] = made
    scale[...] = made_scale
    output[...] = (made * vec[G_TWO : G_TWO + 1, :] + vec[S_TWO : S_TWO + 1, :]).astype(BF16)


def rows_sum(values):
    return jnp.sum(values, axis=0, keepdims=True)


def place_in(tab, places, chips, chip, ordered):
    return chip if ordered else tab[places * chips + chip]


def lower_back(smem, vmem, hbm, outs, scratch, ordered=False):
    (tab,) = smem
    grad, unit, scale, vec, activated = vmem
    sum_grad, lowered_grad, send, keep, sums = outs
    chips, rows, part = send.shape
    core = tab[4 * chips]
    g = grad[...].astype(F32)
    u = unit[...]
    made = norm_rows_back(u, scale[...], g * vec[G_TWO : G_TWO + 1, :])
    sum_grad[...] = made
    low = made.astype(BF16)
    half = low.shape[1] // 2
    lowered_grad[0] = low[:, :half]
    lowered_grad[1] = low[:, half:]
    sums[...] = jnp.zeros_like(sums)
    sums[0:1, :] = rows_sum(g * u)
    sums[1:2, :] = rows_sum(g)
    sums[2:3, :] = rows_sum(low.astype(F32))
    deep = activated.shape[2]
    wide = part // 4
    for out, hand, places in ((send, 1 - core, 3), (keep, core, 2)):
        right = lowered_grad[hand]
        for h in (0, 1):
            for j in range(deep // (8 * rows)):
                made = mm_tn(activated[h, :, 8 * rows * j : 8 * rows * (j + 1)], right).astype(BF16)
                for i in (0, 1):
                    chip = h * deep // (4 * rows) + 2 * j + i
                    to = place_in(tab, places, chips, chip, ordered)
                    for g in range(4):
                        at = (4 * i + g) * rows
                        out[to, :, g * wide : (g + 1) * wide] = made[at : at + rows]


def lift_back(smem, vmem, hbm, outs, scratch, ordered=False):
    (tab,) = smem
    lowered_grad, slope, middle = vmem
    lifted_grad, send, keep, sums = outs
    whole, sems, turned = scratch
    copies = bring(tab, hbm, "down", whole, sems)
    chips, rows, part = send.shape
    core = tab[4 * chips]
    turned[...] = middle[...].T
    finish(copies)
    width = sums.shape[1]
    step = width // 2
    sums[...] = jnp.zeros_like(sums)
    for h in (0, 1):
        for j in range(part // step):
            at = slice(j * step, (j + 1) * step)
            deep = slice(h * part + j * step, h * part + (j + 1) * step)
            made = mm_nt(lowered_grad[0], whole[0, deep, :]) + mm_nt(lowered_grad[1], whole[1, deep, :])
            made = (made * slope[h, :, at].astype(F32)).astype(BF16)
            lifted_grad[h, :, at] = made
            column = h * part + j * step
            sums[column // width : column // width + 1, column % width : column % width + step] = rows_sum(made.astype(F32))
    for out, hand, places in ((send, 1 - core, 3), (keep, core, 2)):
        for j in range(part // step):
            at = slice(j * step, (j + 1) * step)
            made = mm(turned[...], lifted_grad[hand, :, at]).astype(BF16)
            for chip in range(chips):
                out[place_in(tab, places, chips, chip, ordered), :, at] = made[chip * rows : (chip + 1) * rows]


def attend_back_first(smem, vmem, hbm, outs, scratch):
    (tab,) = smem
    sum_grad, lifted_grad, unit, scale, vec = vmem
    first_grad, attended_grad, context_grad, sums = outs
    whole, sems, o_whole, o_sems = scratch
    half = o_whole.shape[2]
    up_parts, four_parts = hbm[: len(hbm) // 2], hbm[len(hbm) // 2 :]
    copies = bring(tab, up_parts, "up", whole, sems)
    o_copies = bring(tab, four_parts, "four", o_whole, o_sems, columns=(3 * half, 4 * half))
    finish(copies)
    grad = sum_grad[...] + mm_nt(lifted_grad[0], whole[0]) + mm_nt(lifted_grad[1], whole[1])
    u = unit[...]
    made = norm_rows_back(u, scale[...], grad * vec[G_ONE : G_ONE + 1, :])
    first_grad[...] = made
    low = made.astype(BF16)
    attended_grad[0] = low[:, :half]
    attended_grad[1] = low[:, half:]
    sums[...] = jnp.zeros_like(sums)
    sums[0:1, :] = rows_sum(grad * u)
    sums[1:2, :] = rows_sum(grad)
    sums[2:3, :] = rows_sum(low.astype(F32))
    finish(o_copies)
    context_grad[...] = (mm_nt(low[:, :half], o_whole[0]) + mm_nt(low[:, half:], o_whole[1])).astype(BF16)


def attend_back_second(smem, vmem, hbm, outs, scratch):
    q, k, v, p, context_grad, attended_grad = vmem
    (grads,) = outs
    half = attended_grad.shape[2]
    items = q.shape[0] // ITEM
    low = lax.broadcasted_iota(jnp.int32, (ITEM, 2 * HEAD_DIM), 1) < HEAD_DIM
    pairs = HEADS // 4
    for h in (0, 1):
        grads[h, :, 3 * half :] = attended_grad[h]

        def pair(i, carry, h=h):
            at = pl.ds(pl.multiple_of(h * half + i * 2 * HEAD_DIM, 2 * HEAD_DIM), 2 * HEAD_DIM)
            for item in range(items):
                rows = slice(item * ITEM, (item + 1) * ITEM)
                qs, ks, vs, cs = q[rows, at], k[rows, at], v[rows, at], context_grad[rows, at]
                made = []
                for side in (0, 1):
                    own = low if side == 0 else jnp.logical_not(low)
                    w = p[item * HEADS + 2 * (h * pairs + i) + side]
                    wide = w.astype(F32)
                    g = mm_nt(jnp.where(own, cs, jnp.zeros_like(cs)), vs)
                    g = wide * g
                    d = (g - wide * jnp.sum(g, axis=-1, keepdims=True)).astype(BF16)
                    made.append((mm(d, ks), mm_tn(d, qs), mm_tn(w, cs)))
                for place, scale in ((0, 0.125), (1, 0.125), (2, 1.0)):
                    both = jnp.where(low, made[0][place], made[1][place]) * scale
                    to = pl.ds(pl.multiple_of(place * half + i * 2 * HEAD_DIM, 2 * HEAD_DIM), 2 * HEAD_DIM)
                    grads[h, rows, to] = both.astype(BF16)
            return carry

        lax.fori_loop(0, pairs, pair, 0)


def attend_back_third(smem, vmem, hbm, outs, scratch, ordered=False):
    (tab,) = smem
    x, context, grads = vmem
    send, keep, sums = outs
    x_turned, c_turned = scratch
    chips, rows, part = send.shape
    half = part // 4
    core = tab[4 * chips]
    x_turned[...] = x[...].T
    c_turned[...] = context[...].T
    for out, hand, places in ((send, 1 - core, 3), (keep, core, 2)):
        for j in range(4):
            at = slice(j * half, (j + 1) * half)
            made = mm((c_turned if j == 3 else x_turned)[...], grads[hand, :, at]).astype(BF16)
            for chip in range(chips):
                out[place_in(tab, places, chips, chip, ordered), :, at] = made[chip * rows : (chip + 1) * rows]
    sums[...] = jnp.zeros_like(sums)
    for h in (0, 1):
        at = slice(h * half, (h + 1) * half)
        sums[0:1, at] = rows_sum(grads[h, :, 0:half].astype(F32))
        sums[1:2, at] = rows_sum(grads[h, :, 2 * half : 3 * half].astype(F32))


def attend_back_last(smem, vmem, hbm, outs, scratch):
    (tab,) = smem
    first_grad, grads = vmem
    (out,) = outs
    whole, sems = scratch
    deep = whole.shape[2]
    finish(bring(tab, hbm, "four", whole, sems, columns=(0, deep)))
    out[...] = first_grad[...] + mm_nt(grads[0, :, :deep], whole[0]) + mm_nt(grads[1, :, :deep], whole[1])


def add_halves(smem, vmem, hbm, outs, scratch):
    keep, came = vmem
    send, kept = outs
    half = send.shape[0]

    def block(b, carry):
        kept[b] = (keep[b].astype(F32) + came[b].astype(F32)).astype(BF16)
        send[b] = (keep[half + b].astype(F32) + came[half + b].astype(F32)).astype(BF16)
        return carry

    lax.fori_loop(0, half, block, 0)


def add_spread(smem, vmem, hbm, outs, scratch):
    keep, came = vmem
    for b, out in enumerate(outs):
        out[...] = (keep[b].astype(F32) + came[b].astype(F32)).astype(out.dtype)


def add_packed(smem, vmem, hbm, outs, scratch):
    (out,) = outs
    rows = vmem[0].shape[1]

    def block(b, carry):
        for i in range(len(vmem) // 2):
            both = vmem[2 * i][b].astype(F32) + vmem[2 * i + 1][b].astype(F32)
            out[b, i * rows : (i + 1) * rows] = both.astype(BF16)
        return carry

    lax.fori_loop(0, out.shape[0], block, 0)


def add_last(smem, vmem, hbm, outs, scratch, kinds=()):
    (tab,) = smem
    core = tab[tab.shape[0] - 1]
    (total,) = scratch
    made = vmem[0][...].astype(F32)
    for came in vmem[1:]:
        made = made + came[...].astype(F32)
    total[...] = made
    rows = total.shape[0] // len(kinds)
    for i, kind in enumerate(kinds):
        for out, hand in ((outs[2 * i], core), (outs[2 * i + 1], 1 - core)):
            if kind == "down":
                wide = total.shape[1] // 2
                out[...] = total[i * rows : (i + 1) * rows, pl.ds(pl.multiple_of(hand * wide, 128), wide)]
            else:
                half = rows // 2
                out[...] = total[pl.ds(pl.multiple_of(i * rows + hand * half, 8), half), :]


def write_out(smem, vmem, hbm, outs, scratch, kind=""):
    (tab,) = smem
    core = tab[tab.shape[0] - 1]
    half = outs[0].shape[2] // 2
    for layer in range(len(vmem) // 2):
        for hand, part in ((core, vmem[2 * layer]), (1 - core, vmem[2 * layer + 1])):
            at = pl.ds(pl.multiple_of(hand * half, 128), half)
            if kind == "down":
                rows = part.shape[0]
                for g in (0, 1):
                    outs[0][layer, g * rows : (g + 1) * rows, at] = part[:, g * half : (g + 1) * half]
                continue
            for i, out in enumerate(outs):
                out[layer, :, at] = part[:, i * half : (i + 1) * half]


def join_packed(smem, vmem, hbm, outs, scratch):
    (tab,) = smem
    first = tab[tab.shape[0] - 1] == 0
    (out,) = outs
    joined = []
    for i in range(3):
        mine, came = vmem[2 * i][...].astype(F32), vmem[2 * i + 1][...].astype(F32)
        joined.append([jnp.where(first, mine, came), jnp.where(first, came, mine)])
    rows = out.shape[0] // 3
    for i in (0, 1):
        out[i * rows : (i + 1) * rows] = jnp.concatenate(joined[i], axis=0).astype(BF16)
    wide = joined[2][0].shape[1]
    for g in range(4):
        part = joined[2][g // 2][g % 2 * rows : (g % 2 + 1) * rows]
        out[2 * rows :, g * wide : (g + 1) * wide] = part.astype(BF16)


def add_two(smem, vmem, hbm, outs, scratch):
    outs[0][...] = vmem[0][...] + vmem[1][...]


class Chain:
    def __init__(self):
        self.token = None

    def __call__(self, body, outs, after=(), **kinds):
        deps = list(after) + ([] if self.token is None else [self.token])
        made = launch(body, outs, deps=deps, **kinds)
        self.token = min(made, key=lambda m: m.size)
        return made


def spread_vectors(small, owners):
    me = lax.axis_index("dp")
    layers = small[0].shape[0]
    short = [v for v in small if v.shape[1] == small[0].shape[1]]
    (long,) = [v for v in small if v.shape[1] != small[0].shape[1]]
    width = short[0].shape[1] * owners
    lanes = jnp.arange(width, dtype=jnp.int32)

    def spread(values, start):
        count = values.shape[1]
        hit = lanes[None, :] == start + jnp.arange(count, dtype=jnp.int32)[:, None]
        return jnp.dot(values, hit.astype(BF16), preferred_element_type=F32)

    count = short[0].shape[1]
    plain = spread(jnp.stack(short, axis=1).reshape(-1, count), me * count)
    count = long.shape[1]
    rows = count * owners // width
    wide = spread(long, me * count % width)
    row = jnp.arange(rows, dtype=jnp.int32)[None, :, None] == me * count // width
    wide = jnp.where(row, wide[:, None, :], 0.0)
    own = jnp.concatenate([plain.reshape(layers, -1, width), wide], axis=1)
    return own.reshape(-1, width).astype(BF16)


def own_share(total, counts, owners):
    me = lax.axis_index("dp")
    layers, _, width = total.shape
    out = []
    row = 0
    for count in counts:
        rows = count * owners // width
        whole = total[:, row : row + rows].reshape(layers, -1)
        out.append(lax.dynamic_slice_in_dim(whole, me * count, count, axis=1))
        row += rows
    return out


def blocks(weights, small, mask, hidden, cotangent, seq):
    q_weight, k_weight, v_weight, o_weight, up_weight, down_weight = weights
    owners = lax.axis_size("dp")
    chips = owners // 2
    depth = chips // 4
    layers, rows, width = q_weight.shape
    wide = up_weight.shape[2]
    items = hidden.shape[0] // seq
    tall = items * ITEM
    tab = table_of(owners)
    chain = Chain()
    dma = lambda n: pltpu.SemaphoreType.DMA((n,))
    xy_one = lambda v: flip(v, owners, 2, 4)
    xy_two = lambda v: flip(v, owners, 4, 2)
    core_flip = lambda v: flip(v, owners, 1, 1)
    z_flip = lambda v, k: flip(v, owners, 8 * k, 8 * k)
    bits = [lambda v, b=b: flip(v, owners, 1 << b, 1 << b) for b in range(int(math.log2(owners)))]
    same_core = [list(range(core, owners, 2)) for core in (0, 1)]

    def padded(values):
        spread = values.reshape(items, seq, width)
        return jnp.pad(spread, ((0, 0), (0, ITEM - seq), (0, 0))).reshape(tall, width)

    x = padded(hidden)
    grad = padded(cotangent)

    block = (2 * rows, 2 * width)
    shape = {"four": block, "up": (2 * rows, wide // 2), "down": (2 * down_weight.shape[1], width // 2)}
    kinds = ("four", "up", "down")
    halves = [((shape[k][0] // 2, shape[k][1]), BF16) for k in kinds]
    split = chain(split_own, halves * 2 * layers, smem=[tab], vmem=list(weights))
    mine = lambda layer: split[6 * layer : 6 * layer + 3]
    other = [[core_flip(v) for v in split[6 * layer + 3 : 6 * layer + 6]] for layer in range(layers)]
    both = lambda layer: [v for two in zip(mine(layer), other[layer]) for v in two]
    own, near, far = {}, {}, {}
    z_came, x_one, x_two, stacked = {}, {}, {}, {}

    (pack,) = chain(join_packed, [((3 * block[0], block[1]), BF16)], smem=[tab], vmem=both(1))
    packed = lax.all_gather(pack, "dp", axis=0, tiled=True, axis_index_groups=same_core)
    made = chain(join_rows, [(shape[k], BF16) for k in kinds], smem=[tab], vmem=both(0))
    for kind, value in zip(kinds, made):
        own[kind] = value

    def z_round(kind):
        z_came[kind] = [z_flip(own[kind], k) for k in range(1, depth)]

    def first_stack(kind, after=()):
        r, c = shape[kind]
        (stacked[kind],) = chain(join_blocks, [((depth, r, c), BF16)], hbm=[own[kind]] + z_came[kind], scratch=[dma(depth)], after=after)
        x_one[kind] = xy_one(stacked[kind])

    def second_stack(kind, after=()):
        r, c = shape[kind]
        (made,) = chain(join_blocks, [((2 * depth, r, c), BF16)], hbm=[stacked[kind], x_one[kind]], scratch=[dma(2)], after=after)
        x_two[kind] = xy_two(made)
        near[kind] = [made, x_two[kind]]
        far[kind] = [core_flip(made)]

    def third(kind):
        far[kind].append(core_flip(x_two[kind]))

    vectors = spread_vectors(small, owners)

    def vector_round(bit):
        nonlocal vectors
        (vectors,) = chain(add_two, [(vectors.shape, vectors.dtype)], vmem=[vectors, bits[bit](vectors)])

    def land():
        nonlocal packed
        value = lax.optimization_barrier((packed, chain.token))[0].reshape((chips,) + pack.shape)
        packed = [value, core_flip(value)]

    parts = lambda layer, kind: near[kind] + far[kind] if layer == 0 else packed
    whole = lambda kind, columns=None: [pltpu.VMEM((2, shape[kind][0] * chips, columns or shape[kind][1]), BF16), dma(8 * chips)]
    xs, kept = [x], [{} for _ in range(layers)]
    row = lambda dtype: ((tall, width), dtype)
    column = ((tall, 1), F32)
    deep = ((2, tall, wide // 2), BF16)

    def forward_attend(layer):
        s = kept[layer]
        s["q"], s["k"], s["v"], s["p"], s["context"], s["unit_one"], s["scale_one"], s["middle"] = chain(
            attend_forward,
            [row(BF16)] * 3 + [((items * HEADS, ITEM, ITEM), BF16), row(BF16), row(F32), column, row(BF16)],
            smem=[tab], vmem=[xs[layer], vec[layer], mask], hbm=parts(layer, "four"), scratch=whole("four"),
        )

    def forward_lift(layer):
        s = kept[layer]
        s["activated"], s["slope"] = chain(
            lift, [deep, deep], smem=[tab], vmem=[s["middle"], vec[layer]], hbm=parts(layer, "up"), scratch=whole("up"),
        )

    def forward_lower(layer):
        s = kept[layer]
        output, s["unit_two"], s["scale_two"] = chain(
            lower, [row(BF16), row(F32), column], smem=[tab], vmem=[s["activated"], s["middle"], vec[layer]],
            hbm=parts(layer, "down"), scratch=whole("down"),
        )
        xs.append(output)

    z_round("four")
    z_round("up")
    vector_round(0)
    first_stack("four")
    vector_round(1)
    vector_round(2)
    second_stack("four")
    vector_round(3)
    z_round("down")
    first_stack("up")
    vector_round(4)
    vec = vectors.astype(F32).reshape(layers, -1, width)
    third("four")
    second_stack("up", after=[x_two["four"]])
    first_stack("down")
    forward_attend(0)
    third("up")
    second_stack("down", after=[x_two["up"]])
    forward_lift(0)
    third("down")
    land()
    forward_lower(0)
    forward_attend(1)
    forward_lift(1)
    forward_lower(1)

    pair = [((chips,) + block, BF16)] * 2
    keep, came, fanned, last = {}, {}, {}, {}
    sums = [{} for _ in range(layers)]
    flowing = [None] * (layers + 1)
    flowing[layers] = grad

    def leave(piece, send, kept_blocks):
        keep[piece] = kept_blocks
        came[piece] = core_flip(send)

    def back_lower(layer):
        s = kept[layer]
        s["sum_grad"], s["lowered_grad"], send, rest, sums[layer]["down"] = chain(
            functools.partial(lower_back, ordered=layer > 0),
            [row(F32), ((2, tall, width // 2), BF16)] + pair + [((8, width), F32)],
            smem=[tab], vmem=[flowing[layer + 1], s["unit_two"], s["scale_two"], vec[layer], s["activated"]],
        )
        leave((layer, "down"), send, rest)

    def back_lift(layer):
        s = kept[layer]
        s["lifted_grad"], send, rest, sums[layer]["up"] = chain(
            functools.partial(lift_back, ordered=layer > 0), [deep] + pair + [((8, width), F32)],
            smem=[tab], vmem=[s["lowered_grad"], s["slope"], s["middle"]], hbm=parts(layer, "down"),
            scratch=whole("down") + [pltpu.VMEM((width, tall), BF16)],
        )
        leave((layer, "up"), send, rest)

    def back_one(layer):
        s = kept[layer]
        s["first_grad"], s["attended_grad"], s["context_grad"], sums[layer]["one"] = chain(
            attend_back_first, [row(F32), ((2, tall, width // 2), BF16), row(BF16), ((8, width), F32)],
            smem=[tab], vmem=[s["sum_grad"], s["lifted_grad"], s["unit_one"], s["scale_one"], vec[layer]],
            hbm=parts(layer, "up") + parts(layer, "four"), scratch=whole("up") + whole("four", width // 2),
        )

    def back_two(layer):
        s = kept[layer]
        (s["grads"],) = chain(
            attend_back_second, [((2, tall, 2 * width), BF16)],
            vmem=[s["q"], s["k"], s["v"], s["p"], s["context_grad"], s["attended_grad"]],
        )

    def back_three(layer):
        s = kept[layer]
        send, rest, sums[layer]["four"] = chain(
            attend_back_third, pair + [((8, width), F32)], smem=[tab], vmem=[xs[layer], s["context"], s["grads"]],
            scratch=[pltpu.VMEM((width, tall), BF16)] * 2,
        )
        leave((layer, "four"), send, rest)

    def back_last(layer):
        s = kept[layer]
        (flowing[layer],) = chain(
            attend_back_last, [row(F32)], smem=[tab], vmem=[s["first_grad"], s["grads"]], hbm=parts(layer, "four"),
            scratch=whole("four", width * 3 // 2),
        )

    def fold(piece):
        half = keep[piece].shape[0] // 2
        send, keep[piece] = chain(add_halves, [((half,) + block, BF16)] * 2, vmem=[keep[piece], came[piece]])
        came[piece] = xy_two(send) if half == 2 * depth else xy_one(send)

    def fan(piece):
        made = chain(add_spread, [(block, F32)] + [(block, BF16)] * (depth - 1), vmem=[keep[piece], came[piece]])
        keep[piece] = made[0]
        fanned[piece] = [z_flip(made[k], k) for k in range(1, depth)]

    def owned(kind):
        return (block[0], block[1] // 2) if kind == "down" else (block[0] // 2, block[1])

    def total(pieces, values):
        outs = [(owned(kind), F32) for _, kind in pieces for _ in (0, 1)]
        made = chain(
            functools.partial(add_last, kinds=tuple(kind for _, kind in pieces)), outs, smem=[tab], vmem=values,
            scratch=[pltpu.VMEM((len(pieces) * block[0], block[1]), F32)],
        )
        for i, piece in enumerate(pieces):
            last[piece] = [made[2 * i], core_flip(made[2 * i + 1])]

    def finished(kind, count):
        height = down_weight.shape[1] if kind == "down" else rows
        columns = wide if kind == "up" else width
        return chain(
            functools.partial(write_out, kind=kind), [((layers, height, columns), F32)] * count, smem=[tab],
            vmem=[v for layer in range(layers) for v in last[layer, kind]],
        )

    back_lower(1)
    back_lift(1)
    d1, u1, f1, d0, u0, f0 = [(layer, kind) for layer in (1, 0) for kind in ("down", "up", "four")]
    back_one(1)
    (gone,) = chain(
        add_packed, [((chips, 2 * block[0], block[1]), BF16)], vmem=[keep[d1], came[d1], keep[u1], came[u1]]
    )
    gone = lax.psum_scatter(
        gone.reshape(-1, block[1]), "dp", scatter_dimension=0, tiled=True, axis_index_groups=same_core
    )
    back_two(1)
    back_three(1)
    back_last(1)
    fold(f1)
    back_lower(0)
    fold(f1)
    back_lift(0)
    fold(d0)
    fan(f1)
    back_one(0)
    fold(d0)
    fold(u0)
    total([f1], [keep[f1]] + fanned[f1])
    back_two(0)
    fan(d0)
    fold(u0)
    back_three(0)
    total([d0], [keep[d0]] + fanned[d0])
    total([d1, u1], [gone])
    fan(u0)
    fold(f0)
    rows_of = []
    for layer in range(layers):
        s = sums[layer]
        rows_of += [s["four"][0:2], s["one"][2:3], s["one"][0:2], s["down"][2:3], s["down"][0:2], s["up"][0 : wide // width]]
    vectors = jnp.concatenate(rows_of)
    back_last(0)
    fold(f0)
    total([u0], [keep[u0]] + fanned[u0])
    vector_round(0)
    vector_round(1)
    (down_grad,) = finished("down", 1)
    fan(f0)
    vector_round(2)
    (up_grad,) = finished("up", 1)
    vector_round(3)
    vector_round(4)
    total([f0], [keep[f0]] + fanned[f0])
    four_grads = finished("four", 4)

    order = [v for v in small if v.shape[1] == rows] + [v for v in small if v.shape[1] != rows]
    shares = own_share(vectors.reshape(layers, -1, width), [v.shape[1] for v in order], owners)
    cut = lambda values: values.reshape(items, ITEM, width)[:, :seq].reshape(items * seq, width)
    q_b, v_b, o_b, g_one, s_one, d_b, g_two, s_two, u_b = shares
    return (
        cut(xs[-1]), cut(flowing[0]), *four_grads,
        q_b, v_b, o_b, g_one, s_one, up_grad, u_b, down_grad, d_b, g_two, s_two,
    )


def shards(
    hidden, region_count, text_mask,
    q_weight, k_weight, v_weight, o_weight, q_bias, v_bias, o_bias, gain_one, shift_one,
    up_weight, up_bias, down_weight, down_bias, gain_two, shift_two, cotangent,
):
    owners = lax.axis_size("dp")
    valid_keys = slot_valid(region_count, text_mask)
    weights = (q_weight, k_weight, v_weight, o_weight, up_weight, down_weight)
    small = (q_bias, v_bias, o_bias, gain_one, shift_one, up_bias, down_bias, gain_two, shift_two)
    seq = valid_keys.shape[1]
    width = hidden.shape[1]
    fits = (
        owners in (16, 32)
        and q_weight.shape[1] % 8 == 0
        and up_weight.shape[2] % (2 * width) == 0
        and seq <= ITEM
        and q_weight.shape[0] == 2
    )
    if not fits:
        return plain(weights, small, valid_keys, hidden, cotangent)
    mask = (valid_keys - 1.0) * 10000.0
    mask = jnp.pad(mask, ((0, 0), (0, ITEM - seq)), constant_values=PAD)[:, None, :]
    return blocks(weights, small, mask, hidden, cotangent, seq)


def solution(mesh):
    rows = P("dp", None)
    matrix = P(None, "dp", None)
    vector = P(None, "dp")
    four = (matrix,) * 4
    return jax.shard_map(
        shards,
        mesh=mesh,
        in_specs=(rows, P("dp"), rows) + four + (vector,) * 5
        + (matrix, vector, matrix, vector, vector, vector, rows),
        out_specs=(rows, rows) + four + (vector,) * 5
        + (matrix, vector, matrix, vector, vector, vector),
        check_vma=False,
    )
```

```python
import functools
import math

import jax
import jax.numpy as jnp
from jax import lax
from jax.experimental import pallas as pl
from jax.experimental.pallas import tpu as pltpu
from jax.sharding import PartitionSpec as P

HEADS = 12
HEAD_DIM = 64
REGIONS = 100

epsilon = 1e-12
F32 = jnp.float32
BF16 = jnp.bfloat16


def dense(left, right):
    return jnp.dot(left, right, preferred_element_type=F32)


def outer(left, right):
    return lax.dot_general(left, right, (((0,), (0,)), ((), ())), preferred_element_type=F32)


def back_dense(left, right):
    return lax.dot_general(left, right, (((1,), (1,)), ((), ())), preferred_element_type=F32)


def column_sum(values):
    return jnp.sum(values.astype(F32), axis=0)


def slot_valid(region_count, text_mask):
    region_slot = jnp.arange(REGIONS, dtype=jnp.int32)[None, :] < region_count[:, None]
    return jnp.concatenate([text_mask.astype(F32), region_slot.astype(F32)], axis=1)


def norm(values, gain, shift):
    center = values - jnp.mean(values, axis=-1, keepdims=True)
    spread = jnp.mean(center * center, axis=-1, keepdims=True)
    scale = lax.rsqrt(spread + epsilon)
    unit = center * scale
    return unit * gain + shift, (unit, scale)


def norm_back(saved, gain, grad):
    unit, scale = saved
    inner = grad * gain
    into = scale * (
        inner
        - jnp.mean(inner, axis=-1, keepdims=True)
        - unit * jnp.mean(inner * unit, axis=-1, keepdims=True)
    )
    return into, column_sum(grad * unit), column_sum(grad)


def forward_layer(inputs, weights, vectors, valid_keys):
    q_weight, k_weight, v_weight, o_weight, up_weight, down_weight = weights
    q_bias, v_bias, o_bias, gain_one, shift_one, up_bias, down_bias, gain_two, shift_two = vectors
    item_count = valid_keys.shape[0]
    row_count, width = inputs.shape

    def heads_of(values):
        return values.reshape(item_count, row_count // item_count, HEADS, HEAD_DIM)

    queries = heads_of((dense(inputs, q_weight) + q_bias).astype(BF16))
    key_rows = heads_of(dense(inputs, k_weight).astype(BF16))
    value_rows = heads_of((dense(inputs, v_weight) + v_bias).astype(BF16))
    scores = (
        jnp.einsum("bqhd,bkhd->bhqk", queries, key_rows, preferred_element_type=F32) * 0.125
    )
    scores = scores + (valid_keys[:, None, None, :] - 1.0) * 10000.0
    attention = jax.nn.softmax(scores, axis=-1)
    attention_low = attention.astype(BF16)
    context = jnp.einsum("bhqk,bkhd->bqhd", attention_low, value_rows, preferred_element_type=F32)
    context = context.astype(BF16).reshape(row_count, width)
    first_sum = inputs.astype(F32) + dense(context, o_weight) + o_bias
    middle, norm_one = norm(first_sum, gain_one, shift_one)
    middle = middle.astype(BF16)
    lifted = dense(middle, up_weight) + up_bias
    half = 0.5 * lax.erf(lifted * math.sqrt(0.5)) + 0.5
    activated = (lifted * half).astype(BF16)
    slope = half + lifted * jnp.exp(-0.5 * lifted * lifted) * (1.0 / math.sqrt(2.0 * math.pi))
    slope = slope.astype(BF16)
    second_sum = middle.astype(F32) + dense(activated, down_weight) + down_bias
    output, norm_two = norm(second_sum, gain_two, shift_two)
    saved = (queries, key_rows, value_rows, attention, attention_low, context, norm_one, middle, slope, activated, norm_two)
    return output.astype(BF16), saved


def backward_layer(inputs, weights, vectors, saved, out_grad, send):
    q_weight, k_weight, v_weight, o_weight, up_weight, down_weight = weights
    q_bias, v_bias, o_bias, gain_one, shift_one, up_bias, down_bias, gain_two, shift_two = vectors
    queries, key_rows, value_rows, attention, attention_low, context, norm_one, middle, slope, activated, norm_two = saved
    row_count, width = inputs.shape
    sum_grad, gain_two_grad, shift_two_grad = norm_back(norm_two, gain_two, out_grad)
    lowered_grad = sum_grad.astype(BF16)
    send("down", [outer(activated, lowered_grad)])
    lifted_grad = (back_dense(lowered_grad, down_weight) * slope).astype(BF16)
    send("up", [outer(middle, lifted_grad)])
    middle_grad = sum_grad + back_dense(lifted_grad, up_weight)
    first_grad, gain_one_grad, shift_one_grad = norm_back(norm_one, gain_one, middle_grad)
    attended_grad = first_grad.astype(BF16)
    o_grad = outer(context, attended_grad)
    context_grad = back_dense(attended_grad, o_weight).astype(BF16).reshape(queries.shape)
    attention_grad = jnp.einsum(
        "bqhd,bkhd->bhqk", context_grad, value_rows, preferred_element_type=F32
    )
    value_grad = jnp.einsum(
        "bhqk,bqhd->bkhd", attention_low, context_grad, preferred_element_type=F32
    )
    value_grad = value_grad.astype(BF16).reshape(row_count, width)
    weighed = attention * attention_grad
    score_grad = (weighed - attention * jnp.sum(weighed, axis=-1, keepdims=True)).astype(BF16)
    query_grad = (
        jnp.einsum("bhqk,bkhd->bqhd", score_grad, key_rows, preferred_element_type=F32) * 0.125
    )
    query_grad = query_grad.astype(BF16).reshape(row_count, width)
    key_grad = (
        jnp.einsum("bhqk,bqhd->bkhd", score_grad, queries, preferred_element_type=F32) * 0.125
    )
    key_grad = key_grad.astype(BF16).reshape(row_count, width)
    send("four", [outer(inputs, query_grad), outer(inputs, key_grad), outer(inputs, value_grad), o_grad])
    input_grad = (
        first_grad
        + back_dense(query_grad, q_weight)
        + back_dense(key_grad, k_weight)
        + back_dense(value_grad, v_weight)
    )
    small = (column_sum(query_grad), column_sum(value_grad), column_sum(attended_grad), gain_one_grad, shift_one_grad, column_sum(lifted_grad), column_sum(lowered_grad), gain_two_grad, shift_two_grad)
    return input_grad, small


def plain(weights, small, valid_keys, hidden, cotangent):
    owners = lax.axis_size("dp")
    layers = weights[0].shape[0]
    packed = jnp.concatenate([v.reshape(1, -1) for v in small], axis=1)
    packed = lax.all_gather(packed, "dp", axis=0, tiled=True).astype(F32)
    vectors = []
    offset = 0
    for v in small:
        size = v.shape[0] * v.shape[1]
        part = packed[:, offset : offset + size].reshape((owners,) + v.shape)
        vectors.append(jnp.swapaxes(part, 0, 1).reshape(layers, -1))
        offset += size
    vectors = [tuple(v[layer] for v in vectors) for layer in range(layers)]
    gathered = [
        tuple(lax.all_gather(w[layer], "dp", axis=0, tiled=True) for w in weights)
        for layer in range(layers)
    ]
    current = hidden
    inputs, saved = [], []
    for layer in range(layers):
        inputs.append(current)
        current, kept = forward_layer(current, gathered[layer], vectors[layer], valid_keys)
        saved.append(kept)
    flowing = cotangent.astype(F32)
    big = [{} for _ in range(layers)]
    tiny = [None] * layers
    for layer in reversed(range(layers)):

        def send(name, grads, layer=layer):
            big[layer][name] = [
                lax.psum_scatter(g.astype(BF16).reshape(owners, -1, g.shape[-1]), "dp", scatter_dimension=0, tiled=True)[0].astype(F32)
                for g in grads
            ]

        flowing, tiny[layer] = backward_layer(
            inputs[layer], gathered[layer], vectors[layer], saved[layer], flowing, send
        )
    flat = jnp.concatenate(
        [g.reshape(owners, -1) for layer in range(layers) for g in tiny[layer]], axis=1
    )
    flat = lax.psum_scatter(flat, "dp", scatter_dimension=0, tiled=True).reshape(layers, -1)
    summed = []
    offset = 0
    for v in small:
        summed.append(flat[:, offset : offset + v.shape[1]])
        offset += v.shape[1]
    q_b, v_b, o_b, g_one, s_one, u_b, d_b, g_two, s_two = summed
    fours = [jnp.stack([big[layer]["four"][i] for layer in range(layers)]) for i in range(4)]
    up = jnp.stack([big[layer]["up"][0] for layer in range(layers)])
    down = jnp.stack([big[layer]["down"][0] for layer in range(layers)])
    return (
        current, flowing, *fours,
        q_b, v_b, o_b, g_one, s_one, up, u_b, down, d_b, g_two, s_two,
    )


ITEM = 256
PAD = -1e30


def table_of(owners):
    chips = owners // 2
    depth = chips // 4
    me = lax.axis_index("dp")
    chip, core = me // 2, me % 2
    walk = jnp.arange(chips, dtype=jnp.int32)

    def chip_at(position, core):
        z, first, second = position % depth, position // depth % 2, position // (2 * depth)
        return chip ^ (z * 4 + jnp.where(core == 0, second * 2 + first, first * 2 + second))

    def place_of(other, core):
        z, y, x = (other ^ chip) // 4, (other ^ chip) // 2 % 2, (other ^ chip) % 2
        return z + depth * jnp.where(core == 0, x + 2 * y, y + 2 * x)

    return jnp.concatenate(
        [chip_at(walk, core), chip_at(walk, 1 - core), place_of(walk, core), place_of(walk, 1 - core), core[None]]
    ).astype(jnp.int32)


def flip(value, owners, even, odd):
    return lax.ppermute(value, "dp", [(i, i ^ (odd if i % 2 else even)) for i in range(owners)])


MICROS = 50


def padded_bytes(shape, dtype):
    *lead, rows, columns = (1,) * max(0, 2 - len(shape)) + tuple(shape)
    return math.prod(lead) * (-(-rows // 16) * 16) * (-(-columns // 128) * 128) * jnp.dtype(dtype).itemsize


class Held:
    def __init__(self, room, copy, inward):
        self.room, self.copy, self.inward, self.open = room, copy, inward, True
        self.shape, self.dtype = room.shape, room.dtype
        self.begun = False

    def begin(self):
        if self.inward and not self.begun:
            self.copy.start()
            self.begun = True

    def ready(self):
        if self.inward and self.open:
            self.begin()
            self.copy.wait()
            self.open = False

    def send(self):
        if not self.inward and self.open:
            self.copy.start()
            self.open = False

    def __getitem__(self, at):
        self.ready()
        return self.room[at]

    def __setitem__(self, at, value):
        self.room[at] = value


def launch(body, outs, smem=(), vmem=(), hbm=(), deps=(), scratch=(), extra=3, far=pl.ANY, held=False, late=()):
    counts = (len(smem), len(vmem), len(hbm), len(deps), len(outs))
    name = getattr(body, "func", body).__name__
    sizes = [(v.shape, v.dtype) for v in vmem] + list(outs)
    large = [held and padded_bytes(*v) > 2**16 for v in sizes]
    rooms = [pltpu.VMEM(*v) for v, big in zip(sizes, large) if big]
    own = len(scratch)
    scratch = list(scratch) + rooms + ([pltpu.SemaphoreType.DMA((len(rooms),))] if rooms else [])
    budget = sizes + [(v.shape, v.dtype) for v in scratch[:own] if jnp.issubdtype(v.dtype, jnp.floating)]
    limit = (extra + 10 * held) * 2**20 + sum(padded_bytes(shape, dtype) for shape, dtype in budget)

    def kernel(*refs):
        groups, at = [], 0
        for count in counts:
            groups.append(list(refs[at : at + count]))
            at += count
        left = list(refs[at + own :])
        sems = left.pop() if rooms else None
        moved = []
        for group, base, inward in ((groups[1], 0, True), (groups[4], len(vmem), False)):
            for i, ref in enumerate(group):
                if large[base + i]:
                    room, sem = left.pop(0), sems.at[len(moved)]
                    copy = pltpu.make_async_copy(ref, room, sem) if inward else pltpu.make_async_copy(room, ref, sem)
                    group[i] = Held(room, copy, inward)
                    moved.append(group[i])
                    if inward and i not in late:
                        group[i].begin()
        body(groups[0], groups[1], groups[2], groups[4], refs[at : at + own])
        for one in moved:
            one.ready()
            one.send()
        for one in moved:
            if not one.inward:
                one.copy.wait()

    space = lambda big: pl.BlockSpec(memory_space=pl.ANY if big else pltpu.VMEM)
    in_specs = (
        [pl.BlockSpec(memory_space=pltpu.SMEM)] * len(smem)
        + [space(big) for big in large[: len(vmem)]]
        + [pl.BlockSpec(memory_space=far)] * len(hbm)
        + [pl.BlockSpec(memory_space=pl.ANY)] * len(deps)
    )
    return pl.pallas_call(
        kernel,
        out_shape=[jax.ShapeDtypeStruct(s, d) for s, d in outs],
        in_specs=in_specs,
        out_specs=[space(big) for big in large[len(vmem) :]],
        scratch_shapes=list(scratch),
        name=name,
        compiler_params=pltpu.CompilerParams(vmem_limit_bytes=limit),
        cost_estimate=pl.CostEstimate(
            flops=int(MICROS * 1e9), bytes_accessed=int(MICROS * 3e6), transcendentals=0
        ),
    )(*smem, *vmem, *hbm, *deps)


def mm(left, right):
    return jnp.dot(left, right, preferred_element_type=F32)


def mm_nt(left, right):
    return lax.dot_general(left, right, (((1,), (1,)), ((), ())), preferred_element_type=F32)


def mm_tn(left, right):
    return lax.dot_general(left, right, (((0,), (0,)), ((), ())), preferred_element_type=F32)


def fetch(tab, parts, kind, section, whole, sems, columns=None, step=768):
    near, near_more, far, far_more = parts
    half = near.shape[0]
    rows = whole.shape[-2] // (2 * half)
    core = tab[8 * half]
    first, last = (0, whole.shape[-1]) if columns is None else columns
    if (last - first) % step:
        step = last - first
    count = 0
    sides = []
    for side, group in enumerate(((near, near_more), (far, far_more))):
        hand = core if side == 0 else 1 - core
        steps = []
        for at in [0] if kind == "down" else range(first, last, step):
            copies = []
            for which, part in enumerate(group):
                for b in range(half):
                    start = pl.multiple_of(tab[(2 * side + which) * half + b] * rows, 16)
                    moves = []
                    if kind == "down":
                        wide, deep = part.shape[2] // 4, rows // 4
                        for g in range(4):
                            source = part.at[b, pl.ds(section * deep, deep), pl.ds(g * wide, wide)]
                            to = pl.ds(start + g * deep, deep)
                            if len(whole.shape) == 3:
                                moves.append((source, whole.at[hand, to]))
                            else:
                                at = pl.ds(pl.multiple_of(hand * wide, 128), wide)
                                moves.append((source, whole.at[to, at]))
                    else:
                        wide = 768 if step % 768 == 0 else 384
                        for piece in range(at, at + step, wide):
                            source = part.at[b, pl.ds(section * rows, rows), pl.ds(piece, wide)]
                            target = whole.at[hand, pl.ds(start, rows), pl.ds(piece - first, wide)]
                            moves.append((source, target))
                    for source, target in moves:
                        copies.append(pltpu.make_async_copy(source, target, sems.at[count]))
                        copies[-1].start()
                        count += 1
            steps.append(copies)
        sides.append(steps)
    return sides


def finish_all(sides):
    for steps in sides:
        for copies in steps:
            finish(copies)


def finish(copies):
    for copy in copies:
        copy.wait()


def norm_rows(values):
    center = values - jnp.mean(values, axis=-1, keepdims=True)
    scale = lax.rsqrt(jnp.mean(center * center, axis=-1, keepdims=True) + epsilon)
    return center * scale, scale


def norm_rows_back(unit, scale, inner):
    return scale * (
        inner
        - jnp.mean(inner, axis=-1, keepdims=True)
        - unit * jnp.mean(inner * unit, axis=-1, keepdims=True)
    )


def gelu_and_slope(v):
    phi = 0.5 + 0.5 * lax.erf(v * math.sqrt(0.5))
    return v * phi, phi + v * jnp.exp(-0.5 * v * v) * (1.0 / math.sqrt(2.0 * math.pi))


def put_rows_apart(source, room, seq):
    count = source.shape[0]
    room[count:, :] = jnp.zeros((room.shape[0] - count, room.shape[1]), F32)
    room[0:count, :] = source[...].astype(F32)
    row = lax.broadcasted_iota(jnp.int32, (ITEM, room.shape[1]), 0)
    return [
        jnp.where(row < seq, room[i * seq : i * seq + ITEM, :], 0.0) for i in range(count // seq)
    ]


def put_rows_together(values, out, seq):
    for i in range(values.shape[0] // ITEM):
        out[i * seq : (i + 1) * seq, :] = values[i * ITEM : i * ITEM + seq]


Q_B, V_B, O_B, G_ONE, S_ONE, D_B, G_TWO, S_TWO, UP_B = range(9)


def split_own(smem, vmem, hbm, outs, scratch):
    (tab,) = smem
    core = tab[tab.shape[0] - 1]
    copies = [pltpu.make_async_copy(w, room, scratch[-1].at[i]) for i, (w, room) in enumerate(zip(hbm, scratch))]
    for copy in copies:
        copy.start()
    finish(copies)
    table = scratch[-2]
    vmem = scratch[6 : len(hbm)]
    table[...] = jnp.zeros_like(table)
    short = [v for v in vmem if v.shape[1] == vmem[0].shape[1]]
    (long,) = [v for v in vmem if v.shape[1] != vmem[0].shape[1]]
    layers = long.shape[0]
    for layer in range(layers):
        for i, v in enumerate(short):
            at = layer * len(short) + i
            table[at : at + 1, 0 : v.shape[1]] = v[layer : layer + 1, :].astype(F32)
        at = layers * len(short) + layer
        table[at : at + 1, 0 : long.shape[1]] = long[layer : layer + 1, :].astype(F32)
    q, k, v, o, up, down = scratch[:6]
    for layer in range(layers):
        for place, hand in ((0, core), (1, 1 - core)):
            four, wide, tall = outs[6 * layer + 3 * place : 6 * layer + 3 * place + 3]
            part = q.shape[2] // 2
            at = pl.ds(pl.multiple_of(hand * part, 128), part)
            for i, w in enumerate((q, k, v, o)):
                four[:, i * part : (i + 1) * part] = w[layer, :, at]
            if four.shape[1] > 4 * part:
                four[:, 4 * part :] = table[...].astype(BF16)
            part = up.shape[2] // 2
            wide[...] = up[layer, :, pl.ds(pl.multiple_of(hand * part, 128), part)]
            part = down.shape[2] // 2
            tall[...] = down[layer, :, pl.ds(pl.multiple_of(hand * part, 128), part)]


def join_rows(smem, vmem, hbm, outs, scratch, kinds):
    (tab,) = smem
    first = tab[tab.shape[0] - 1] == 0
    (out,) = outs
    rows = out.shape[0] // len(kinds)
    for i, kind in enumerate(kinds):
        mine, came = vmem[2 * i][...].astype(F32), vmem[2 * i + 1][...].astype(F32)
        upper, lower = jnp.where(first, mine, came), jnp.where(first, came, mine)
        at = slice(i * rows, (i + 1) * rows)
        if kind != "down":
            out[at, :] = jnp.concatenate([upper, lower], axis=0).astype(BF16)
            continue
        wide = upper.shape[1]
        for g in range(4):
            part = (upper, lower)[g // 2][g % 2 * rows : (g % 2 + 1) * rows]
            out[at, g * wide : (g + 1) * wide] = part.astype(BF16)


def place_vectors(smem, vmem, hbm, outs, scratch):
    (tab,) = smem
    room, sems = scratch
    half, rows, side = room.shape[0] // 2, room.shape[1], room.shape[2]
    copies = []
    for i, part in enumerate(hbm):
        source = part.at[:, :, pl.ds(part.shape[2] - side, side)]
        copies.append(pltpu.make_async_copy(source, room.at[pl.ds(i * half, half)], sems.at[i]))
        copies[-1].start()
    finish(copies)
    width = outs[0].shape[1]
    own = rows // 2
    devices = 4 * half
    count = width // devices
    wide = outs[0].shape[0] - 8
    short = jnp.zeros((16, width), F32)
    long = [jnp.zeros((8, width), F32) for _ in range(wide)]
    for b in range(2 * half):
        block = room[b].astype(F32)
        for k in (0, 1):
            device = 2 * tab[b] + k
            part = block[k * own : (k + 1) * own]
            part = jnp.concatenate([part, jnp.zeros((own, width - side), F32)], axis=1)
            short = short + pltpu.roll(part[:16], device * count, 1)
            start = device * count * wide
            moved = pltpu.roll(part[16:24], start % width, 1)
            for i in range(wide):
                long[i] = long[i] + jnp.where(start // width == i, moved, 0.0)
    for layer, out in enumerate(outs):
        out[0:8, :] = short[8 * layer : 8 * layer + 8]
        for i in range(wide):
            out[8 + i : 9 + i, :] = long[i][layer : layer + 1]


def join_blocks(smem, vmem, hbm, outs, scratch, rows_at=0):
    (out,) = outs
    (sems,) = scratch
    at = 0
    copies = []
    for part in hbm:
        if len(part.shape) == 3:
            source, target = part, out.at[pl.ds(at, part.shape[0])]
            at += part.shape[0]
        else:
            source, target = part.at[pl.ds(rows_at, out.shape[1])], out.at[at]
            at += 1
        copies.append(pltpu.make_async_copy(source, target, sems.at[len(copies)]))
        copies[-1].start()
    finish(copies)


def attend_forward(smem, vmem, hbm, outs, scratch, sections, seq):
    (tab,) = smem
    x, vec, mask = vmem
    q, k, v, p, context, unit, scale, middle = outs[:8]
    whole, o_whole = outs[8].room, outs[9].room
    sems, o_sems = scratch[:2]
    half = x.shape[1] // 2
    sides = fetch(tab, hbm, "four", sections[0], whole, sems, columns=(0, 3 * half), step=3 * half)
    late = fetch(tab, hbm, "four", sections[0], o_whole, o_sems, columns=(3 * half, 4 * half))
    if len(outs) > 10:
        for i, item in enumerate(put_rows_apart(x, scratch[2], seq)):
            outs[10][i * ITEM : (i + 1) * ITEM, :] = item.astype(BF16)
        x = outs[10]
        x.send()
    core = tab[tab.shape[0] - 1]
    for steps, h in zip(sides, (core, 1 - core)):
        finish(steps[0])
        at = pl.ds(pl.multiple_of(h * half, 128), half)
        made = mm(x[...], whole[h])
        if h is not core:
            outs[8].send()
        q[:, at] = (made[:, 0:half] + vec[Q_B : Q_B + 1, at]).astype(BF16)
        k[:, at] = made[:, half : 2 * half].astype(BF16)
        v[:, at] = (made[:, 2 * half :] + vec[V_B : V_B + 1, at]).astype(BF16)
    low = lax.broadcasted_iota(jnp.int32, (ITEM, 2 * HEAD_DIM), 1) < HEAD_DIM
    items = x.shape[0] // ITEM

    for i in range(HEADS // 2):
        at = slice(i * 2 * HEAD_DIM, (i + 1) * 2 * HEAD_DIM)
        for item in range(items):
            rows = slice(item * ITEM, (item + 1) * ITEM)
            qs, ks, vs = q[rows, at], k[rows, at], v[rows, at]
            made = []
            for side in (0, 1):
                own = low if side == 0 else jnp.logical_not(low)
                s = mm_nt(jnp.where(own, qs, jnp.zeros_like(qs)), ks) * 0.125 + mask[item]
                e = jnp.exp(s - jnp.max(s, axis=-1, keepdims=True))
                w = (e * (1.0 / jnp.sum(e, axis=-1, keepdims=True))).astype(BF16)
                p[item * HEADS + 2 * i + side] = w
                made.append(mm(w, vs))
            context[rows, at] = jnp.where(low, made[0], made[1]).astype(BF16)
    finish_all(late)
    for out in (q, k, v, p, context, outs[9]):
        out.send()
    attended = jnp.concatenate([mm(context[...], o_whole[h]) for h in (0, 1)], axis=1)
    first = x[...].astype(F32) + (attended + vec[O_B : O_B + 1, :])
    made, made_scale = norm_rows(first)
    unit[...] = made
    scale[...] = made_scale
    middle[...] = (made * vec[G_ONE : G_ONE + 1, :] + vec[S_ONE : S_ONE + 1, :]).astype(BF16)


def lift(smem, vmem, hbm, outs, scratch, sections):
    (tab,) = smem
    middle, vec = vmem
    activated, slope, kept = outs
    whole = kept.room
    (sems,) = scratch
    width = vec.shape[1]
    sides = fetch(tab, hbm, "up", sections[0], whole, sems, step=width)
    core = tab[tab.shape[0] - 1]
    step = width // 3
    for steps, h in zip(sides, (core, 1 - core)):
        for i, copies in enumerate(steps):
            finish(copies)
            for j in range(3):
                at = slice(i * width + j * step, i * width + (j + 1) * step)
                bias = vec[pl.ds(UP_B + h * len(steps) + i, 1), j * step : (j + 1) * step]
                a, s = gelu_and_slope(mm(middle[...], whole[h, :, at]) + bias)
                activated[h, :, at] = a.astype(BF16)
                slope[h, :, at] = s.astype(BF16)
    kept.send()


def lower(smem, vmem, hbm, outs, scratch, sections, seq):
    (tab,) = smem
    activated, middle, vec = vmem
    output, unit, scale, kept = outs
    whole = kept.room
    finish_all(fetch(tab, hbm, "down", sections[0], whole, scratch[0]))
    kept.send()
    deep = activated.shape[2]
    lowered = mm(activated[0], whole[0:deep, :]) + mm(activated[1], whole[deep:, :])
    second = middle[...].astype(F32) + (lowered + vec[D_B : D_B + 1, :])
    made, made_scale = norm_rows(second)
    unit[...] = made
    scale[...] = made_scale
    made = made * vec[G_TWO : G_TWO + 1, :] + vec[S_TWO : S_TWO + 1, :]
    if len(scratch) > 1:
        put_rows_together(made, scratch[1], seq)
        output[...] = scratch[1][...].astype(BF16)
    else:
        output[...] = made.astype(BF16)


def rows_sum(values):
    return jnp.sum(values, axis=0, keepdims=True)


SUM_G_TWO, SUM_S_TWO, SUM_D_B, SUM_UP_B = 0, 1, 2, 8
SUM_G_ONE, SUM_S_ONE, SUM_O_B = 0, 1, 2


def feed_back(smem, vmem, hbm, outs, scratch, seq):
    (tab,) = smem
    grad, unit_two, scale_two, vec, activated, down_whole, slope, middle = vmem
    sum_grad, lifted_grad, down_send, down_keep, up_send, up_keep, sums = outs
    turned, low_grad = scratch[:2]
    chips, rows, part = up_send.shape
    core = tab[4 * chips]
    if len(scratch) > 2:
        g = jnp.concatenate(put_rows_apart(grad, scratch[2], seq), axis=0)
    else:
        g = grad[...]
    u = unit_two[...]
    made = norm_rows_back(u, scale_two[...], g * vec[G_TWO : G_TWO + 1, :])
    sum_grad[...] = made
    sum_grad.send()
    low = made.astype(BF16)
    half = low.shape[1] // 2
    low_grad[0] = low[:, :half]
    low_grad[1] = low[:, half:]
    sums[...] = jnp.zeros_like(sums)
    sums[SUM_G_TWO : SUM_G_TWO + 1, :] = rows_sum(g * u)
    sums[SUM_S_TWO : SUM_S_TWO + 1, :] = rows_sum(g)
    sums[SUM_D_B : SUM_D_B + 1, :] = rows_sum(low.astype(F32))
    activated.ready()
    for one in (down_whole, slope, middle):
        one.begin()
    deep = activated.shape[2]
    wide = part // 4
    for out, hand, places in ((down_send, 1 - core, 3), (down_keep, core, 2)):
        right = low_grad[hand]
        for h in (0, 1):
            for j in range(deep // (8 * rows)):
                made = mm_tn(activated[h, :, 8 * rows * j : 8 * rows * (j + 1)], right).astype(BF16)
                for i in (0, 1):
                    chip = h * deep // (4 * rows) + 2 * j + i
                    to = tab[places * chips + chip]
                    for g in range(4):
                        at = (4 * i + g) * rows
                        out[to, :, g * wide : (g + 1) * wide] = made[at : at + rows]
    for out in (down_send, down_keep):
        out.send()
    turned[...] = middle[...].T
    down_whole.ready()
    slope.ready()
    width = sums.shape[1]
    step = width
    for h in (0, 1):
        for j in range(part // step):
            at = slice(j * step, (j + 1) * step)
            rows_at = slice(h * part + j * step, h * part + (j + 1) * step)
            made = mm_nt(low, down_whole[rows_at, :])
            made = (made * slope[h, :, at].astype(F32)).astype(BF16)
            lifted_grad[h, :, at] = made
            column = h * part + j * step
            to = SUM_UP_B + column // width
            sums[to : to + 1, column % width : column % width + step] = rows_sum(made.astype(F32))
    lifted_grad.send()
    for out, hand, places in ((up_send, 1 - core, 3), (up_keep, core, 2)):
        for j in range(part // step):
            at = slice(j * step, (j + 1) * step)
            made = mm(turned[...], lifted_grad[hand, :, at]).astype(BF16)
            for chip in range(chips):
                out[tab[places * chips + chip], :, at] = made[chip * rows : (chip + 1) * rows]
        out.send()


def first_norm_back(smem, vmem, hbm, outs, scratch):
    lifted_grad, up_whole, sum_grad, unit_one, scale_one, vec = vmem
    first_grad, attended_grad, sums = outs
    sums[...] = jnp.zeros_like(sums)
    g = sum_grad[...] + mm_nt(lifted_grad[0], up_whole[0]) + mm_nt(lifted_grad[1], up_whole[1])
    u = unit_one[...]
    made = norm_rows_back(u, scale_one[...], g * vec[G_ONE : G_ONE + 1, :])
    first_grad[...] = made
    low = made.astype(BF16)
    half = low.shape[1] // 2
    attended_grad[0] = low[:, :half]
    attended_grad[1] = low[:, half:]
    sums[SUM_G_ONE : SUM_G_ONE + 1, :] = rows_sum(g * u)
    sums[SUM_S_ONE : SUM_S_ONE + 1, :] = rows_sum(g)
    sums[SUM_O_B : SUM_O_B + 1, :] = rows_sum(low.astype(F32))


def attend_back(smem, vmem, hbm, outs, scratch):
    (tab,) = smem
    attended_grad, o_whole, q, k, v, p, x, context = vmem[:8]
    send, keep, sums, grads = outs
    x_turned, c_turned, context_grad = scratch[:3]
    chips, rows, _ = send.shape
    half = x.shape[1] // 2
    core = tab[4 * chips]
    x_turned[...] = x[...].T
    c_turned[...] = context[...].T
    made = mm_nt(attended_grad[0], o_whole[0]) + mm_nt(attended_grad[1], o_whole[1])
    context_grad[...] = made.astype(BF16)
    items = q.shape[0] // ITEM
    low = lax.broadcasted_iota(jnp.int32, (ITEM, 2 * HEAD_DIM), 1) < HEAD_DIM
    pairs = HEADS // 4
    sides = (low, jnp.logical_not(low))
    apart = lambda values: [jnp.where(own, values, jnp.zeros_like(values)) for own in sides]
    for h in (0, 1):
        grads[h, :, 3 * half :] = attended_grad[h]
        for i in range(pairs):
            at = slice(h * half + i * 2 * HEAD_DIM, h * half + (i + 1) * 2 * HEAD_DIM)
            for item in range(items):
                rows_at = slice(item * ITEM, (item + 1) * ITEM)
                qs, ks, vs, cs = q[rows_at, at], k[rows_at, at], v[rows_at, at], context_grad[rows_at, at]
                ws = [p[item * HEADS + 2 * (h * pairs + i) + side] for side in (0, 1)]
                ds = []
                for w, c in zip(ws, apart(cs)):
                    wide = w.astype(F32)
                    g = wide * mm_nt(c, vs)
                    ds.append((g - wide * jnp.sum(g, axis=-1, keepdims=True)).astype(BF16))
                stacked = lambda values: jnp.concatenate(apart(values), axis=0)
                made = (
                    mm(jnp.concatenate(ds, axis=1), stacked(ks)) * 0.125,
                    mm_tn(jnp.concatenate(ds, axis=0), stacked(qs)) * 0.125,
                    mm_tn(jnp.concatenate(ws, axis=0), stacked(cs)),
                )
                for place, both in enumerate(made):
                    start = place * half + i * 2 * HEAD_DIM
                    grads[h, rows_at, start : start + 2 * HEAD_DIM] = both.astype(BF16)
    grads.send()
    for out, hand, places in ((send, 1 - core, 3), (keep, core, 2)):
        for j in range(4):
            at = slice(j * half, (j + 1) * half)
            made = mm((c_turned if j == 3 else x_turned)[...], grads[hand, :, at]).astype(BF16)
            for chip in range(chips):
                out[tab[places * chips + chip], :, at] = made[chip * rows : (chip + 1) * rows]
        if len(vmem) == 8:
            out.send()
    sums[...] = jnp.zeros_like(sums)
    for h in (0, 1):
        at = slice(h * half, (h + 1) * half)
        sums[0:1, at] = rows_sum(grads[h, :, 0:half].astype(F32))
        sums[1:2, at] = rows_sum(grads[h, :, 2 * half : 3 * half].astype(F32))
    if len(vmem) == 8:
        return
    short, long = scratch[3:5]
    wide = long.shape[0] // 2
    for layer, (feed, other, four) in enumerate((vmem[8:10] + [sums], vmem[10:13])):
        at = layer * 8
        short[at : at + 2, :] = four[0:2, :]
        short[at + 2 : at + 3, :] = other[SUM_O_B : SUM_O_B + 1, :]
        short[at + 3 : at + 5, :] = other[SUM_G_ONE : SUM_G_ONE + 2, :]
        short[at + 5 : at + 6, :] = feed[SUM_D_B : SUM_D_B + 1, :]
        short[at + 6 : at + 8, :] = feed[SUM_G_TWO : SUM_G_TWO + 2, :]
        long[layer * wide : (layer + 1) * wide, :] = feed[SUM_UP_B : SUM_UP_B + wide, :]
    width = x.shape[1]
    side = send.shape[2] - 4 * half
    count = width // (2 * chips)
    lanes = lax.broadcasted_iota(jnp.int32, (16, side), 1)
    last = lax.broadcasted_iota(jnp.int32, (8, side), 0)
    for chip in range(chips):
        shares = []
        for device in (2 * chip, 2 * chip + 1):
            part = pltpu.roll(short[...], (width - device * count) % width, 1)[:, :side]
            shares.append(jnp.where(lanes < count, part, 0.0))
            start = device * count * wide
            turn = (width - start % width) % width
            part = pltpu.roll(long[...], turn, 1)[:, :side]
            first, second = start // width, wide + start // width
            part = jnp.where(last == 0, part[first : first + 1], jnp.where(last == 1, part[second : second + 1], 0.0))
            shares.append(jnp.where(lanes[:8] < count * wide, part, 0.0))
        block = jnp.concatenate(shares, axis=0).astype(BF16)
        for out, places in ((send, 3), (keep, 2)):
            out[tab[places * chips + chip], :, 4 * half :] = block


def attend_back_last(smem, vmem, hbm, outs, scratch, seq):
    first_grad, grads, whole = vmem
    (out,) = outs
    deep = whole.shape[2]
    made = first_grad[...] + mm_nt(grads[0, :, :deep], whole[0]) + mm_nt(grads[1, :, :deep], whole[1])
    if out.shape[0] == made.shape[0]:
        out[...] = made
    else:
        put_rows_together(made, out, seq)


def add_halves(smem, vmem, hbm, outs, scratch):
    send, kept = outs
    half = send.shape[0]
    rows = send.shape[1] // (len(vmem) // 2)

    def block(b, carry):
        for i in range(len(vmem) // 2):
            keep, came = vmem[2 * i], vmem[2 * i + 1]
            at = slice(i * rows, (i + 1) * rows)
            kept[b, at] = (keep[b].astype(F32) + came[b].astype(F32)).astype(BF16)
            send[b, at] = (keep[half + b].astype(F32) + came[half + b].astype(F32)).astype(BF16)
        return carry

    lax.fori_loop(0, half, block, 0)


def add_spread(smem, vmem, hbm, outs, scratch):
    at = 0
    for keep, came in zip(vmem[0::2], vmem[1::2]):
        rows = keep.shape[1]
        for b, out in enumerate(outs):
            out[at : at + rows] = (keep[b].astype(F32) + came[b].astype(F32)).astype(out.dtype)
        at += rows


def add_last(smem, vmem, hbm, outs, scratch, kinds=()):
    (tab,) = smem
    core = tab[tab.shape[0] - 1]
    (total,) = scratch
    made = vmem[0][...].astype(F32)
    for came in vmem[1:]:
        made = made + came[...].astype(F32)
    total[...] = made
    rows = total.shape[0] // len(kinds)
    half = rows // 2
    for i, kind in enumerate(kinds):
        to = slice(i * half, (i + 1) * half)
        for out, hand in zip(outs, (core, 1 - core)):
            if kind == "down":
                wide = total.shape[1] // 2
                at = pl.ds(pl.multiple_of(hand * wide, 128), wide)
                for g in (0, 1):
                    part = total[i * rows + g * half : i * rows + (g + 1) * half, at]
                    out[to, g * wide : (g + 1) * wide] = part
            else:
                out[to, :] = total[pl.ds(pl.multiple_of(i * rows + hand * half, 8), half), :]


def write_out(smem, vmem, hbm, outs, scratch, kind, sections):
    (tab,) = smem
    core = tab[tab.shape[0] - 1]
    half = outs[0].shape[2] // 2
    for layer, section in enumerate(sections):
        for hand, part in ((core, vmem[2 * layer]), (1 - core, vmem[2 * layer + 1])):
            at = pl.ds(pl.multiple_of(hand * half, 128), half)
            if kind == "down":
                rows = outs[0].shape[1] // 4
                for g in range(4):
                    start = (g % 2 * 2 + g // 2) * half
                    to = slice(g * rows, (g + 1) * rows)
                    outs[0][layer, to, at] = part[section * rows : (section + 1) * rows, start : start + half]
                continue
            rows = outs[0].shape[1]
            for i, out in enumerate(outs[:4] if kind == "four" else outs):
                out[layer, :, at] = part[section * rows : (section + 1) * rows, i * half : (i + 1) * half]
    if kind != "four":
        return
    part = vmem[0]
    start = 4 * half
    for i, out in enumerate(outs[4:]):
        count = out.shape[1]
        for layer in range(out.shape[0]):
            at = 16 + layer if i == 8 else 8 * layer + i
            out[layer : layer + 1, :] = part[at : at + 1, start : start + count]


class Chain:
    def __init__(self):
        self.token = None

    def __call__(self, body, outs, after=(), **kinds):
        deps = list(after) + ([] if self.token is None else [self.token])
        made = launch(body, outs, deps=deps, **kinds)
        self.token = min(made, key=lambda m: m.size)
        return made


def blocks(weights, small, mask, hidden, cotangent, seq):
    q_weight, k_weight, v_weight, o_weight, up_weight, down_weight = weights
    owners = lax.axis_size("dp")
    chips = owners // 2
    depth = chips // 4
    layers, rows, width = q_weight.shape
    wide = up_weight.shape[2]
    tall = hidden.shape[0] // seq * ITEM
    tab = table_of(owners)
    chain = Chain()
    dma = lambda n: pltpu.SemaphoreType.DMA((n,))
    vmem = lambda shape, dtype: pltpu.VMEM(shape, dtype)
    xy_one = lambda v: flip(v, owners, 2, 4)
    xy_two = lambda v: flip(v, owners, 4, 2)
    core_flip = lambda v: flip(v, owners, 1, 1)
    z_flip = lambda v, k: flip(v, owners, 8 * k, 8 * k)
    order = [v for v in small if v.shape[1] == rows] + [v for v in small if v.shape[1] != rows]

    side = 128
    block = (2 * rows, 2 * width)
    kinds = ("four", "up", "down")
    groups = [[(layer, kind)] for layer in range(layers) for kind in kinds]
    shapes = [(len(g) * block[0], block[1] + (side if i == 0 else 0)) for i, g in enumerate(groups)]
    halves = lambda layer: [((rows, 2 * width + (0 if layer else side)), BF16), ((rows, wide // 2), BF16), ((down_weight.shape[1], width // 2), BF16)]
    split = chain(
        split_own, [h for layer in range(layers) for h in halves(layer) * 2], smem=[tab], hbm=list(weights) + order, far=pltpu.HBM,
        scratch=[vmem(w.shape, BF16) for w in list(weights) + order] + [vmem((rows, side), F32), dma(6 + len(order))], extra=57,
    )
    mine = {(layer, kind): split[6 * layer + i] for layer in range(layers) for i, kind in enumerate(kinds)}
    other = {(layer, kind): core_flip(split[6 * layer + 3 + i]) for layer in range(layers) for i, kind in enumerate(kinds)}
    own, z_came, x_one, x_two, stacked, near, far = ({} for _ in range(7))

    direct = 2
    rest = [piece for group in groups[direct:] for piece in group]
    row_of = {piece: i * block[0] for i, piece in enumerate(rest)}

    def join(pieces, shape):
        (made,) = chain(
            functools.partial(join_rows, kinds=tuple(kind for _, kind in pieces)), [(shape, BF16)], smem=[tab],
            vmem=[v for piece in pieces for v in (mine[piece], other[piece])],
        )
        return made

    def begin():
        for g in range(direct):
            own[g] = join(groups[g], shapes[g])
            z_came[g] = [z_flip(own[g], k) for k in range(1, depth)]
        own["rest"] = join(rest, (len(rest) * block[0], block[1]))
        z_came["rest"] = z_flip(own["rest"], 1)

    def stack(sources, count, shape, rows_at=0, after=()):
        (made,) = chain(functools.partial(join_blocks, rows_at=rows_at), [((count,) + shape, BF16)], hbm=sources, scratch=[dma(count)], after=after)
        return made

    def far_round(g):
        stacked[g] = stack([own["rest"], z_came["rest"]], 2, shapes[g], row_of[groups[g][0]])
        z_came[g, 2] = z_flip(stacked[g], 2)

    def first_stack(g, after=()):
        sources = [own[g]] + z_came[g] if g < direct else [stacked[g], z_came[g, 2]]
        stacked[g] = stack(sources, depth, shapes[g], after=after)
        x_one[g] = xy_one(stacked[g])

    def second_stack(g, after=()):
        made = stack([stacked[g], x_one[g]], 2 * depth, shapes[g], after=after)
        x_two[g] = xy_two(made)
        near[g] = [made, x_two[g]]
        far[g] = [core_flip(made)]

    def third(g):
        value = lax.optimization_barrier((x_two[g], chain.token))[0]
        x_two[g] = value
        near[g][1] = value
        far[g].append(core_flip(value))

    def parts(layer, kind):
        (g,) = [i for i, group in enumerate(groups) if (layer, kind) in group]
        return near[g] + far[g]

    def section(layer, kind):
        return [group.index((layer, kind)) for group in groups if (layer, kind) in group][0]

    height = {"four": width, "up": width, "down": wide}
    across = {"four": 2 * width, "up": wide // 2, "down": width // 2}
    whole = lambda kind, columns=None: [vmem((2, height[kind], columns or across[kind]), BF16), dma(8 * chips)]
    xs, kept = [hidden], [{} for _ in range(layers)]
    row = lambda dtype: ((tall, width), dtype)
    column = ((tall, 1), F32)
    deep = ((2, tall, wide // 2), BF16)
    items = tall // ITEM

    def forward_attend(layer):
        s = kept[layer]
        raw = xs[layer].shape[0] != tall
        made = chain(
            functools.partial(attend_forward, sections=[section(layer, "four")], seq=seq),
            [row(BF16)] * 3 + [((items * HEADS, ITEM, ITEM), BF16), row(BF16), row(F32), column, row(BF16)]
            + [((2, width, width * 3 // 2), BF16), ((2, width, width // 2), BF16)] + [row(BF16)] * raw,
            held=True, smem=[tab], vmem=[xs[layer], vec[layer], mask], hbm=parts(layer, "four"),
            scratch=[dma(8 * chips)] * 2 + [vmem((tall, width), F32)] * raw,
        )
        s["q"], s["k"], s["v"], s["p"], s["context"], s["unit_one"], s["scale_one"], s["middle"] = made[:8]
        s["three"], s["o"] = made[8:10]
        if raw:
            xs[layer] = made[10]

    def forward_lift(layer):
        s = kept[layer]
        s["activated"], s["slope"], s["up"] = chain(
            functools.partial(lift, sections=[section(layer, "up")]), [deep, deep, ((2, width, wide // 2), BF16)],
            held=True, smem=[tab], vmem=[s["middle"], vec[layer]], hbm=parts(layer, "up"), scratch=[dma(8 * chips)],
        )

    def forward_lower(layer):
        s = kept[layer]
        last_one = layer == layers - 1
        shape = hidden.shape if last_one else (tall, width)
        output, s["unit_two"], s["scale_two"], s["down"] = chain(
            functools.partial(lower, sections=[section(layer, "down")], seq=seq),
            [(shape, BF16), row(F32), column, ((wide, width), BF16)],
            held=True, smem=[tab], vmem=[s["activated"], s["middle"], vec[layer]], hbm=parts(layer, "down"),
            scratch=[dma(8 * chips)] + [vmem(shape, F32)] * last_one,
        )
        xs.append(output)

    begin()
    first_stack(0)
    second_stack(0)
    first_stack(1)
    far_round(2)
    vec = chain(
        place_vectors, [((8 + wide // width, width), F32)] * layers, smem=[tab], hbm=near[0],
        scratch=[vmem((chips, block[0], side), BF16), dma(2)],
    )
    third(0)
    second_stack(1)
    first_stack(2)
    far_round(3)
    forward_attend(0)
    third(1)
    second_stack(2)
    first_stack(3)
    far_round(4)
    forward_lift(0)
    third(2)
    second_stack(3)
    first_stack(4)
    far_round(5)
    forward_lower(0)
    third(3)
    second_stack(4)
    first_stack(5)
    forward_attend(1)
    third(4)
    second_stack(5)
    forward_lift(1)
    third(5)
    forward_lower(1)

    keep, came, fanned, last = {}, {}, {}, {}
    sums = [{} for _ in range(layers)]
    flowing = [None] * (layers + 1)
    flowing[layers] = cotangent
    pair = lambda extra=0: [((chips, block[0], block[1] + extra), BF16)] * 2

    def leave(piece, send, kept_blocks):
        keep[piece] = kept_blocks
        came[piece] = core_flip(send)

    def back_feed(layer):
        s = kept[layer]
        raw = flowing[layer + 1].shape[0] != tall
        s["sum_grad"], s["lifted_grad"], d_send, d_keep, u_send, u_keep, sums[layer]["feed"] = chain(
            functools.partial(feed_back, seq=seq), [row(F32), deep] + pair() * 2 + [((16, width), F32)], held=True,
            smem=[tab],
            vmem=[flowing[layer + 1], s["unit_two"], s["scale_two"], vec[layer], s["activated"], s["down"], s["slope"],
                  s["middle"]],
            late=(5, 6, 7),
            scratch=[vmem((width, tall), BF16), vmem((2, tall, width // 2), BF16)] + [vmem((tall, width), F32)] * raw,
        )
        leave((layer, "down"), d_send, d_keep)
        leave((layer, "up"), u_send, u_keep)

    def back_norm(layer):
        s = kept[layer]
        s["first_grad"], s["attended_grad"], sums[layer]["norm"] = chain(
            first_norm_back, [row(F32), ((2, tall, width // 2), BF16), ((8, width), F32)], held=True,
            vmem=[s["lifted_grad"], s["up"], s["sum_grad"], s["unit_one"], s["scale_one"], vec[layer]],
        )

    def back_attend(layer):
        s = kept[layer]
        more, room = [], []
        if layer == 0:
            more = [sums[0]["feed"], sums[0]["norm"], sums[1]["feed"], sums[1]["norm"], sums[1]["four"]]
            room = [vmem((16, width), F32), vmem((2 * wide // width, width), F32)]
        send, rest, sums[layer]["four"], s["grads"] = chain(
            attend_back, pair(0 if layer else side) + [((8, width), F32), ((2, tall, 2 * width), BF16)], held=True,
            smem=[tab],
            vmem=[s["attended_grad"], s["o"], s["q"], s["k"], s["v"], s["p"], xs[layer], s["context"]] + more,
            scratch=[vmem((width, tall), BF16)] * 2 + [vmem((tall, width), BF16)] + room,
        )
        leave((layer, "four"), send, rest)

    def back_last(layer):
        s = kept[layer]
        shape = (tall, width) if layer else hidden.shape
        (flowing[layer],) = chain(
            functools.partial(attend_back_last, seq=seq), [(shape, F32)], held=True,
            vmem=[s["first_grad"], s["grads"], s["three"]],
        )

    def fold(*pieces, after=()):
        half = keep[pieces[0]].shape[0] // 2
        r, c = keep[pieces[0]].shape[1:]
        at = pieces if len(pieces) > 1 else pieces[0]
        send, keep[at] = chain(add_halves, [((half, r * len(pieces), c), BF16)] * 2, vmem=[v for piece in pieces for v in (keep[piece], came[piece])], after=after)
        came[at] = xy_two(send) if half == 2 * depth else xy_one(send)

    def fan(*ats):
        at = ats[0] if len(ats) == 1 else sum((a if isinstance(a[0], tuple) else (a,) for a in ats), ())
        shape = (sum(keep[a].shape[1] for a in ats), keep[ats[0]].shape[2])
        made = chain(add_spread, [(shape, F32)] + [(shape, BF16)] * (depth - 1), vmem=[v for a in ats for v in (keep[a], came[a])])
        keep[at] = made[0]
        fanned[at] = [z_flip(made[k], k) for k in range(1, depth)]

    def total(at, after=()):
        pieces = at if isinstance(at[0], tuple) else (at,)
        shape = keep[at].shape
        made = chain(
            functools.partial(add_last, kinds=tuple(kind for _, kind in pieces)), [((shape[0] // 2, shape[1]), F32)] * 2,
            smem=[tab], vmem=[keep[at]] + fanned[at], scratch=[vmem(shape, F32)], after=after,
        )
        both = [made[0], core_flip(made[1])]
        for i, piece in enumerate(pieces):
            last[piece] = (both, i)
        return both[1:]

    def finished(kind, count):
        own_rows = down_weight.shape[1] if kind == "down" else rows
        columns = wide if kind == "up" else width
        outs = [((layers, own_rows, columns), F32)] * count
        if kind == "four":
            outs += [(v.shape, F32) for v in order]
        return chain(
            functools.partial(write_out, kind=kind, sections=[last[layer, kind][1] for layer in range(layers)]), outs,
            smem=[tab], vmem=[v for layer in range(layers) for v in last[layer, kind][0]],
        )

    d1, u1, f1, d0, u0, f0 = [(layer, kind) for layer in (1, 0) for kind in ("down", "up", "four")]
    back_feed(1)
    back_norm(1)
    fold(d1, u1)
    back_attend(1)
    back_last(1)
    fold(f1)
    back_feed(0)
    fold((d1, u1))
    fold(f1)
    back_norm(0)
    fold(d0, u0)
    back_attend(0)
    fan((d1, u1), f1)
    back_last(0)
    fold((d0, u0))
    fold(f0)
    done = total((d1, u1, f1))
    fan((d0, u0))
    fold(f0, after=done)
    fan(f0)
    total((d0, u0))
    total(f0)
    (down_grad,) = finished("down", 1)
    (up_grad,) = finished("up", 1)
    grads = finished("four", 4)
    q_b, v_b, o_b, g_one, s_one, d_b, g_two, s_two, u_b = grads[4:]
    return (
        xs[-1], flowing[0], *grads[:4],
        q_b, v_b, o_b, g_one, s_one, up_grad, u_b, down_grad, d_b, g_two, s_two,
    )


def shards(
    hidden, region_count, text_mask,
    q_weight, k_weight, v_weight, o_weight, q_bias, v_bias, o_bias, gain_one, shift_one,
    up_weight, up_bias, down_weight, down_bias, gain_two, shift_two, cotangent,
):
    owners = lax.axis_size("dp")
    valid_keys = slot_valid(region_count, text_mask)
    weights = (q_weight, k_weight, v_weight, o_weight, up_weight, down_weight)
    small = (q_bias, v_bias, o_bias, gain_one, shift_one, up_bias, down_bias, gain_two, shift_two)
    seq = valid_keys.shape[1]
    width = hidden.shape[1]
    fits = (
        owners in (16, 32)
        and q_weight.shape[1] % 8 == 0
        and up_weight.shape[2] % (2 * width) == 0
        and seq <= ITEM
        and q_weight.shape[0] == 2
    )
    if not fits:
        return plain(weights, small, valid_keys, hidden, cotangent)
    mask = (valid_keys - 1.0) * 10000.0
    mask = jnp.pad(mask, ((0, 0), (0, ITEM - seq)), constant_values=PAD)[:, None, :]
    return blocks(weights, small, mask, hidden, cotangent, seq)


def solution(mesh):
    rows = P("dp", None)
    matrix = P(None, "dp", None)
    vector = P(None, "dp")
    four = (matrix,) * 4
    return jax.shard_map(
        shards,
        mesh=mesh,
        in_specs=(rows, P("dp"), rows) + four + (vector,) * 5
        + (matrix, vector, matrix, vector, vector, vector, rows),
        out_specs=(rows, rows) + four + (vector,) * 5
        + (matrix, vector, matrix, vector, vector, vector),
        check_vma=False,
    )
```

```python
import functools
import math

import jax
import jax.numpy as jnp
from jax import lax
from jax.experimental import pallas as pl
from jax.experimental.pallas import tpu as pltpu
from jax.sharding import PartitionSpec as P

HEADS = 12
HEAD_DIM = 64
REGIONS = 100

epsilon = 1e-12
F32 = jnp.float32
BF16 = jnp.bfloat16


def dense(left, right):
    return jnp.dot(left, right, preferred_element_type=F32)


def outer(left, right):
    return lax.dot_general(left, right, (((0,), (0,)), ((), ())), preferred_element_type=F32)


def back_dense(left, right):
    return lax.dot_general(left, right, (((1,), (1,)), ((), ())), preferred_element_type=F32)


def column_sum(values):
    return jnp.sum(values.astype(F32), axis=0)


def slot_valid(region_count, text_mask):
    region_slot = jnp.arange(REGIONS, dtype=jnp.int32)[None, :] < region_count[:, None]
    return jnp.concatenate([text_mask.astype(F32), region_slot.astype(F32)], axis=1)


def norm(values, gain, shift):
    center = values - jnp.mean(values, axis=-1, keepdims=True)
    spread = jnp.mean(center * center, axis=-1, keepdims=True)
    scale = lax.rsqrt(spread + epsilon)
    unit = center * scale
    return unit * gain + shift, (unit, scale)


def norm_back(saved, gain, grad):
    unit, scale = saved
    inner = grad * gain
    into = scale * (
        inner
        - jnp.mean(inner, axis=-1, keepdims=True)
        - unit * jnp.mean(inner * unit, axis=-1, keepdims=True)
    )
    return into, column_sum(grad * unit), column_sum(grad)


def forward_layer(inputs, weights, vectors, valid_keys):
    q_weight, k_weight, v_weight, o_weight, up_weight, down_weight = weights
    q_bias, v_bias, o_bias, gain_one, shift_one, up_bias, down_bias, gain_two, shift_two = vectors
    item_count = valid_keys.shape[0]
    row_count, width = inputs.shape

    def heads_of(values):
        return values.reshape(item_count, row_count // item_count, HEADS, HEAD_DIM)

    queries = heads_of((dense(inputs, q_weight) + q_bias).astype(BF16))
    key_rows = heads_of(dense(inputs, k_weight).astype(BF16))
    value_rows = heads_of((dense(inputs, v_weight) + v_bias).astype(BF16))
    scores = (
        jnp.einsum("bqhd,bkhd->bhqk", queries, key_rows, preferred_element_type=F32) * 0.125
    )
    scores = scores + (valid_keys[:, None, None, :] - 1.0) * 10000.0
    attention = jax.nn.softmax(scores, axis=-1)
    attention_low = attention.astype(BF16)
    context = jnp.einsum("bhqk,bkhd->bqhd", attention_low, value_rows, preferred_element_type=F32)
    context = context.astype(BF16).reshape(row_count, width)
    first_sum = inputs.astype(F32) + dense(context, o_weight) + o_bias
    middle, norm_one = norm(first_sum, gain_one, shift_one)
    middle = middle.astype(BF16)
    lifted = dense(middle, up_weight) + up_bias
    half = 0.5 * lax.erf(lifted * math.sqrt(0.5)) + 0.5
    activated = (lifted * half).astype(BF16)
    slope = half + lifted * jnp.exp(-0.5 * lifted * lifted) * (1.0 / math.sqrt(2.0 * math.pi))
    slope = slope.astype(BF16)
    second_sum = middle.astype(F32) + dense(activated, down_weight) + down_bias
    output, norm_two = norm(second_sum, gain_two, shift_two)
    saved = (queries, key_rows, value_rows, attention, attention_low, context, norm_one, middle, slope, activated, norm_two)
    return output.astype(BF16), saved


def backward_layer(inputs, weights, vectors, saved, out_grad, send):
    q_weight, k_weight, v_weight, o_weight, up_weight, down_weight = weights
    q_bias, v_bias, o_bias, gain_one, shift_one, up_bias, down_bias, gain_two, shift_two = vectors
    queries, key_rows, value_rows, attention, attention_low, context, norm_one, middle, slope, activated, norm_two = saved
    row_count, width = inputs.shape
    sum_grad, gain_two_grad, shift_two_grad = norm_back(norm_two, gain_two, out_grad)
    lowered_grad = sum_grad.astype(BF16)
    send("down", [outer(activated, lowered_grad)])
    lifted_grad = (back_dense(lowered_grad, down_weight) * slope).astype(BF16)
    send("up", [outer(middle, lifted_grad)])
    middle_grad = sum_grad + back_dense(lifted_grad, up_weight)
    first_grad, gain_one_grad, shift_one_grad = norm_back(norm_one, gain_one, middle_grad)
    attended_grad = first_grad.astype(BF16)
    o_grad = outer(context, attended_grad)
    context_grad = back_dense(attended_grad, o_weight).astype(BF16).reshape(queries.shape)
    attention_grad = jnp.einsum(
        "bqhd,bkhd->bhqk", context_grad, value_rows, preferred_element_type=F32
    )
    value_grad = jnp.einsum(
        "bhqk,bqhd->bkhd", attention_low, context_grad, preferred_element_type=F32
    )
    value_grad = value_grad.astype(BF16).reshape(row_count, width)
    weighed = attention * attention_grad
    score_grad = (weighed - attention * jnp.sum(weighed, axis=-1, keepdims=True)).astype(BF16)
    query_grad = (
        jnp.einsum("bhqk,bkhd->bqhd", score_grad, key_rows, preferred_element_type=F32) * 0.125
    )
    query_grad = query_grad.astype(BF16).reshape(row_count, width)
    key_grad = (
        jnp.einsum("bhqk,bqhd->bkhd", score_grad, queries, preferred_element_type=F32) * 0.125
    )
    key_grad = key_grad.astype(BF16).reshape(row_count, width)
    send("four", [outer(inputs, query_grad), outer(inputs, key_grad), outer(inputs, value_grad), o_grad])
    input_grad = (
        first_grad
        + back_dense(query_grad, q_weight)
        + back_dense(key_grad, k_weight)
        + back_dense(value_grad, v_weight)
    )
    small = (column_sum(query_grad), column_sum(value_grad), column_sum(attended_grad), gain_one_grad, shift_one_grad, column_sum(lifted_grad), column_sum(lowered_grad), gain_two_grad, shift_two_grad)
    return input_grad, small


def plain(weights, small, valid_keys, hidden, cotangent):
    owners = lax.axis_size("dp")
    layers = weights[0].shape[0]
    packed = jnp.concatenate([v.reshape(1, -1) for v in small], axis=1)
    packed = lax.all_gather(packed, "dp", axis=0, tiled=True).astype(F32)
    vectors = []
    offset = 0
    for v in small:
        size = v.shape[0] * v.shape[1]
        part = packed[:, offset : offset + size].reshape((owners,) + v.shape)
        vectors.append(jnp.swapaxes(part, 0, 1).reshape(layers, -1))
        offset += size
    vectors = [tuple(v[layer] for v in vectors) for layer in range(layers)]
    gathered = [
        tuple(lax.all_gather(w[layer], "dp", axis=0, tiled=True) for w in weights)
        for layer in range(layers)
    ]
    current = hidden
    inputs, saved = [], []
    for layer in range(layers):
        inputs.append(current)
        current, kept = forward_layer(current, gathered[layer], vectors[layer], valid_keys)
        saved.append(kept)
    flowing = cotangent.astype(F32)
    big = [{} for _ in range(layers)]
    tiny = [None] * layers
    for layer in reversed(range(layers)):

        def send(name, grads, layer=layer):
            big[layer][name] = [
                lax.psum_scatter(g.astype(BF16).reshape(owners, -1, g.shape[-1]), "dp", scatter_dimension=0, tiled=True)[0].astype(F32)
                for g in grads
            ]

        flowing, tiny[layer] = backward_layer(
            inputs[layer], gathered[layer], vectors[layer], saved[layer], flowing, send
        )
    flat = jnp.concatenate(
        [g.reshape(owners, -1) for layer in range(layers) for g in tiny[layer]], axis=1
    )
    flat = lax.psum_scatter(flat, "dp", scatter_dimension=0, tiled=True).reshape(layers, -1)
    summed = []
    offset = 0
    for v in small:
        summed.append(flat[:, offset : offset + v.shape[1]])
        offset += v.shape[1]
    q_b, v_b, o_b, g_one, s_one, u_b, d_b, g_two, s_two = summed
    fours = [jnp.stack([big[layer]["four"][i] for layer in range(layers)]) for i in range(4)]
    up = jnp.stack([big[layer]["up"][0] for layer in range(layers)])
    down = jnp.stack([big[layer]["down"][0] for layer in range(layers)])
    return (
        current, flowing, *fours,
        q_b, v_b, o_b, g_one, s_one, up, u_b, down, d_b, g_two, s_two,
    )


ITEM = 256
PAD = -1e30


def table_of(owners):
    chips = owners // 2
    depth = chips // 4
    me = lax.axis_index("dp")
    chip, core = me // 2, me % 2
    walk = jnp.arange(chips, dtype=jnp.int32)

    def chip_at(position, core):
        z, first, second = position % depth, position // depth % 2, position // (2 * depth)
        return chip ^ (z * 4 + jnp.where(core == 0, second * 2 + first, first * 2 + second))

    def place_of(other, core):
        z, y, x = (other ^ chip) // 4, (other ^ chip) // 2 % 2, (other ^ chip) % 2
        return z + depth * jnp.where(core == 0, x + 2 * y, y + 2 * x)

    return jnp.concatenate(
        [chip_at(walk, core), chip_at(walk, 1 - core), place_of(walk, core), place_of(walk, 1 - core), core[None]]
    ).astype(jnp.int32)


def flip(value, owners, even, odd):
    return lax.ppermute(value, "dp", [(i, i ^ (odd if i % 2 else even)) for i in range(owners)])


MICROS = 50


def padded_bytes(shape, dtype):
    *lead, rows, columns = (1,) * max(0, 2 - len(shape)) + tuple(shape)
    return math.prod(lead) * (-(-rows // 16) * 16) * (-(-columns // 128) * 128) * jnp.dtype(dtype).itemsize


class Held:
    def __init__(self, room, copy, inward):
        self.room, self.copy, self.inward, self.open = room, copy, inward, True
        self.shape, self.dtype = room.shape, room.dtype
        self.begun = False

    def begin(self):
        if self.inward and not self.begun:
            self.copy.start()
            self.begun = True

    def ready(self):
        if self.inward and self.open:
            self.begin()
            self.copy.wait()
            self.open = False

    def send(self):
        if not self.inward and self.open:
            self.copy.start()
            self.open = False

    def __getitem__(self, at):
        self.ready()
        return self.room[at]

    def __setitem__(self, at, value):
        self.room[at] = value


class Near:
    def __init__(self, room):
        self.room, self.shape, self.dtype = room, room.shape, room.dtype

    def begin(self):
        pass

    def ready(self):
        pass

    def send(self):
        pass

    def __getitem__(self, at):
        return self.room[at]

    def __setitem__(self, at, value):
        self.room[at] = value


HELD = ("feed_back",)


def launch(body, outs, smem=(), vmem=(), hbm=(), deps=(), scratch=(), extra=3, far=pl.ANY, held=False, late=()):
    counts = (len(smem), len(vmem), len(hbm), len(deps), len(outs))
    name = getattr(body, "func", body).__name__
    wrap = held
    held = name in HELD
    sizes = [(v.shape, v.dtype) for v in vmem] + list(outs)
    large = [held and padded_bytes(*v) > 2**16 for v in sizes]
    rooms = [pltpu.VMEM(*v) for v, big in zip(sizes, large) if big]
    own = len(scratch)
    scratch = list(scratch) + rooms + ([pltpu.SemaphoreType.DMA((len(rooms),))] if rooms else [])
    budget = sizes + [(v.shape, v.dtype) for v in scratch[:own] if jnp.issubdtype(v.dtype, jnp.floating)]
    limit = (extra + 10 * wrap) * 2**20 + sum(padded_bytes(shape, dtype) for shape, dtype in budget)

    def kernel(*refs):
        groups, at = [], 0
        for count in counts:
            groups.append(list(refs[at : at + count]))
            at += count
        left = list(refs[at + own :])
        sems = left.pop() if rooms else None
        moved = []
        for group, base, inward in ((groups[1], 0, True), (groups[4], len(vmem), False)):
            for i, ref in enumerate(group):
                if large[base + i]:
                    room, sem = left.pop(0), sems.at[len(moved)]
                    copy = pltpu.make_async_copy(ref, room, sem) if inward else pltpu.make_async_copy(room, ref, sem)
                    group[i] = Held(room, copy, inward)
                    moved.append(group[i])
                    if inward and i not in late:
                        group[i].begin()
                elif wrap:
                    group[i] = Near(ref)
        body(groups[0], groups[1], groups[2], groups[4], refs[at : at + own])
        for one in moved:
            one.ready()
            one.send()
        for one in moved:
            if not one.inward:
                one.copy.wait()

    space = lambda big: pl.BlockSpec(memory_space=pl.ANY if big else pltpu.VMEM)
    in_specs = (
        [pl.BlockSpec(memory_space=pltpu.SMEM)] * len(smem)
        + [space(big) for big in large[: len(vmem)]]
        + [pl.BlockSpec(memory_space=far)] * len(hbm)
        + [pl.BlockSpec(memory_space=pl.ANY)] * len(deps)
    )
    return pl.pallas_call(
        kernel,
        out_shape=[jax.ShapeDtypeStruct(s, d) for s, d in outs],
        in_specs=in_specs,
        out_specs=[space(big) for big in large[len(vmem) :]],
        scratch_shapes=list(scratch),
        name=name,
        compiler_params=pltpu.CompilerParams(vmem_limit_bytes=limit),
        cost_estimate=pl.CostEstimate(
            flops=int(MICROS * 1e9), bytes_accessed=int(MICROS * 3e6), transcendentals=0
        ),
    )(*smem, *vmem, *hbm, *deps)


def mm(left, right):
    return jnp.dot(left, right, preferred_element_type=F32)


def mm_nt(left, right):
    return lax.dot_general(left, right, (((1,), (1,)), ((), ())), preferred_element_type=F32)


def mm_tn(left, right):
    return lax.dot_general(left, right, (((0,), (0,)), ((), ())), preferred_element_type=F32)


def fetch(tab, parts, kind, section, whole, sems, columns=None, step=768):
    near, near_more, far, far_more = parts
    half = near.shape[0]
    rows = whole.shape[-2] // (2 * half)
    core = tab[8 * half]
    first, last = (0, whole.shape[-1]) if columns is None else columns
    if (last - first) % step:
        step = last - first
    count = 0
    sides = []
    for side, group in enumerate(((near, near_more), (far, far_more))):
        hand = core if side == 0 else 1 - core
        steps = []
        for at in [0] if kind == "down" else range(first, last, step):
            copies = []
            for which, part in enumerate(group):
                for b in range(half):
                    start = pl.multiple_of(tab[(2 * side + which) * half + b] * rows, 16)
                    moves = []
                    if kind == "down":
                        wide, deep = part.shape[2] // 4, rows // 4
                        for g in range(4):
                            source = part.at[b, pl.ds(section * deep, deep), pl.ds(g * wide, wide)]
                            to = pl.ds(start + g * deep, deep)
                            if len(whole.shape) == 3:
                                moves.append((source, whole.at[hand, to]))
                            else:
                                at = pl.ds(pl.multiple_of(hand * wide, 128), wide)
                                moves.append((source, whole.at[to, at]))
                    else:
                        wide = 768 if step % 768 == 0 else 384
                        for piece in range(at, at + step, wide):
                            source = part.at[b, pl.ds(section * rows, rows), pl.ds(piece, wide)]
                            target = whole.at[hand, pl.ds(start, rows), pl.ds(piece - first, wide)]
                            moves.append((source, target))
                    for source, target in moves:
                        copies.append(pltpu.make_async_copy(source, target, sems.at[count]))
                        copies[-1].start()
                        count += 1
            steps.append(copies)
        sides.append(steps)
    return sides


def finish_all(sides):
    for steps in sides:
        for copies in steps:
            finish(copies)


def finish(copies):
    for copy in copies:
        copy.wait()


def norm_rows(values):
    center = values - jnp.mean(values, axis=-1, keepdims=True)
    scale = lax.rsqrt(jnp.mean(center * center, axis=-1, keepdims=True) + epsilon)
    return center * scale, scale


def norm_rows_back(unit, scale, inner):
    return scale * (
        inner
        - jnp.mean(inner, axis=-1, keepdims=True)
        - unit * jnp.mean(inner * unit, axis=-1, keepdims=True)
    )


def gelu_and_slope(v):
    phi = 0.5 + 0.5 * lax.erf(v * math.sqrt(0.5))
    return v * phi, phi + v * jnp.exp(-0.5 * v * v) * (1.0 / math.sqrt(2.0 * math.pi))


def put_rows_apart(source, room, seq):
    count = source.shape[0]
    room[count:, :] = jnp.zeros((room.shape[0] - count, room.shape[1]), F32)
    room[0:count, :] = source[...].astype(F32)
    row = lax.broadcasted_iota(jnp.int32, (ITEM, room.shape[1]), 0)
    return [
        jnp.where(row < seq, room[i * seq : i * seq + ITEM, :], 0.0) for i in range(count // seq)
    ]


def put_rows_together(values, out, seq):
    for i in range(values.shape[0] // ITEM):
        out[i * seq : (i + 1) * seq, :] = values[i * ITEM : i * ITEM + seq]


Q_B, V_B, O_B, G_ONE, S_ONE, D_B, G_TWO, S_TWO, UP_B = range(9)


def split_own(smem, vmem, hbm, outs, scratch):
    (tab,) = smem
    core = tab[tab.shape[0] - 1]
    copies = [pltpu.make_async_copy(w, room, scratch[-1].at[i]) for i, (w, room) in enumerate(zip(hbm, scratch))]
    for copy in copies:
        copy.start()
    finish(copies)
    table = scratch[-2]
    vmem = scratch[6 : len(hbm)]
    table[...] = jnp.zeros_like(table)
    short = [v for v in vmem if v.shape[1] == vmem[0].shape[1]]
    (long,) = [v for v in vmem if v.shape[1] != vmem[0].shape[1]]
    layers = long.shape[0]
    for layer in range(layers):
        for i, v in enumerate(short):
            at = layer * len(short) + i
            table[at : at + 1, 0 : v.shape[1]] = v[layer : layer + 1, :].astype(F32)
        at = layers * len(short) + layer
        table[at : at + 1, 0 : long.shape[1]] = long[layer : layer + 1, :].astype(F32)
    q, k, v, o, up, down = scratch[:6]
    for layer in range(layers):
        for place, hand in ((0, core), (1, 1 - core)):
            four, wide, tall = outs[6 * layer + 3 * place : 6 * layer + 3 * place + 3]
            part = q.shape[2] // 2
            at = pl.ds(pl.multiple_of(hand * part, 128), part)
            for i, w in enumerate((q, k, v, o)):
                four[:, i * part : (i + 1) * part] = w[layer, :, at]
            if four.shape[1] > 4 * part:
                four[:, 4 * part :] = table[...].astype(BF16)
            part = up.shape[2] // 2
            wide[...] = up[layer, :, pl.ds(pl.multiple_of(hand * part, 128), part)]
            part = down.shape[2] // 2
            tall[...] = down[layer, :, pl.ds(pl.multiple_of(hand * part, 128), part)]


def join_rows(smem, vmem, hbm, outs, scratch, kinds):
    (tab,) = smem
    first = tab[tab.shape[0] - 1] == 0
    (out,) = outs
    rows = out.shape[0] // len(kinds)
    for i, kind in enumerate(kinds):
        mine, came = vmem[2 * i][...].astype(F32), vmem[2 * i + 1][...].astype(F32)
        upper, lower = jnp.where(first, mine, came), jnp.where(first, came, mine)
        at = slice(i * rows, (i + 1) * rows)
        if kind != "down":
            out[at, :] = jnp.concatenate([upper, lower], axis=0).astype(BF16)
            continue
        wide = upper.shape[1]
        for g in range(4):
            part = (upper, lower)[g // 2][g % 2 * rows : (g % 2 + 1) * rows]
            out[at, g * wide : (g + 1) * wide] = part.astype(BF16)


def place_vectors(smem, vmem, hbm, outs, scratch):
    (tab,) = smem
    room, sems = scratch
    half, rows, side = room.shape[0] // 2, room.shape[1], room.shape[2]
    copies = []
    for i, part in enumerate(hbm):
        source = part.at[:, :, pl.ds(part.shape[2] - side, side)]
        copies.append(pltpu.make_async_copy(source, room.at[pl.ds(i * half, half)], sems.at[i]))
        copies[-1].start()
    finish(copies)
    width = outs[0].shape[1]
    own = rows // 2
    devices = 4 * half
    count = width // devices
    wide = outs[0].shape[0] - 8
    short = jnp.zeros((16, width), F32)
    long = [jnp.zeros((8, width), F32) for _ in range(wide)]
    for b in range(2 * half):
        block = room[b].astype(F32)
        for k in (0, 1):
            device = 2 * tab[b] + k
            part = block[k * own : (k + 1) * own]
            part = jnp.concatenate([part, jnp.zeros((own, width - side), F32)], axis=1)
            short = short + pltpu.roll(part[:16], device * count, 1)
            start = device * count * wide
            moved = pltpu.roll(part[16:24], start % width, 1)
            for i in range(wide):
                long[i] = long[i] + jnp.where(start // width == i, moved, 0.0)
    for layer, out in enumerate(outs):
        out[0:8, :] = short[8 * layer : 8 * layer + 8]
        for i in range(wide):
            out[8 + i : 9 + i, :] = long[i][layer : layer + 1]


def join_blocks(smem, vmem, hbm, outs, scratch, rows_at=0):
    (out,) = outs
    (sems,) = scratch
    at = 0
    copies = []
    for part in hbm:
        if len(part.shape) == 3:
            source, target = part, out.at[pl.ds(at, part.shape[0])]
            at += part.shape[0]
        else:
            source, target = part.at[pl.ds(rows_at, out.shape[1])], out.at[at]
            at += 1
        copies.append(pltpu.make_async_copy(source, target, sems.at[len(copies)]))
        copies[-1].start()
    finish(copies)


def attend_forward(smem, vmem, hbm, outs, scratch, sections, seq):
    (tab,) = smem
    x, vec, mask = vmem
    q, k, v, p, context, unit, scale, middle = outs[:8]
    whole, o_whole = outs[8].room, outs[9].room
    sems, o_sems = scratch[:2]
    half = x.shape[1] // 2
    sides = fetch(tab, hbm, "four", sections[0], whole, sems, columns=(0, 3 * half), step=3 * half)
    late = fetch(tab, hbm, "four", sections[0], o_whole, o_sems, columns=(3 * half, 4 * half))
    if len(outs) > 10:
        for i, item in enumerate(put_rows_apart(x, scratch[2], seq)):
            outs[10][i * ITEM : (i + 1) * ITEM, :] = item.astype(BF16)
        x = outs[10]
        x.send()
    core = tab[tab.shape[0] - 1]
    for steps, h in zip(sides, (core, 1 - core)):
        finish(steps[0])
        at = pl.ds(pl.multiple_of(h * half, 128), half)
        made = mm(x[...], whole[h])
        if h is not core:
            outs[8].send()
        q[:, at] = (made[:, 0:half] + vec[Q_B : Q_B + 1, at]).astype(BF16)
        k[:, at] = made[:, half : 2 * half].astype(BF16)
        v[:, at] = (made[:, 2 * half :] + vec[V_B : V_B + 1, at]).astype(BF16)
    low = lax.broadcasted_iota(jnp.int32, (ITEM, 2 * HEAD_DIM), 1) < HEAD_DIM
    items = x.shape[0] // ITEM

    for i in range(HEADS // 2):
        at = slice(i * 2 * HEAD_DIM, (i + 1) * 2 * HEAD_DIM)
        for item in range(items):
            rows = slice(item * ITEM, (item + 1) * ITEM)
            qs, ks, vs = q[rows, at], k[rows, at], v[rows, at]
            made = []
            for side in (0, 1):
                own = low if side == 0 else jnp.logical_not(low)
                s = mm_nt(jnp.where(own, qs, jnp.zeros_like(qs)), ks) * 0.125 + mask[item]
                e = jnp.exp(s - jnp.max(s, axis=-1, keepdims=True))
                w = (e * (1.0 / jnp.sum(e, axis=-1, keepdims=True))).astype(BF16)
                p[item * HEADS + 2 * i + side] = w
                made.append(mm(w, vs))
            context[rows, at] = jnp.where(low, made[0], made[1]).astype(BF16)
    finish_all(late)
    for out in (q, k, v, p, context, outs[9]):
        out.send()
    attended = jnp.concatenate([mm(context[...], o_whole[h]) for h in (0, 1)], axis=1)
    first = x[...].astype(F32) + (attended + vec[O_B : O_B + 1, :])
    made, made_scale = norm_rows(first)
    unit[...] = made
    scale[...] = made_scale
    middle[...] = (made * vec[G_ONE : G_ONE + 1, :] + vec[S_ONE : S_ONE + 1, :]).astype(BF16)


def lift(smem, vmem, hbm, outs, scratch, sections):
    (tab,) = smem
    middle, vec = vmem
    activated, slope, kept = outs
    whole = kept.room
    (sems,) = scratch
    width = vec.shape[1]
    sides = fetch(tab, hbm, "up", sections[0], whole, sems, step=width)
    core = tab[tab.shape[0] - 1]
    step = width // 3
    for steps, h in zip(sides, (core, 1 - core)):
        for i, copies in enumerate(steps):
            finish(copies)
            for j in range(3):
                at = slice(i * width + j * step, i * width + (j + 1) * step)
                bias = vec[pl.ds(UP_B + h * len(steps) + i, 1), j * step : (j + 1) * step]
                a, s = gelu_and_slope(mm(middle[...], whole[h, :, at]) + bias)
                activated[h, :, at] = a.astype(BF16)
                slope[h, :, at] = s.astype(BF16)
    kept.send()


def lower(smem, vmem, hbm, outs, scratch, sections, seq):
    (tab,) = smem
    activated, middle, vec = vmem
    output, unit, scale, kept = outs
    whole = kept.room
    finish_all(fetch(tab, hbm, "down", sections[0], whole, scratch[0]))
    kept.send()
    deep = activated.shape[2]
    lowered = mm(activated[0], whole[0:deep, :]) + mm(activated[1], whole[deep:, :])
    second = middle[...].astype(F32) + (lowered + vec[D_B : D_B + 1, :])
    made, made_scale = norm_rows(second)
    unit[...] = made
    scale[...] = made_scale
    made = made * vec[G_TWO : G_TWO + 1, :] + vec[S_TWO : S_TWO + 1, :]
    if len(scratch) > 1:
        put_rows_together(made, scratch[1], seq)
        output[...] = scratch[1][...].astype(BF16)
    else:
        output[...] = made.astype(BF16)


def rows_sum(values):
    return jnp.sum(values, axis=0, keepdims=True)


SUM_G_TWO, SUM_S_TWO, SUM_D_B, SUM_UP_B = 0, 1, 2, 8
SUM_G_ONE, SUM_S_ONE, SUM_O_B = 0, 1, 2


def feed_back(smem, vmem, hbm, outs, scratch, seq):
    (tab,) = smem
    grad, unit_two, scale_two, vec, activated, down_whole, slope, middle = vmem
    sum_grad, lifted_grad, down_send, down_keep, up_send, up_keep, sums = outs
    turned, low_grad = scratch[:2]
    chips, rows, part = up_send.shape
    core = tab[4 * chips]
    if len(scratch) > 2:
        g = jnp.concatenate(put_rows_apart(grad, scratch[2], seq), axis=0)
    else:
        g = grad[...]
    u = unit_two[...]
    made = norm_rows_back(u, scale_two[...], g * vec[G_TWO : G_TWO + 1, :])
    sum_grad[...] = made
    sum_grad.send()
    low = made.astype(BF16)
    half = low.shape[1] // 2
    low_grad[0] = low[:, :half]
    low_grad[1] = low[:, half:]
    sums[...] = jnp.zeros_like(sums)
    sums[SUM_G_TWO : SUM_G_TWO + 1, :] = rows_sum(g * u)
    sums[SUM_S_TWO : SUM_S_TWO + 1, :] = rows_sum(g)
    sums[SUM_D_B : SUM_D_B + 1, :] = rows_sum(low.astype(F32))
    activated.ready()
    for one in (down_whole, slope, middle):
        one.begin()
    deep = activated.shape[2]
    wide = part // 4
    for out, hand, places in ((down_send, 1 - core, 3), (down_keep, core, 2)):
        right = low_grad[hand]
        for h in (0, 1):
            for j in range(deep // (8 * rows)):
                made = mm_tn(activated[h, :, 8 * rows * j : 8 * rows * (j + 1)], right).astype(BF16)
                for i in (0, 1):
                    chip = h * deep // (4 * rows) + 2 * j + i
                    to = tab[places * chips + chip]
                    for g in range(4):
                        at = (4 * i + g) * rows
                        out[to, :, g * wide : (g + 1) * wide] = made[at : at + rows]
    for out in (down_send, down_keep):
        out.send()
    turned[...] = middle[...].T
    down_whole.ready()
    slope.ready()
    width = sums.shape[1]
    step = width
    for h in (0, 1):
        for j in range(part // step):
            at = slice(j * step, (j + 1) * step)
            rows_at = slice(h * part + j * step, h * part + (j + 1) * step)
            made = mm_nt(low, down_whole[rows_at, :])
            made = (made * slope[h, :, at].astype(F32)).astype(BF16)
            lifted_grad[h, :, at] = made
            column = h * part + j * step
            to = SUM_UP_B + column // width
            sums[to : to + 1, column % width : column % width + step] = rows_sum(made.astype(F32))
    lifted_grad.send()
    for out, hand, places in ((up_send, 1 - core, 3), (up_keep, core, 2)):
        for j in range(part // step):
            at = slice(j * step, (j + 1) * step)
            made = mm(turned[...], lifted_grad[hand, :, at]).astype(BF16)
            for chip in range(chips):
                out[tab[places * chips + chip], :, at] = made[chip * rows : (chip + 1) * rows]
        out.send()


def first_norm_back(smem, vmem, hbm, outs, scratch):
    lifted_grad, up_whole, sum_grad, unit_one, scale_one, vec = vmem
    first_grad, attended_grad, sums = outs
    sums[...] = jnp.zeros_like(sums)
    g = sum_grad[...] + mm_nt(lifted_grad[0], up_whole[0]) + mm_nt(lifted_grad[1], up_whole[1])
    u = unit_one[...]
    made = norm_rows_back(u, scale_one[...], g * vec[G_ONE : G_ONE + 1, :])
    first_grad[...] = made
    low = made.astype(BF16)
    half = low.shape[1] // 2
    attended_grad[0] = low[:, :half]
    attended_grad[1] = low[:, half:]
    sums[SUM_G_ONE : SUM_G_ONE + 1, :] = rows_sum(g * u)
    sums[SUM_S_ONE : SUM_S_ONE + 1, :] = rows_sum(g)
    sums[SUM_O_B : SUM_O_B + 1, :] = rows_sum(low.astype(F32))


def attend_back(smem, vmem, hbm, outs, scratch):
    (tab,) = smem
    attended_grad, o_whole, q, k, v, p, x, context = vmem[:8]
    send, keep, sums, grads = outs
    x_turned, c_turned, context_grad = scratch[:3]
    chips, rows, _ = send.shape
    half = x.shape[1] // 2
    core = tab[4 * chips]
    x_turned[...] = x[...].T
    c_turned[...] = context[...].T
    made = mm_nt(attended_grad[0], o_whole[0]) + mm_nt(attended_grad[1], o_whole[1])
    context_grad[...] = made.astype(BF16)
    items = q.shape[0] // ITEM
    low = lax.broadcasted_iota(jnp.int32, (ITEM, 2 * HEAD_DIM), 1) < HEAD_DIM
    pairs = HEADS // 4
    sides = (low, jnp.logical_not(low))
    apart = lambda values: [jnp.where(own, values, jnp.zeros_like(values)) for own in sides]
    for h in (0, 1):
        grads[h, :, 3 * half :] = attended_grad[h]
        for i in range(pairs):
            at = slice(h * half + i * 2 * HEAD_DIM, h * half + (i + 1) * 2 * HEAD_DIM)
            for item in range(items):
                rows_at = slice(item * ITEM, (item + 1) * ITEM)
                qs, ks, vs, cs = q[rows_at, at], k[rows_at, at], v[rows_at, at], context_grad[rows_at, at]
                ws = [p[item * HEADS + 2 * (h * pairs + i) + side] for side in (0, 1)]
                ds = []
                for w, c in zip(ws, apart(cs)):
                    wide = w.astype(F32)
                    g = wide * mm_nt(c, vs)
                    ds.append((g - wide * jnp.sum(g, axis=-1, keepdims=True)).astype(BF16))
                stacked = lambda values: jnp.concatenate(apart(values), axis=0)
                made = (
                    mm(jnp.concatenate(ds, axis=1), stacked(ks)) * 0.125,
                    mm_tn(jnp.concatenate(ds, axis=0), stacked(qs)) * 0.125,
                    mm_tn(jnp.concatenate(ws, axis=0), stacked(cs)),
                )
                for place, both in enumerate(made):
                    start = place * half + i * 2 * HEAD_DIM
                    grads[h, rows_at, start : start + 2 * HEAD_DIM] = both.astype(BF16)
    grads.send()
    for out, hand, places in ((send, 1 - core, 3), (keep, core, 2)):
        for j in range(4):
            at = slice(j * half, (j + 1) * half)
            made = mm((c_turned if j == 3 else x_turned)[...], grads[hand, :, at]).astype(BF16)
            for chip in range(chips):
                out[tab[places * chips + chip], :, at] = made[chip * rows : (chip + 1) * rows]
        if len(vmem) == 8:
            out.send()
    sums[...] = jnp.zeros_like(sums)
    for h in (0, 1):
        at = slice(h * half, (h + 1) * half)
        sums[0:1, at] = rows_sum(grads[h, :, 0:half].astype(F32))
        sums[1:2, at] = rows_sum(grads[h, :, 2 * half : 3 * half].astype(F32))
    if len(vmem) == 8:
        return
    short, long = scratch[3:5]
    wide = long.shape[0] // 2
    for layer, (feed, other, four) in enumerate((vmem[8:10] + [sums], vmem[10:13])):
        at = layer * 8
        short[at : at + 2, :] = four[0:2, :]
        short[at + 2 : at + 3, :] = other[SUM_O_B : SUM_O_B + 1, :]
        short[at + 3 : at + 5, :] = other[SUM_G_ONE : SUM_G_ONE + 2, :]
        short[at + 5 : at + 6, :] = feed[SUM_D_B : SUM_D_B + 1, :]
        short[at + 6 : at + 8, :] = feed[SUM_G_TWO : SUM_G_TWO + 2, :]
        long[layer * wide : (layer + 1) * wide, :] = feed[SUM_UP_B : SUM_UP_B + wide, :]
    width = x.shape[1]
    side = send.shape[2] - 4 * half
    count = width // (2 * chips)
    lanes = lax.broadcasted_iota(jnp.int32, (16, side), 1)
    last = lax.broadcasted_iota(jnp.int32, (8, side), 0)
    for chip in range(chips):
        shares = []
        for device in (2 * chip, 2 * chip + 1):
            part = pltpu.roll(short[...], (width - device * count) % width, 1)[:, :side]
            shares.append(jnp.where(lanes < count, part, 0.0))
            start = device * count * wide
            turn = (width - start % width) % width
            part = pltpu.roll(long[...], turn, 1)[:, :side]
            first, second = start // width, wide + start // width
            part = jnp.where(last == 0, part[first : first + 1], jnp.where(last == 1, part[second : second + 1], 0.0))
            shares.append(jnp.where(lanes[:8] < count * wide, part, 0.0))
        block = jnp.concatenate(shares, axis=0).astype(BF16)
        for out, places in ((send, 3), (keep, 2)):
            out[tab[places * chips + chip], :, 4 * half :] = block


def attend_back_last(smem, vmem, hbm, outs, scratch, seq):
    first_grad, grads, whole = vmem
    (out,) = outs
    deep = whole.shape[2]
    made = first_grad[...] + mm_nt(grads[0, :, :deep], whole[0]) + mm_nt(grads[1, :, :deep], whole[1])
    if out.shape[0] == made.shape[0]:
        out[...] = made
    else:
        put_rows_together(made, out, seq)


def add_halves(smem, vmem, hbm, outs, scratch):
    send, kept = outs
    half = send.shape[0]
    rows = send.shape[1] // (len(vmem) // 2)

    def block(b, carry):
        for i in range(len(vmem) // 2):
            keep, came = vmem[2 * i], vmem[2 * i + 1]
            at = slice(i * rows, (i + 1) * rows)
            kept[b, at] = (keep[b].astype(F32) + came[b].astype(F32)).astype(BF16)
            send[b, at] = (keep[half + b].astype(F32) + came[half + b].astype(F32)).astype(BF16)
        return carry

    lax.fori_loop(0, half, block, 0)


def add_spread(smem, vmem, hbm, outs, scratch):
    at = 0
    for keep, came in zip(vmem[0::2], vmem[1::2]):
        rows = keep.shape[1]
        for b, out in enumerate(outs):
            out[at : at + rows] = (keep[b].astype(F32) + came[b].astype(F32)).astype(out.dtype)
        at += rows


def add_last(smem, vmem, hbm, outs, scratch, kinds=()):
    (tab,) = smem
    core = tab[tab.shape[0] - 1]
    (total,) = scratch
    made = vmem[0][...].astype(F32)
    for came in vmem[1:]:
        made = made + came[...].astype(F32)
    total[...] = made
    rows = total.shape[0] // len(kinds)
    half = rows // 2
    for i, kind in enumerate(kinds):
        to = slice(i * half, (i + 1) * half)
        for out, hand in zip(outs, (core, 1 - core)):
            if kind == "down":
                wide = total.shape[1] // 2
                at = pl.ds(pl.multiple_of(hand * wide, 128), wide)
                for g in (0, 1):
                    part = total[i * rows + g * half : i * rows + (g + 1) * half, at]
                    out[to, g * wide : (g + 1) * wide] = part
            else:
                out[to, :] = total[pl.ds(pl.multiple_of(i * rows + hand * half, 8), half), :]


def write_out(smem, vmem, hbm, outs, scratch, kind, sections):
    (tab,) = smem
    core = tab[tab.shape[0] - 1]
    half = outs[0].shape[2] // 2
    for layer, section in enumerate(sections):
        for hand, part in ((core, vmem[2 * layer]), (1 - core, vmem[2 * layer + 1])):
            at = pl.ds(pl.multiple_of(hand * half, 128), half)
            if kind == "down":
                rows = outs[0].shape[1] // 4
                for g in range(4):
                    start = (g % 2 * 2 + g // 2) * half
                    to = slice(g * rows, (g + 1) * rows)
                    outs[0][layer, to, at] = part[section * rows : (section + 1) * rows, start : start + half]
                continue
            rows = outs[0].shape[1]
            for i, out in enumerate(outs[:4] if kind == "four" else outs):
                out[layer, :, at] = part[section * rows : (section + 1) * rows, i * half : (i + 1) * half]
    if kind != "four":
        return
    part = vmem[0]
    start = 4 * half
    for i, out in enumerate(outs[4:]):
        count = out.shape[1]
        for layer in range(out.shape[0]):
            at = 16 + layer if i == 8 else 8 * layer + i
            out[layer : layer + 1, :] = part[at : at + 1, start : start + count]


class Chain:
    def __init__(self):
        self.token = None

    def __call__(self, body, outs, after=(), **kinds):
        deps = list(after) + ([] if self.token is None else [self.token])
        made = launch(body, outs, deps=deps, **kinds)
        self.token = min(made, key=lambda m: m.size)
        return made


def blocks(weights, small, mask, hidden, cotangent, seq):
    q_weight, k_weight, v_weight, o_weight, up_weight, down_weight = weights
    owners = lax.axis_size("dp")
    chips = owners // 2
    depth = chips // 4
    layers, rows, width = q_weight.shape
    wide = up_weight.shape[2]
    tall = hidden.shape[0] // seq * ITEM
    tab = table_of(owners)
    chain = Chain()
    dma = lambda n: pltpu.SemaphoreType.DMA((n,))
    vmem = lambda shape, dtype: pltpu.VMEM(shape, dtype)
    xy_one = lambda v: flip(v, owners, 2, 4)
    xy_two = lambda v: flip(v, owners, 4, 2)
    core_flip = lambda v: flip(v, owners, 1, 1)
    z_flip = lambda v, k: flip(v, owners, 8 * k, 8 * k)
    order = [v for v in small if v.shape[1] == rows] + [v for v in small if v.shape[1] != rows]

    side = 128
    block = (2 * rows, 2 * width)
    kinds = ("four", "up", "down")
    groups = [[(layer, kind)] for layer in range(layers) for kind in kinds]
    shapes = [(len(g) * block[0], block[1] + (side if i == 0 else 0)) for i, g in enumerate(groups)]
    halves = lambda layer: [((rows, 2 * width + (0 if layer else side)), BF16), ((rows, wide // 2), BF16), ((down_weight.shape[1], width // 2), BF16)]
    split = chain(
        split_own, [h for layer in range(layers) for h in halves(layer) * 2], smem=[tab], hbm=list(weights) + order, far=pltpu.HBM,
        scratch=[vmem(w.shape, BF16) for w in list(weights) + order] + [vmem((rows, side), F32), dma(6 + len(order))], extra=57,
    )
    mine = {(layer, kind): split[6 * layer + i] for layer in range(layers) for i, kind in enumerate(kinds)}
    other = {(layer, kind): core_flip(split[6 * layer + 3 + i]) for layer in range(layers) for i, kind in enumerate(kinds)}
    own, z_came, x_one, x_two, stacked, near, far = ({} for _ in range(7))

    direct = 2
    rest = [piece for group in groups[direct:] for piece in group]
    row_of = {piece: i * block[0] for i, piece in enumerate(rest)}

    def join(pieces, shape):
        (made,) = chain(
            functools.partial(join_rows, kinds=tuple(kind for _, kind in pieces)), [(shape, BF16)], smem=[tab],
            vmem=[v for piece in pieces for v in (mine[piece], other[piece])],
        )
        return made

    def begin():
        for g in range(direct):
            own[g] = join(groups[g], shapes[g])
            z_came[g] = [z_flip(own[g], k) for k in range(1, depth)]
        own["rest"] = join(rest, (len(rest) * block[0], block[1]))
        z_came["rest"] = z_flip(own["rest"], 1)

    def stack(sources, count, shape, rows_at=0, after=()):
        (made,) = chain(functools.partial(join_blocks, rows_at=rows_at), [((count,) + shape, BF16)], hbm=sources, scratch=[dma(count)], after=after)
        return made

    def far_round(g):
        stacked[g] = stack([own["rest"], z_came["rest"]], 2, shapes[g], row_of[groups[g][0]])
        z_came[g, 2] = z_flip(stacked[g], 2)

    def first_stack(g, after=()):
        sources = [own[g]] + z_came[g] if g < direct else [stacked[g], z_came[g, 2]]
        stacked[g] = stack(sources, depth, shapes[g], after=after)
        x_one[g] = xy_one(stacked[g])

    def second_stack(g, after=()):
        made = stack([stacked[g], x_one[g]], 2 * depth, shapes[g], after=after)
        x_two[g] = xy_two(made)
        near[g] = [made, x_two[g]]
        far[g] = [core_flip(made)]

    def third(g):
        value = lax.optimization_barrier((x_two[g], chain.token))[0]
        x_two[g] = value
        near[g][1] = value
        far[g].append(core_flip(value))

    def parts(layer, kind):
        (g,) = [i for i, group in enumerate(groups) if (layer, kind) in group]
        return near[g] + far[g]

    def section(layer, kind):
        return [group.index((layer, kind)) for group in groups if (layer, kind) in group][0]

    height = {"four": width, "up": width, "down": wide}
    across = {"four": 2 * width, "up": wide // 2, "down": width // 2}
    whole = lambda kind, columns=None: [vmem((2, height[kind], columns or across[kind]), BF16), dma(8 * chips)]
    xs, kept = [hidden], [{} for _ in range(layers)]
    row = lambda dtype: ((tall, width), dtype)
    column = ((tall, 1), F32)
    deep = ((2, tall, wide // 2), BF16)
    items = tall // ITEM

    def forward_attend(layer):
        s = kept[layer]
        raw = xs[layer].shape[0] != tall
        made = chain(
            functools.partial(attend_forward, sections=[section(layer, "four")], seq=seq),
            [row(BF16)] * 3 + [((items * HEADS, ITEM, ITEM), BF16), row(BF16), row(F32), column, row(BF16)]
            + [((2, width, width * 3 // 2), BF16), ((2, width, width // 2), BF16)] + [row(BF16)] * raw,
            held=True, smem=[tab], vmem=[xs[layer], vec[layer], mask], hbm=parts(layer, "four"),
            scratch=[dma(8 * chips)] * 2 + [vmem((tall, width), F32)] * raw,
        )
        s["q"], s["k"], s["v"], s["p"], s["context"], s["unit_one"], s["scale_one"], s["middle"] = made[:8]
        s["three"], s["o"] = made[8:10]
        if raw:
            xs[layer] = made[10]

    def forward_lift(layer):
        s = kept[layer]
        s["activated"], s["slope"], s["up"] = chain(
            functools.partial(lift, sections=[section(layer, "up")]), [deep, deep, ((2, width, wide // 2), BF16)],
            held=True, smem=[tab], vmem=[s["middle"], vec[layer]], hbm=parts(layer, "up"), scratch=[dma(8 * chips)],
        )

    def forward_lower(layer):
        s = kept[layer]
        last_one = layer == layers - 1
        shape = hidden.shape if last_one else (tall, width)
        output, s["unit_two"], s["scale_two"], s["down"] = chain(
            functools.partial(lower, sections=[section(layer, "down")], seq=seq),
            [(shape, BF16), row(F32), column, ((wide, width), BF16)],
            held=True, smem=[tab], vmem=[s["activated"], s["middle"], vec[layer]], hbm=parts(layer, "down"),
            scratch=[dma(8 * chips)] + [vmem(shape, F32)] * last_one,
        )
        xs.append(output)

    begin()
    first_stack(0)
    second_stack(0)
    first_stack(1)
    far_round(2)
    third(0)
    vec = chain(
        place_vectors, [((8 + wide // width, width), F32)] * layers, smem=[tab], hbm=near[0],
        scratch=[vmem((chips, block[0], side), BF16), dma(2)],
    )
    second_stack(1)
    first_stack(2)
    far_round(3)
    forward_attend(0)
    third(1)
    second_stack(2)
    first_stack(3)
    far_round(4)
    forward_lift(0)
    third(2)
    second_stack(3)
    first_stack(4)
    far_round(5)
    forward_lower(0)
    first_stack(5)
    third(3)
    second_stack(4)
    forward_attend(1)
    third(4)
    second_stack(5)
    forward_lift(1)
    third(5)
    forward_lower(1)

    keep, came, fanned, last = {}, {}, {}, {}
    sums = [{} for _ in range(layers)]
    flowing = [None] * (layers + 1)
    flowing[layers] = cotangent
    pair = lambda extra=0: [((chips, block[0], block[1] + extra), BF16)] * 2

    def leave(piece, send, kept_blocks):
        keep[piece] = kept_blocks
        came[piece] = core_flip(send)

    def back_feed(layer):
        s = kept[layer]
        raw = flowing[layer + 1].shape[0] != tall
        s["sum_grad"], s["lifted_grad"], d_send, d_keep, u_send, u_keep, sums[layer]["feed"] = chain(
            functools.partial(feed_back, seq=seq), [row(F32), deep] + pair() * 2 + [((16, width), F32)], held=True,
            smem=[tab],
            vmem=[flowing[layer + 1], s["unit_two"], s["scale_two"], vec[layer], s["activated"], s["down"], s["slope"],
                  s["middle"]],
            late=(5, 6, 7),
            scratch=[vmem((width, tall), BF16), vmem((2, tall, width // 2), BF16)] + [vmem((tall, width), F32)] * raw,
        )
        leave((layer, "down"), d_send, d_keep)
        leave((layer, "up"), u_send, u_keep)

    def back_norm(layer):
        s = kept[layer]
        s["first_grad"], s["attended_grad"], sums[layer]["norm"] = chain(
            first_norm_back, [row(F32), ((2, tall, width // 2), BF16), ((8, width), F32)], held=True,
            vmem=[s["lifted_grad"], s["up"], s["sum_grad"], s["unit_one"], s["scale_one"], vec[layer]],
        )

    def back_attend(layer):
        s = kept[layer]
        more, room = [], []
        if layer == 0:
            more = [sums[0]["feed"], sums[0]["norm"], sums[1]["feed"], sums[1]["norm"], sums[1]["four"]]
            room = [vmem((16, width), F32), vmem((2 * wide // width, width), F32)]
        send, rest, sums[layer]["four"], s["grads"] = chain(
            attend_back, pair(0 if layer else side) + [((8, width), F32), ((2, tall, 2 * width), BF16)], held=True,
            smem=[tab],
            vmem=[s["attended_grad"], s["o"], s["q"], s["k"], s["v"], s["p"], xs[layer], s["context"]] + more,
            scratch=[vmem((width, tall), BF16)] * 2 + [vmem((tall, width), BF16)] + room,
        )
        leave((layer, "four"), send, rest)

    def back_last(layer):
        s = kept[layer]
        shape = (tall, width) if layer else hidden.shape
        (flowing[layer],) = chain(
            functools.partial(attend_back_last, seq=seq), [(shape, F32)], held=True,
            vmem=[s["first_grad"], s["grads"], s["three"]],
        )

    def fold(*pieces, after=()):
        half = keep[pieces[0]].shape[0] // 2
        r, c = keep[pieces[0]].shape[1:]
        at = pieces if len(pieces) > 1 else pieces[0]
        send, keep[at] = chain(add_halves, [((half, r * len(pieces), c), BF16)] * 2, vmem=[v for piece in pieces for v in (keep[piece], came[piece])], after=after)
        came[at] = xy_two(send) if half == 2 * depth else xy_one(send)

    def fan(*ats, after=()):
        at = ats[0] if len(ats) == 1 else sum((a if isinstance(a[0], tuple) else (a,) for a in ats), ())
        shape = (sum(keep[a].shape[1] for a in ats), keep[ats[0]].shape[2])
        made = chain(add_spread, [(shape, F32)] + [(shape, BF16)] * (depth - 1), vmem=[v for a in ats for v in (keep[a], came[a])], after=after)
        keep[at] = made[0]
        fanned[at] = [z_flip(made[k], k) for k in range(1, depth)]

    def total(at, after=()):
        pieces = at if isinstance(at[0], tuple) else (at,)
        shape = keep[at].shape
        made = chain(
            functools.partial(add_last, kinds=tuple(kind for _, kind in pieces)), [((shape[0] // 2, shape[1]), F32)] * 2,
            smem=[tab], vmem=[keep[at]] + fanned[at], scratch=[vmem(shape, F32)], after=after,
        )
        both = [made[0], core_flip(made[1])]
        for i, piece in enumerate(pieces):
            last[piece] = (both, i)
        return both[1:]

    def finished(kind, count):
        own_rows = down_weight.shape[1] if kind == "down" else rows
        columns = wide if kind == "up" else width
        outs = [((layers, own_rows, columns), F32)] * count
        if kind == "four":
            outs += [(v.shape, F32) for v in order]
        return chain(
            functools.partial(write_out, kind=kind, sections=[last[layer, kind][1] for layer in range(layers)]), outs,
            smem=[tab], vmem=[v for layer in range(layers) for v in last[layer, kind][0]],
        )

    d1, u1, f1, d0, u0, f0 = [(layer, kind) for layer in (1, 0) for kind in ("down", "up", "four")]
    back_feed(1)
    back_norm(1)
    fold(d1, u1)
    back_attend(1)
    back_last(1)
    fold(f1)
    back_feed(0)
    fold((d1, u1))
    fold(f1)
    back_norm(0)
    fold(d0, u0)
    back_attend(0)
    fan((d1, u1), f1)
    fold(f0)
    back_last(0)
    fold((d0, u0))
    done = total((d1, u1, f1))
    fan((d0, u0))
    fold(f0, after=done)
    total((d0, u0))
    fan(f0)
    (down_grad,) = finished("down", 1)
    (up_grad,) = finished("up", 1)
    total(f0)
    grads = finished("four", 4)
    q_b, v_b, o_b, g_one, s_one, d_b, g_two, s_two, u_b = grads[4:]
    return (
        xs[-1], flowing[0], *grads[:4],
        q_b, v_b, o_b, g_one, s_one, up_grad, u_b, down_grad, d_b, g_two, s_two,
    )


def shards(
    hidden, region_count, text_mask,
    q_weight, k_weight, v_weight, o_weight, q_bias, v_bias, o_bias, gain_one, shift_one,
    up_weight, up_bias, down_weight, down_bias, gain_two, shift_two, cotangent,
):
    owners = lax.axis_size("dp")
    valid_keys = slot_valid(region_count, text_mask)
    weights = (q_weight, k_weight, v_weight, o_weight, up_weight, down_weight)
    small = (q_bias, v_bias, o_bias, gain_one, shift_one, up_bias, down_bias, gain_two, shift_two)
    seq = valid_keys.shape[1]
    width = hidden.shape[1]
    fits = (
        owners in (16, 32)
        and q_weight.shape[1] % 8 == 0
        and up_weight.shape[2] % (2 * width) == 0
        and seq <= ITEM
        and q_weight.shape[0] == 2
    )
    if not fits:
        return plain(weights, small, valid_keys, hidden, cotangent)
    mask = (valid_keys - 1.0) * 10000.0
    mask = jnp.pad(mask, ((0, 0), (0, ITEM - seq)), constant_values=PAD)[:, None, :]
    return blocks(weights, small, mask, hidden, cotangent, seq)


def solution(mesh):
    rows = P("dp", None)
    matrix = P(None, "dp", None)
    vector = P(None, "dp")
    four = (matrix,) * 4
    return jax.shard_map(
        shards,
        mesh=mesh,
        in_specs=(rows, P("dp"), rows) + four + (vector,) * 5
        + (matrix, vector, matrix, vector, vector, vector, rows),
        out_specs=(rows, rows) + four + (vector,) * 5
        + (matrix, vector, matrix, vector, vector, vector),
        check_vma=False,
    )
```

```python
import functools
import math

import jax
import jax.numpy as jnp
from jax import lax
from jax.experimental import pallas as pl
from jax.experimental.pallas import tpu as pltpu
from jax.sharding import PartitionSpec as P

HEADS = 12
HEAD_DIM = 64
REGIONS = 100

epsilon = 1e-12
F32 = jnp.float32
BF16 = jnp.bfloat16


def dense(left, right):
    return jnp.dot(left, right, preferred_element_type=F32)


def outer(left, right):
    return lax.dot_general(left, right, (((0,), (0,)), ((), ())), preferred_element_type=F32)


def back_dense(left, right):
    return lax.dot_general(left, right, (((1,), (1,)), ((), ())), preferred_element_type=F32)


def column_sum(values):
    return jnp.sum(values.astype(F32), axis=0)


def slot_valid(region_count, text_mask):
    region_slot = jnp.arange(REGIONS, dtype=jnp.int32)[None, :] < region_count[:, None]
    return jnp.concatenate([text_mask.astype(F32), region_slot.astype(F32)], axis=1)


def norm(values, gain, shift):
    center = values - jnp.mean(values, axis=-1, keepdims=True)
    spread = jnp.mean(center * center, axis=-1, keepdims=True)
    scale = lax.rsqrt(spread + epsilon)
    unit = center * scale
    return unit * gain + shift, (unit, scale)


def norm_back(saved, gain, grad):
    unit, scale = saved
    inner = grad * gain
    into = scale * (
        inner
        - jnp.mean(inner, axis=-1, keepdims=True)
        - unit * jnp.mean(inner * unit, axis=-1, keepdims=True)
    )
    return into, column_sum(grad * unit), column_sum(grad)


def forward_layer(inputs, weights, vectors, valid_keys):
    q_weight, k_weight, v_weight, o_weight, up_weight, down_weight = weights
    q_bias, v_bias, o_bias, gain_one, shift_one, up_bias, down_bias, gain_two, shift_two = vectors
    item_count = valid_keys.shape[0]
    row_count, width = inputs.shape

    def heads_of(values):
        return values.reshape(item_count, row_count // item_count, HEADS, HEAD_DIM)

    queries = heads_of((dense(inputs, q_weight) + q_bias).astype(BF16))
    key_rows = heads_of(dense(inputs, k_weight).astype(BF16))
    value_rows = heads_of((dense(inputs, v_weight) + v_bias).astype(BF16))
    scores = (
        jnp.einsum("bqhd,bkhd->bhqk", queries, key_rows, preferred_element_type=F32) * 0.125
    )
    scores = scores + (valid_keys[:, None, None, :] - 1.0) * 10000.0
    attention = jax.nn.softmax(scores, axis=-1)
    attention_low = attention.astype(BF16)
    context = jnp.einsum("bhqk,bkhd->bqhd", attention_low, value_rows, preferred_element_type=F32)
    context = context.astype(BF16).reshape(row_count, width)
    first_sum = inputs.astype(F32) + dense(context, o_weight) + o_bias
    middle, norm_one = norm(first_sum, gain_one, shift_one)
    middle = middle.astype(BF16)
    lifted = dense(middle, up_weight) + up_bias
    half = 0.5 * lax.erf(lifted * math.sqrt(0.5)) + 0.5
    activated = (lifted * half).astype(BF16)
    slope = half + lifted * jnp.exp(-0.5 * lifted * lifted) * (1.0 / math.sqrt(2.0 * math.pi))
    slope = slope.astype(BF16)
    second_sum = middle.astype(F32) + dense(activated, down_weight) + down_bias
    output, norm_two = norm(second_sum, gain_two, shift_two)
    saved = (queries, key_rows, value_rows, attention, attention_low, context, norm_one, middle, slope, activated, norm_two)
    return output.astype(BF16), saved


def backward_layer(inputs, weights, vectors, saved, out_grad, send):
    q_weight, k_weight, v_weight, o_weight, up_weight, down_weight = weights
    q_bias, v_bias, o_bias, gain_one, shift_one, up_bias, down_bias, gain_two, shift_two = vectors
    queries, key_rows, value_rows, attention, attention_low, context, norm_one, middle, slope, activated, norm_two = saved
    row_count, width = inputs.shape
    sum_grad, gain_two_grad, shift_two_grad = norm_back(norm_two, gain_two, out_grad)
    lowered_grad = sum_grad.astype(BF16)
    send("down", [outer(activated, lowered_grad)])
    lifted_grad = (back_dense(lowered_grad, down_weight) * slope).astype(BF16)
    send("up", [outer(middle, lifted_grad)])
    middle_grad = sum_grad + back_dense(lifted_grad, up_weight)
    first_grad, gain_one_grad, shift_one_grad = norm_back(norm_one, gain_one, middle_grad)
    attended_grad = first_grad.astype(BF16)
    o_grad = outer(context, attended_grad)
    context_grad = back_dense(attended_grad, o_weight).astype(BF16).reshape(queries.shape)
    attention_grad = jnp.einsum(
        "bqhd,bkhd->bhqk", context_grad, value_rows, preferred_element_type=F32
    )
    value_grad = jnp.einsum(
        "bhqk,bqhd->bkhd", attention_low, context_grad, preferred_element_type=F32
    )
    value_grad = value_grad.astype(BF16).reshape(row_count, width)
    weighed = attention * attention_grad
    score_grad = (weighed - attention * jnp.sum(weighed, axis=-1, keepdims=True)).astype(BF16)
    query_grad = (
        jnp.einsum("bhqk,bkhd->bqhd", score_grad, key_rows, preferred_element_type=F32) * 0.125
    )
    query_grad = query_grad.astype(BF16).reshape(row_count, width)
    key_grad = (
        jnp.einsum("bhqk,bqhd->bkhd", score_grad, queries, preferred_element_type=F32) * 0.125
    )
    key_grad = key_grad.astype(BF16).reshape(row_count, width)
    send("four", [outer(inputs, query_grad), outer(inputs, key_grad), outer(inputs, value_grad), o_grad])
    input_grad = (
        first_grad
        + back_dense(query_grad, q_weight)
        + back_dense(key_grad, k_weight)
        + back_dense(value_grad, v_weight)
    )
    small = (column_sum(query_grad), column_sum(value_grad), column_sum(attended_grad), gain_one_grad, shift_one_grad, column_sum(lifted_grad), column_sum(lowered_grad), gain_two_grad, shift_two_grad)
    return input_grad, small


def plain(weights, small, valid_keys, hidden, cotangent):
    owners = lax.axis_size("dp")
    layers = weights[0].shape[0]
    packed = jnp.concatenate([v.reshape(1, -1) for v in small], axis=1)
    packed = lax.all_gather(packed, "dp", axis=0, tiled=True).astype(F32)
    vectors = []
    offset = 0
    for v in small:
        size = v.shape[0] * v.shape[1]
        part = packed[:, offset : offset + size].reshape((owners,) + v.shape)
        vectors.append(jnp.swapaxes(part, 0, 1).reshape(layers, -1))
        offset += size
    vectors = [tuple(v[layer] for v in vectors) for layer in range(layers)]
    gathered = [
        tuple(lax.all_gather(w[layer], "dp", axis=0, tiled=True) for w in weights)
        for layer in range(layers)
    ]
    current = hidden
    inputs, saved = [], []
    for layer in range(layers):
        inputs.append(current)
        current, kept = forward_layer(current, gathered[layer], vectors[layer], valid_keys)
        saved.append(kept)
    flowing = cotangent.astype(F32)
    big = [{} for _ in range(layers)]
    tiny = [None] * layers
    for layer in reversed(range(layers)):

        def send(name, grads, layer=layer):
            big[layer][name] = [
                lax.psum_scatter(g.astype(BF16).reshape(owners, -1, g.shape[-1]), "dp", scatter_dimension=0, tiled=True)[0].astype(F32)
                for g in grads
            ]

        flowing, tiny[layer] = backward_layer(
            inputs[layer], gathered[layer], vectors[layer], saved[layer], flowing, send
        )
    flat = jnp.concatenate(
        [g.reshape(owners, -1) for layer in range(layers) for g in tiny[layer]], axis=1
    )
    flat = lax.psum_scatter(flat, "dp", scatter_dimension=0, tiled=True).reshape(layers, -1)
    summed = []
    offset = 0
    for v in small:
        summed.append(flat[:, offset : offset + v.shape[1]])
        offset += v.shape[1]
    q_b, v_b, o_b, g_one, s_one, u_b, d_b, g_two, s_two = summed
    fours = [jnp.stack([big[layer]["four"][i] for layer in range(layers)]) for i in range(4)]
    up = jnp.stack([big[layer]["up"][0] for layer in range(layers)])
    down = jnp.stack([big[layer]["down"][0] for layer in range(layers)])
    return (
        current, flowing, *fours,
        q_b, v_b, o_b, g_one, s_one, up, u_b, down, d_b, g_two, s_two,
    )


ITEM = 256
PAD = -1e30


def table_of(owners):
    chips = owners // 2
    depth = chips // 4
    me = lax.axis_index("dp")
    chip, core = me // 2, me % 2
    walk = jnp.arange(chips, dtype=jnp.int32)

    def chip_at(position, core):
        z, first, second = position % depth, position // depth % 2, position // (2 * depth)
        return chip ^ (z * 4 + jnp.where(core == 0, second * 2 + first, first * 2 + second))

    def place_of(other, core):
        z, y, x = (other ^ chip) // 4, (other ^ chip) // 2 % 2, (other ^ chip) % 2
        return z + depth * jnp.where(core == 0, x + 2 * y, y + 2 * x)

    return jnp.concatenate(
        [chip_at(walk, core), chip_at(walk, 1 - core), place_of(walk, core), place_of(walk, 1 - core), core[None]]
    ).astype(jnp.int32)


def flip(value, owners, even, odd):
    return lax.ppermute(value, "dp", [(i, i ^ (odd if i % 2 else even)) for i in range(owners)])


MICROS = 50


def padded_bytes(shape, dtype):
    *lead, rows, columns = (1,) * max(0, 2 - len(shape)) + tuple(shape)
    return math.prod(lead) * (-(-rows // 16) * 16) * (-(-columns // 128) * 128) * jnp.dtype(dtype).itemsize


class Held:
    def __init__(self, room, copy, inward):
        self.room, self.copy, self.inward, self.open = room, copy, inward, True
        self.shape, self.dtype = room.shape, room.dtype
        self.begun = False

    def begin(self):
        if self.inward and not self.begun:
            self.copy.start()
            self.begun = True

    def ready(self):
        if self.inward and self.open:
            self.begin()
            self.copy.wait()
            self.open = False

    def send(self):
        if not self.inward and self.open:
            self.copy.start()
            self.open = False

    def __getitem__(self, at):
        self.ready()
        return self.room[at]

    def __setitem__(self, at, value):
        self.room[at] = value


class Near:
    def __init__(self, room):
        self.room, self.shape, self.dtype = room, room.shape, room.dtype

    def begin(self):
        pass

    def ready(self):
        pass

    def send(self):
        pass

    def __getitem__(self, at):
        return self.room[at]

    def __setitem__(self, at, value):
        self.room[at] = value


HELD = ("feed_back",)


def launch(body, outs, smem=(), vmem=(), hbm=(), deps=(), scratch=(), extra=3, far=pl.ANY, held=False, late=()):
    counts = (len(smem), len(vmem), len(hbm), len(deps), len(outs))
    name = getattr(body, "func", body).__name__
    wrap = held
    held = name in HELD
    sizes = [(v.shape, v.dtype) for v in vmem] + list(outs)
    large = [held and padded_bytes(*v) > 2**16 for v in sizes]
    rooms = [pltpu.VMEM(*v) for v, big in zip(sizes, large) if big]
    own = len(scratch)
    scratch = list(scratch) + rooms + ([pltpu.SemaphoreType.DMA((len(rooms),))] if rooms else [])
    budget = sizes + [(v.shape, v.dtype) for v in scratch[:own] if jnp.issubdtype(v.dtype, jnp.floating)]
    limit = (extra + 10 * wrap) * 2**20 + sum(padded_bytes(shape, dtype) for shape, dtype in budget)

    def kernel(*refs):
        groups, at = [], 0
        for count in counts:
            groups.append(list(refs[at : at + count]))
            at += count
        left = list(refs[at + own :])
        sems = left.pop() if rooms else None
        moved = []
        for group, base, inward in ((groups[1], 0, True), (groups[4], len(vmem), False)):
            for i, ref in enumerate(group):
                if large[base + i]:
                    room, sem = left.pop(0), sems.at[len(moved)]
                    copy = pltpu.make_async_copy(ref, room, sem) if inward else pltpu.make_async_copy(room, ref, sem)
                    group[i] = Held(room, copy, inward)
                    moved.append(group[i])
                    if inward and i not in late:
                        group[i].begin()
                elif wrap:
                    group[i] = Near(ref)
        body(groups[0], groups[1], groups[2], groups[4], refs[at : at + own])
        for one in moved:
            one.ready()
            one.send()
        for one in moved:
            if not one.inward:
                one.copy.wait()

    space = lambda big: pl.BlockSpec(memory_space=pl.ANY if big else pltpu.VMEM)
    in_specs = (
        [pl.BlockSpec(memory_space=pltpu.SMEM)] * len(smem)
        + [space(big) for big in large[: len(vmem)]]
        + [pl.BlockSpec(memory_space=far)] * len(hbm)
        + [pl.BlockSpec(memory_space=pl.ANY)] * len(deps)
    )
    return pl.pallas_call(
        kernel,
        out_shape=[jax.ShapeDtypeStruct(s, d) for s, d in outs],
        in_specs=in_specs,
        out_specs=[space(big) for big in large[len(vmem) :]],
        scratch_shapes=list(scratch),
        name=name,
        compiler_params=pltpu.CompilerParams(vmem_limit_bytes=limit),
        cost_estimate=pl.CostEstimate(
            flops=int(MICROS * 1e9), bytes_accessed=int(MICROS * 3e6), transcendentals=0
        ),
    )(*smem, *vmem, *hbm, *deps)


def mm(left, right):
    return jnp.dot(left, right, preferred_element_type=F32)


def mm_nt(left, right):
    return lax.dot_general(left, right, (((1,), (1,)), ((), ())), preferred_element_type=F32)


def mm_tn(left, right):
    return lax.dot_general(left, right, (((0,), (0,)), ((), ())), preferred_element_type=F32)


def fetch(tab, parts, kind, section, whole, sems, columns=None, step=768):
    near, near_more, far, far_more = parts
    half = near.shape[0]
    rows = whole.shape[-2] // (2 * half)
    core = tab[8 * half]
    first, last = (0, whole.shape[-1]) if columns is None else columns
    if (last - first) % step:
        step = last - first
    count = 0
    sides = []
    for side, group in enumerate(((near, near_more), (far, far_more))):
        hand = core if side == 0 else 1 - core
        steps = []
        for at in [0] if kind == "down" else range(first, last, step):
            copies = []
            for which, part in enumerate(group):
                for b in range(half):
                    start = pl.multiple_of(tab[(2 * side + which) * half + b] * rows, 16)
                    moves = []
                    if kind == "down":
                        wide, deep = part.shape[2] // 4, rows // 4
                        for g in range(4):
                            source = part.at[b, pl.ds(section * deep, deep), pl.ds(g * wide, wide)]
                            to = pl.ds(start + g * deep, deep)
                            if len(whole.shape) == 3:
                                moves.append((source, whole.at[hand, to]))
                            else:
                                at = pl.ds(pl.multiple_of(hand * wide, 128), wide)
                                moves.append((source, whole.at[to, at]))
                    else:
                        wide = 768 if step % 768 == 0 else 384
                        for piece in range(at, at + step, wide):
                            source = part.at[b, pl.ds(section * rows, rows), pl.ds(piece, wide)]
                            target = whole.at[hand, pl.ds(start, rows), pl.ds(piece - first, wide)]
                            moves.append((source, target))
                    for source, target in moves:
                        copies.append(pltpu.make_async_copy(source, target, sems.at[count]))
                        copies[-1].start()
                        count += 1
            steps.append(copies)
        sides.append(steps)
    return sides


def finish_all(sides):
    for steps in sides:
        for copies in steps:
            finish(copies)


def finish(copies):
    for copy in copies:
        copy.wait()


def norm_rows(values):
    center = values - jnp.mean(values, axis=-1, keepdims=True)
    scale = lax.rsqrt(jnp.mean(center * center, axis=-1, keepdims=True) + epsilon)
    return center * scale, scale


def norm_rows_back(unit, scale, inner):
    return scale * (
        inner
        - jnp.mean(inner, axis=-1, keepdims=True)
        - unit * jnp.mean(inner * unit, axis=-1, keepdims=True)
    )


def gelu_and_slope(v):
    phi = 0.5 + 0.5 * lax.erf(v * math.sqrt(0.5))
    return v * phi, phi + v * jnp.exp(-0.5 * v * v) * (1.0 / math.sqrt(2.0 * math.pi))


def put_rows_apart(source, room, seq):
    count = source.shape[0]
    room[count:, :] = jnp.zeros((room.shape[0] - count, room.shape[1]), F32)
    room[0:count, :] = source[...].astype(F32)
    row = lax.broadcasted_iota(jnp.int32, (ITEM, room.shape[1]), 0)
    return [
        jnp.where(row < seq, room[i * seq : i * seq + ITEM, :], 0.0) for i in range(count // seq)
    ]


def put_rows_together(values, out, seq):
    for i in range(values.shape[0] // ITEM):
        out[i * seq : (i + 1) * seq, :] = values[i * ITEM : i * ITEM + seq]


Q_B, V_B, O_B, G_ONE, S_ONE, D_B, G_TWO, S_TWO, UP_B = range(9)


def split_own(smem, vmem, hbm, outs, scratch):
    (tab,) = smem
    core = tab[tab.shape[0] - 1]
    copies = [pltpu.make_async_copy(w, room, scratch[-1].at[i]) for i, (w, room) in enumerate(zip(hbm, scratch))]
    for copy in copies:
        copy.start()
    finish(copies)
    table = scratch[-2]
    vmem = scratch[6 : len(hbm)]
    table[...] = jnp.zeros_like(table)
    short = [v for v in vmem if v.shape[1] == vmem[0].shape[1]]
    (long,) = [v for v in vmem if v.shape[1] != vmem[0].shape[1]]
    layers = long.shape[0]
    for layer in range(layers):
        for i, v in enumerate(short):
            at = layer * len(short) + i
            table[at : at + 1, 0 : v.shape[1]] = v[layer : layer + 1, :].astype(F32)
        at = layers * len(short) + layer
        table[at : at + 1, 0 : long.shape[1]] = long[layer : layer + 1, :].astype(F32)
    q, k, v, o, up, down = scratch[:6]
    for layer in range(layers):
        for place, hand in ((0, core), (1, 1 - core)):
            four, wide, tall = outs[6 * layer + 3 * place : 6 * layer + 3 * place + 3]
            part = q.shape[2] // 2
            at = pl.ds(pl.multiple_of(hand * part, 128), part)
            for i, w in enumerate((q, k, v, o)):
                four[:, i * part : (i + 1) * part] = w[layer, :, at]
            if four.shape[1] > 4 * part:
                four[:, 4 * part :] = table[...].astype(BF16)
            part = up.shape[2] // 2
            wide[...] = up[layer, :, pl.ds(pl.multiple_of(hand * part, 128), part)]
            part = down.shape[2] // 2
            tall[...] = down[layer, :, pl.ds(pl.multiple_of(hand * part, 128), part)]


def join_rows(smem, vmem, hbm, outs, scratch, kinds):
    (tab,) = smem
    first = tab[tab.shape[0] - 1] == 0
    (out,) = outs
    rows = out.shape[0] // len(kinds)
    for i, kind in enumerate(kinds):
        mine, came = vmem[2 * i][...].astype(F32), vmem[2 * i + 1][...].astype(F32)
        upper, lower = jnp.where(first, mine, came), jnp.where(first, came, mine)
        at = slice(i * rows, (i + 1) * rows)
        if kind != "down":
            out[at, :] = jnp.concatenate([upper, lower], axis=0).astype(BF16)
            continue
        wide = upper.shape[1]
        for g in range(4):
            part = (upper, lower)[g // 2][g % 2 * rows : (g % 2 + 1) * rows]
            out[at, g * wide : (g + 1) * wide] = part.astype(BF16)


def place_vectors(smem, vmem, hbm, outs, scratch):
    (tab,) = smem
    room, sems = scratch
    half, rows, side = room.shape[0] // 2, room.shape[1], room.shape[2]
    copies = []
    for i, part in enumerate(hbm):
        source = part.at[:, :, pl.ds(part.shape[2] - side, side)]
        copies.append(pltpu.make_async_copy(source, room.at[pl.ds(i * half, half)], sems.at[i]))
        copies[-1].start()
    finish(copies)
    width = outs[0].shape[1]
    own = rows // 2
    devices = 4 * half
    count = width // devices
    wide = outs[0].shape[0] - 8
    short = jnp.zeros((16, width), F32)
    long = [jnp.zeros((8, width), F32) for _ in range(wide)]
    for b in range(2 * half):
        block = room[b].astype(F32)
        for k in (0, 1):
            device = 2 * tab[b] + k
            part = block[k * own : (k + 1) * own]
            part = jnp.concatenate([part, jnp.zeros((own, width - side), F32)], axis=1)
            short = short + pltpu.roll(part[:16], device * count, 1)
            start = device * count * wide
            moved = pltpu.roll(part[16:24], start % width, 1)
            for i in range(wide):
                long[i] = long[i] + jnp.where(start // width == i, moved, 0.0)
    for layer, out in enumerate(outs):
        out[0:8, :] = short[8 * layer : 8 * layer + 8]
        for i in range(wide):
            out[8 + i : 9 + i, :] = long[i][layer : layer + 1]


def join_blocks(smem, vmem, hbm, outs, scratch, rows_at=0):
    (out,) = outs
    (sems,) = scratch
    at = 0
    copies = []
    for part in hbm:
        if len(part.shape) == 3:
            source, target = part, out.at[pl.ds(at, part.shape[0])]
            at += part.shape[0]
        else:
            source, target = part.at[pl.ds(rows_at, out.shape[1])], out.at[at]
            at += 1
        copies.append(pltpu.make_async_copy(source, target, sems.at[len(copies)]))
        copies[-1].start()
    finish(copies)


def attend_forward(smem, vmem, hbm, outs, scratch, sections, seq):
    (tab,) = smem
    x, vec, mask = vmem
    q, k, v, p, context, unit, scale, middle = outs[:8]
    whole, o_whole = outs[8].room, outs[9].room
    sems, o_sems = scratch[:2]
    half = x.shape[1] // 2
    sides = fetch(tab, hbm, "four", sections[0], whole, sems, columns=(0, 3 * half), step=3 * half)
    late = fetch(tab, hbm, "four", sections[0], o_whole, o_sems, columns=(3 * half, 4 * half))
    if len(outs) > 10:
        for i, item in enumerate(put_rows_apart(x, scratch[2], seq)):
            outs[10][i * ITEM : (i + 1) * ITEM, :] = item.astype(BF16)
        x = outs[10]
        x.send()
    core = tab[tab.shape[0] - 1]
    for steps, h in zip(sides, (core, 1 - core)):
        finish(steps[0])
        at = pl.ds(pl.multiple_of(h * half, 128), half)
        made = mm(x[...], whole[h])
        if h is not core:
            outs[8].send()
        q[:, at] = (made[:, 0:half] + vec[Q_B : Q_B + 1, at]).astype(BF16)
        k[:, at] = made[:, half : 2 * half].astype(BF16)
        v[:, at] = (made[:, 2 * half :] + vec[V_B : V_B + 1, at]).astype(BF16)
    low = lax.broadcasted_iota(jnp.int32, (ITEM, 2 * HEAD_DIM), 1) < HEAD_DIM
    items = x.shape[0] // ITEM

    for i in range(HEADS // 2):
        at = slice(i * 2 * HEAD_DIM, (i + 1) * 2 * HEAD_DIM)
        for item in range(items):
            rows = slice(item * ITEM, (item + 1) * ITEM)
            qs, ks, vs = q[rows, at], k[rows, at], v[rows, at]
            made = []
            for side in (0, 1):
                own = low if side == 0 else jnp.logical_not(low)
                s = mm_nt(jnp.where(own, qs, jnp.zeros_like(qs)), ks) * 0.125 + mask[item]
                e = jnp.exp(s - jnp.max(s, axis=-1, keepdims=True))
                w = (e * (1.0 / jnp.sum(e, axis=-1, keepdims=True))).astype(BF16)
                p[item * HEADS + 2 * i + side] = w
                made.append(mm(w, vs))
            context[rows, at] = jnp.where(low, made[0], made[1]).astype(BF16)
    finish_all(late)
    for out in (q, k, v, p, context, outs[9]):
        out.send()
    attended = jnp.concatenate([mm(context[...], o_whole[h]) for h in (0, 1)], axis=1)
    first = x[...].astype(F32) + (attended + vec[O_B : O_B + 1, :])
    made, made_scale = norm_rows(first)
    unit[...] = made
    scale[...] = made_scale
    middle[...] = (made * vec[G_ONE : G_ONE + 1, :] + vec[S_ONE : S_ONE + 1, :]).astype(BF16)


def lift(smem, vmem, hbm, outs, scratch, sections):
    (tab,) = smem
    middle, vec = vmem
    activated, slope, kept = outs
    whole = kept.room
    (sems,) = scratch
    width = vec.shape[1]
    sides = fetch(tab, hbm, "up", sections[0], whole, sems, step=width)
    core = tab[tab.shape[0] - 1]
    step = width // 3
    for steps, h in zip(sides, (core, 1 - core)):
        for i, copies in enumerate(steps):
            finish(copies)
            for j in range(3):
                at = slice(i * width + j * step, i * width + (j + 1) * step)
                bias = vec[pl.ds(UP_B + h * len(steps) + i, 1), j * step : (j + 1) * step]
                a, s = gelu_and_slope(mm(middle[...], whole[h, :, at]) + bias)
                activated[h, :, at] = a.astype(BF16)
                slope[h, :, at] = s.astype(BF16)
    kept.send()


def lower(smem, vmem, hbm, outs, scratch, sections, seq):
    (tab,) = smem
    activated, middle, vec = vmem
    output, unit, scale, kept = outs
    whole = kept.room
    finish_all(fetch(tab, hbm, "down", sections[0], whole, scratch[0]))
    kept.send()
    deep = activated.shape[2]
    lowered = mm(activated[0], whole[0:deep, :]) + mm(activated[1], whole[deep:, :])
    second = middle[...].astype(F32) + (lowered + vec[D_B : D_B + 1, :])
    made, made_scale = norm_rows(second)
    unit[...] = made
    scale[...] = made_scale
    made = made * vec[G_TWO : G_TWO + 1, :] + vec[S_TWO : S_TWO + 1, :]
    if len(scratch) > 1:
        put_rows_together(made, scratch[1], seq)
        output[...] = scratch[1][...].astype(BF16)
    else:
        output[...] = made.astype(BF16)


def rows_sum(values):
    return jnp.sum(values, axis=0, keepdims=True)


SUM_G_TWO, SUM_S_TWO, SUM_D_B, SUM_UP_B = 0, 1, 2, 8
SUM_G_ONE, SUM_S_ONE, SUM_O_B = 0, 1, 2


def feed_back(smem, vmem, hbm, outs, scratch, seq):
    (tab,) = smem
    grad, unit_two, scale_two, vec, activated, down_whole, slope, middle = vmem
    sum_grad, lifted_grad, down_send, down_keep, up_send, up_keep, sums = outs
    turned, low_grad = scratch[:2]
    chips, rows, part = up_send.shape
    core = tab[4 * chips]
    if len(scratch) > 2:
        g = jnp.concatenate(put_rows_apart(grad, scratch[2], seq), axis=0)
    else:
        g = grad[...]
    u = unit_two[...]
    made = norm_rows_back(u, scale_two[...], g * vec[G_TWO : G_TWO + 1, :])
    sum_grad[...] = made
    sum_grad.send()
    low = made.astype(BF16)
    half = low.shape[1] // 2
    low_grad[0] = low[:, :half]
    low_grad[1] = low[:, half:]
    sums[...] = jnp.zeros_like(sums)
    sums[SUM_G_TWO : SUM_G_TWO + 1, :] = rows_sum(g * u)
    sums[SUM_S_TWO : SUM_S_TWO + 1, :] = rows_sum(g)
    sums[SUM_D_B : SUM_D_B + 1, :] = rows_sum(low.astype(F32))
    activated.ready()
    for one in (down_whole, slope, middle):
        one.begin()
    deep = activated.shape[2]
    wide = part // 4
    for out, hand, places in ((down_send, 1 - core, 3), (down_keep, core, 2)):
        right = low_grad[hand]
        for h in (0, 1):
            for j in range(deep // (8 * rows)):
                made = mm_tn(activated[h, :, 8 * rows * j : 8 * rows * (j + 1)], right).astype(BF16)
                for i in (0, 1):
                    chip = h * deep // (4 * rows) + 2 * j + i
                    to = tab[places * chips + chip]
                    for g in range(4):
                        at = (4 * i + g) * rows
                        out[to, :, g * wide : (g + 1) * wide] = made[at : at + rows]
    for out in (down_send, down_keep):
        out.send()
    turned[...] = middle[...].T
    down_whole.ready()
    slope.ready()
    width = sums.shape[1]
    step = width
    for h in (0, 1):
        for j in range(part // step):
            at = slice(j * step, (j + 1) * step)
            rows_at = slice(h * part + j * step, h * part + (j + 1) * step)
            made = mm_nt(low, down_whole[rows_at, :])
            made = (made * slope[h, :, at].astype(F32)).astype(BF16)
            lifted_grad[h, :, at] = made
            column = h * part + j * step
            to = SUM_UP_B + column // width
            sums[to : to + 1, column % width : column % width + step] = rows_sum(made.astype(F32))
    lifted_grad.send()
    for out, hand, places in ((up_send, 1 - core, 3), (up_keep, core, 2)):
        for j in range(part // step):
            at = slice(j * step, (j + 1) * step)
            made = mm(turned[...], lifted_grad[hand, :, at]).astype(BF16)
            for chip in range(chips):
                out[tab[places * chips + chip], :, at] = made[chip * rows : (chip + 1) * rows]
        out.send()


def first_norm_back(smem, vmem, hbm, outs, scratch):
    lifted_grad, up_whole, sum_grad, unit_one, scale_one, vec = vmem
    first_grad, attended_grad, sums = outs
    sums[...] = jnp.zeros_like(sums)
    g = sum_grad[...] + mm_nt(lifted_grad[0], up_whole[0]) + mm_nt(lifted_grad[1], up_whole[1])
    u = unit_one[...]
    made = norm_rows_back(u, scale_one[...], g * vec[G_ONE : G_ONE + 1, :])
    first_grad[...] = made
    low = made.astype(BF16)
    half = low.shape[1] // 2
    attended_grad[0] = low[:, :half]
    attended_grad[1] = low[:, half:]
    sums[SUM_G_ONE : SUM_G_ONE + 1, :] = rows_sum(g * u)
    sums[SUM_S_ONE : SUM_S_ONE + 1, :] = rows_sum(g)
    sums[SUM_O_B : SUM_O_B + 1, :] = rows_sum(low.astype(F32))


def attend_back(smem, vmem, hbm, outs, scratch):
    (tab,) = smem
    attended_grad, o_whole, q, k, v, p, x, context = vmem[:8]
    send, keep, sums, grads = outs
    x_turned, c_turned, context_grad = scratch[:3]
    chips, rows, _ = send.shape
    half = x.shape[1] // 2
    core = tab[4 * chips]
    x_turned[...] = x[...].T
    c_turned[...] = context[...].T
    made = mm_nt(attended_grad[0], o_whole[0]) + mm_nt(attended_grad[1], o_whole[1])
    context_grad[...] = made.astype(BF16)
    items = q.shape[0] // ITEM
    low = lax.broadcasted_iota(jnp.int32, (ITEM, 2 * HEAD_DIM), 1) < HEAD_DIM
    pairs = HEADS // 4
    sides = (low, jnp.logical_not(low))
    apart = lambda values: [jnp.where(own, values, jnp.zeros_like(values)) for own in sides]
    for h in (0, 1):
        grads[h, :, 3 * half :] = attended_grad[h]
        for i in range(pairs):
            at = slice(h * half + i * 2 * HEAD_DIM, h * half + (i + 1) * 2 * HEAD_DIM)
            for item in range(items):
                rows_at = slice(item * ITEM, (item + 1) * ITEM)
                qs, ks, vs, cs = q[rows_at, at], k[rows_at, at], v[rows_at, at], context_grad[rows_at, at]
                ws = [p[item * HEADS + 2 * (h * pairs + i) + side] for side in (0, 1)]
                ds = []
                for w, c in zip(ws, apart(cs)):
                    wide = w.astype(F32)
                    g = wide * mm_nt(c, vs)
                    ds.append((g - wide * jnp.sum(g, axis=-1, keepdims=True)).astype(BF16))
                stacked = lambda values: jnp.concatenate(apart(values), axis=0)
                made = (
                    mm(jnp.concatenate(ds, axis=1), stacked(ks)) * 0.125,
                    mm_tn(jnp.concatenate(ds, axis=0), stacked(qs)) * 0.125,
                    mm_tn(jnp.concatenate(ws, axis=0), stacked(cs)),
                )
                for place, both in enumerate(made):
                    start = place * half + i * 2 * HEAD_DIM
                    grads[h, rows_at, start : start + 2 * HEAD_DIM] = both.astype(BF16)
    grads.send()
    for out, hand, places in ((send, 1 - core, 3), (keep, core, 2)):
        for j in range(4):
            at = slice(j * half, (j + 1) * half)
            made = mm((c_turned if j == 3 else x_turned)[...], grads[hand, :, at]).astype(BF16)
            for chip in range(chips):
                out[tab[places * chips + chip], :, at] = made[chip * rows : (chip + 1) * rows]
        if len(vmem) == 8:
            out.send()
    sums[...] = jnp.zeros_like(sums)
    for h in (0, 1):
        at = slice(h * half, (h + 1) * half)
        sums[0:1, at] = rows_sum(grads[h, :, 0:half].astype(F32))
        sums[1:2, at] = rows_sum(grads[h, :, 2 * half : 3 * half].astype(F32))
    if len(vmem) == 8:
        return
    short, long = scratch[3:5]
    wide = long.shape[0] // 2
    for layer, (feed, other, four) in enumerate((vmem[8:10] + [sums], vmem[10:13])):
        at = layer * 8
        short[at : at + 2, :] = four[0:2, :]
        short[at + 2 : at + 3, :] = other[SUM_O_B : SUM_O_B + 1, :]
        short[at + 3 : at + 5, :] = other[SUM_G_ONE : SUM_G_ONE + 2, :]
        short[at + 5 : at + 6, :] = feed[SUM_D_B : SUM_D_B + 1, :]
        short[at + 6 : at + 8, :] = feed[SUM_G_TWO : SUM_G_TWO + 2, :]
        long[layer * wide : (layer + 1) * wide, :] = feed[SUM_UP_B : SUM_UP_B + wide, :]
    width = x.shape[1]
    side = send.shape[2] - 4 * half
    count = width // (2 * chips)
    lanes = lax.broadcasted_iota(jnp.int32, (16, side), 1)
    last = lax.broadcasted_iota(jnp.int32, (8, side), 0)
    for chip in range(chips):
        shares = []
        for device in (2 * chip, 2 * chip + 1):
            part = pltpu.roll(short[...], (width - device * count) % width, 1)[:, :side]
            shares.append(jnp.where(lanes < count, part, 0.0))
            start = device * count * wide
            turn = (width - start % width) % width
            part = pltpu.roll(long[...], turn, 1)[:, :side]
            first, second = start // width, wide + start // width
            part = jnp.where(last == 0, part[first : first + 1], jnp.where(last == 1, part[second : second + 1], 0.0))
            shares.append(jnp.where(lanes[:8] < count * wide, part, 0.0))
        block = jnp.concatenate(shares, axis=0).astype(BF16)
        for out, places in ((send, 3), (keep, 2)):
            out[tab[places * chips + chip], :, 4 * half :] = block


def attend_back_last(smem, vmem, hbm, outs, scratch, seq):
    first_grad, grads, whole = vmem
    (out,) = outs
    deep = whole.shape[2]
    made = first_grad[...] + mm_nt(grads[0, :, :deep], whole[0]) + mm_nt(grads[1, :, :deep], whole[1])
    if out.shape[0] == made.shape[0]:
        out[...] = made
    else:
        put_rows_together(made, out, seq)


def add_halves(smem, vmem, hbm, outs, scratch):
    send, kept = outs
    half = send.shape[0]
    rows = send.shape[1] // (len(vmem) // 2)

    def block(b, carry):
        for i in range(len(vmem) // 2):
            keep, came = vmem[2 * i], vmem[2 * i + 1]
            at = slice(i * rows, (i + 1) * rows)
            kept[b, at] = (keep[b].astype(F32) + came[b].astype(F32)).astype(BF16)
            send[b, at] = (keep[half + b].astype(F32) + came[half + b].astype(F32)).astype(BF16)
        return carry

    lax.fori_loop(0, half, block, 0)


def add_spread(smem, vmem, hbm, outs, scratch):
    at = 0
    for keep, came in zip(vmem[0::2], vmem[1::2]):
        rows = keep.shape[1]
        for b, out in enumerate(outs):
            out[at : at + rows] = (keep[b].astype(F32) + came[b].astype(F32)).astype(out.dtype)
        at += rows


def add_last(smem, vmem, hbm, outs, scratch, kinds=()):
    (tab,) = smem
    core = tab[tab.shape[0] - 1]
    (total,) = scratch
    made = vmem[0][...].astype(F32)
    for came in vmem[1:]:
        made = made + came[...].astype(F32)
    total[...] = made
    rows = total.shape[0] // len(kinds)
    half = rows // 2
    for i, kind in enumerate(kinds):
        to = slice(i * half, (i + 1) * half)
        for out, hand in zip(outs, (core, 1 - core)):
            if kind == "down":
                wide = total.shape[1] // 2
                at = pl.ds(pl.multiple_of(hand * wide, 128), wide)
                for g in (0, 1):
                    part = total[i * rows + g * half : i * rows + (g + 1) * half, at]
                    out[to, g * wide : (g + 1) * wide] = part
            else:
                out[to, :] = total[pl.ds(pl.multiple_of(i * rows + hand * half, 8), half), :]


def write_out(smem, vmem, hbm, outs, scratch, kind, sections):
    (tab,) = smem
    core = tab[tab.shape[0] - 1]
    half = outs[0].shape[2] // 2
    for layer, section in enumerate(sections):
        for hand, part in ((core, vmem[2 * layer]), (1 - core, vmem[2 * layer + 1])):
            at = pl.ds(pl.multiple_of(hand * half, 128), half)
            if kind == "down":
                rows = outs[0].shape[1] // 4
                for g in range(4):
                    start = (g % 2 * 2 + g // 2) * half
                    to = slice(g * rows, (g + 1) * rows)
                    outs[0][layer, to, at] = part[section * rows : (section + 1) * rows, start : start + half]
                continue
            rows = outs[0].shape[1]
            for i, out in enumerate(outs[:4] if kind == "four" else outs):
                out[layer, :, at] = part[section * rows : (section + 1) * rows, i * half : (i + 1) * half]
    if kind != "four":
        return
    part = vmem[0]
    start = 4 * half
    for i, out in enumerate(outs[4:]):
        count = out.shape[1]
        for layer in range(out.shape[0]):
            at = 16 + layer if i == 8 else 8 * layer + i
            out[layer : layer + 1, :] = part[at : at + 1, start : start + count]


class Chain:
    def __init__(self):
        self.token = None

    def __call__(self, body, outs, after=(), **kinds):
        deps = list(after) + ([] if self.token is None else [self.token])
        made = launch(body, outs, deps=deps, **kinds)
        self.token = min(made, key=lambda m: m.size)
        return made


def blocks(weights, small, mask, hidden, cotangent, seq):
    q_weight, k_weight, v_weight, o_weight, up_weight, down_weight = weights
    owners = lax.axis_size("dp")
    chips = owners // 2
    depth = chips // 4
    layers, rows, width = q_weight.shape
    wide = up_weight.shape[2]
    tall = hidden.shape[0] // seq * ITEM
    tab = table_of(owners)
    chain = Chain()
    dma = lambda n: pltpu.SemaphoreType.DMA((n,))
    vmem = lambda shape, dtype: pltpu.VMEM(shape, dtype)
    xy_one = lambda v: flip(v, owners, 2, 4)
    xy_two = lambda v: flip(v, owners, 4, 2)
    core_flip = lambda v: flip(v, owners, 1, 1)
    z_flip = lambda v, k: flip(v, owners, 8 * k, 8 * k)
    order = [v for v in small if v.shape[1] == rows] + [v for v in small if v.shape[1] != rows]

    side = 128
    block = (2 * rows, 2 * width)
    kinds = ("four", "up", "down")
    groups = [[(layer, kind)] for layer in range(layers) for kind in kinds]
    shapes = [(len(g) * block[0], block[1] + (side if i == 0 else 0)) for i, g in enumerate(groups)]
    halves = lambda layer: [((rows, 2 * width + (0 if layer else side)), BF16), ((rows, wide // 2), BF16), ((down_weight.shape[1], width // 2), BF16)]
    split = chain(
        split_own, [h for layer in range(layers) for h in halves(layer) * 2], smem=[tab], hbm=list(weights) + order, far=pltpu.HBM,
        scratch=[vmem(w.shape, BF16) for w in list(weights) + order] + [vmem((rows, side), F32), dma(6 + len(order))], extra=57,
    )
    mine = {(layer, kind): split[6 * layer + i] for layer in range(layers) for i, kind in enumerate(kinds)}
    other = {(layer, kind): core_flip(split[6 * layer + 3 + i]) for layer in range(layers) for i, kind in enumerate(kinds)}
    own, z_came, x_one, x_two, stacked, near, far = ({} for _ in range(7))

    direct = 2
    rest = [piece for group in groups[direct:] for piece in group]
    row_of = {piece: i * block[0] for i, piece in enumerate(rest)}

    def join(pieces, shape):
        (made,) = chain(
            functools.partial(join_rows, kinds=tuple(kind for _, kind in pieces)), [(shape, BF16)], smem=[tab],
            vmem=[v for piece in pieces for v in (mine[piece], other[piece])],
        )
        return made

    def begin():
        for g in range(direct):
            own[g] = join(groups[g], shapes[g])
            z_came[g] = [z_flip(own[g], k) for k in range(1, depth)]
        own["rest"] = join(rest, (len(rest) * block[0], block[1]))
        z_came["rest"] = z_flip(own["rest"], 1)

    def stack(sources, count, shape, rows_at=0, after=()):
        (made,) = chain(functools.partial(join_blocks, rows_at=rows_at), [((count,) + shape, BF16)], hbm=sources, scratch=[dma(count)], after=after)
        return made

    def far_round(g):
        stacked[g] = stack([own["rest"], z_came["rest"]], 2, shapes[g], row_of[groups[g][0]])
        z_came[g, 2] = z_flip(stacked[g], 2)

    def first_stack(g, after=()):
        sources = [own[g]] + z_came[g] if g < direct else [stacked[g], z_came[g, 2]]
        stacked[g] = stack(sources, depth, shapes[g], after=after)
        x_one[g] = xy_one(stacked[g])

    def second_stack(g, after=()):
        made = stack([stacked[g], x_one[g]], 2 * depth, shapes[g], after=after)
        x_two[g] = xy_two(made)
        near[g] = [made, x_two[g]]
        far[g] = [core_flip(made)]

    def third(g):
        value = lax.optimization_barrier((x_two[g], chain.token))[0]
        x_two[g] = value
        near[g][1] = value
        far[g].append(core_flip(value))

    def parts(layer, kind):
        (g,) = [i for i, group in enumerate(groups) if (layer, kind) in group]
        return near[g] + far[g]

    def section(layer, kind):
        return [group.index((layer, kind)) for group in groups if (layer, kind) in group][0]

    height = {"four": width, "up": width, "down": wide}
    across = {"four": 2 * width, "up": wide // 2, "down": width // 2}
    whole = lambda kind, columns=None: [vmem((2, height[kind], columns or across[kind]), BF16), dma(8 * chips)]
    xs, kept = [hidden], [{} for _ in range(layers)]
    row = lambda dtype: ((tall, width), dtype)
    column = ((tall, 1), F32)
    deep = ((2, tall, wide // 2), BF16)
    items = tall // ITEM

    def forward_attend(layer):
        s = kept[layer]
        raw = xs[layer].shape[0] != tall
        made = chain(
            functools.partial(attend_forward, sections=[section(layer, "four")], seq=seq),
            [row(BF16)] * 3 + [((items * HEADS, ITEM, ITEM), BF16), row(BF16), row(F32), column, row(BF16)]
            + [((2, width, width * 3 // 2), BF16), ((2, width, width // 2), BF16)] + [row(BF16)] * raw,
            held=True, smem=[tab], vmem=[xs[layer], vec[layer], mask], hbm=parts(layer, "four"),
            scratch=[dma(8 * chips)] * 2 + [vmem((tall, width), F32)] * raw,
        )
        s["q"], s["k"], s["v"], s["p"], s["context"], s["unit_one"], s["scale_one"], s["middle"] = made[:8]
        s["three"], s["o"] = made[8:10]
        if raw:
            xs[layer] = made[10]

    def forward_lift(layer):
        s = kept[layer]
        s["activated"], s["slope"], s["up"] = chain(
            functools.partial(lift, sections=[section(layer, "up")]), [deep, deep, ((2, width, wide // 2), BF16)],
            held=True, smem=[tab], vmem=[s["middle"], vec[layer]], hbm=parts(layer, "up"), scratch=[dma(8 * chips)],
        )

    def forward_lower(layer):
        s = kept[layer]
        last_one = layer == layers - 1
        shape = hidden.shape if last_one else (tall, width)
        output, s["unit_two"], s["scale_two"], s["down"] = chain(
            functools.partial(lower, sections=[section(layer, "down")], seq=seq),
            [(shape, BF16), row(F32), column, ((wide, width), BF16)],
            held=True, smem=[tab], vmem=[s["activated"], s["middle"], vec[layer]], hbm=parts(layer, "down"),
            scratch=[dma(8 * chips)] + [vmem(shape, F32)] * last_one,
        )
        xs.append(output)

    begin()
    first_stack(0)
    second_stack(0)
    first_stack(1)
    far_round(2)
    third(0)
    vec = chain(
        place_vectors, [((8 + wide // width, width), F32)] * layers, smem=[tab], hbm=near[0],
        scratch=[vmem((chips, block[0], side), BF16), dma(2)],
    )
    second_stack(1)
    first_stack(2)
    far_round(3)
    forward_attend(0)
    third(1)
    second_stack(2)
    first_stack(3)
    far_round(4)
    forward_lift(0)
    third(2)
    second_stack(3)
    first_stack(4)
    far_round(5)
    forward_lower(0)
    first_stack(5)
    third(3)
    second_stack(4)
    forward_attend(1)
    third(4)
    second_stack(5)
    forward_lift(1)
    third(5)
    forward_lower(1)

    keep, came, fanned, last = {}, {}, {}, {}
    sums = [{} for _ in range(layers)]
    flowing = [None] * (layers + 1)
    flowing[layers] = cotangent
    pair = lambda extra=0: [((chips, block[0], block[1] + extra), BF16)] * 2

    def leave(piece, send, kept_blocks):
        keep[piece] = kept_blocks
        came[piece] = core_flip(send)

    def back_feed(layer):
        s = kept[layer]
        raw = flowing[layer + 1].shape[0] != tall
        s["sum_grad"], s["lifted_grad"], d_send, d_keep, u_send, u_keep, sums[layer]["feed"] = chain(
            functools.partial(feed_back, seq=seq), [row(F32), deep] + pair() * 2 + [((16, width), F32)], held=True,
            smem=[tab],
            vmem=[flowing[layer + 1], s["unit_two"], s["scale_two"], vec[layer], s["activated"], s["down"], s["slope"],
                  s["middle"]],
            late=(5, 6, 7),
            scratch=[vmem((width, tall), BF16), vmem((2, tall, width // 2), BF16)] + [vmem((tall, width), F32)] * raw,
        )
        leave((layer, "down"), d_send, d_keep)
        leave((layer, "up"), u_send, u_keep)

    def back_norm(layer):
        s = kept[layer]
        s["first_grad"], s["attended_grad"], sums[layer]["norm"] = chain(
            first_norm_back, [row(F32), ((2, tall, width // 2), BF16), ((8, width), F32)], held=True,
            vmem=[s["lifted_grad"], s["up"], s["sum_grad"], s["unit_one"], s["scale_one"], vec[layer]],
        )

    def back_attend(layer):
        s = kept[layer]
        more, room = [], []
        if layer == 0:
            more = [sums[0]["feed"], sums[0]["norm"], sums[1]["feed"], sums[1]["norm"], sums[1]["four"]]
            room = [vmem((16, width), F32), vmem((2 * wide // width, width), F32)]
        send, rest, sums[layer]["four"], s["grads"] = chain(
            attend_back, pair(0 if layer else side) + [((8, width), F32), ((2, tall, 2 * width), BF16)], held=True,
            smem=[tab],
            vmem=[s["attended_grad"], s["o"], s["q"], s["k"], s["v"], s["p"], xs[layer], s["context"]] + more,
            scratch=[vmem((width, tall), BF16)] * 2 + [vmem((tall, width), BF16)] + room,
        )
        leave((layer, "four"), send, rest)

    def back_last(layer):
        s = kept[layer]
        shape = (tall, width) if layer else hidden.shape
        (flowing[layer],) = chain(
            functools.partial(attend_back_last, seq=seq), [(shape, F32)], held=True,
            vmem=[s["first_grad"], s["grads"], s["three"]],
        )

    def fold(*pieces, after=()):
        half = keep[pieces[0]].shape[0] // 2
        r, c = keep[pieces[0]].shape[1:]
        at = pieces if len(pieces) > 1 else pieces[0]
        send, keep[at] = chain(add_halves, [((half, r * len(pieces), c), BF16)] * 2, vmem=[v for piece in pieces for v in (keep[piece], came[piece])], after=after)
        came[at] = xy_two(send) if half == 2 * depth else xy_one(send)

    def fan(*ats, after=()):
        at = ats[0] if len(ats) == 1 else sum((a if isinstance(a[0], tuple) else (a,) for a in ats), ())
        shape = (sum(keep[a].shape[1] for a in ats), keep[ats[0]].shape[2])
        made = chain(add_spread, [(shape, F32)] + [(shape, BF16)] * (depth - 1), vmem=[v for a in ats for v in (keep[a], came[a])], after=after)
        keep[at] = made[0]
        fanned[at] = [z_flip(made[k], k) for k in range(1, depth)]

    def total(at, after=()):
        pieces = at if isinstance(at[0], tuple) else (at,)
        shape = keep[at].shape
        made = chain(
            functools.partial(add_last, kinds=tuple(kind for _, kind in pieces)), [((shape[0] // 2, shape[1]), F32)] * 2,
            smem=[tab], vmem=[keep[at]] + fanned[at], scratch=[vmem(shape, F32)], after=after,
        )
        both = [made[0], core_flip(made[1])]
        for i, piece in enumerate(pieces):
            last[piece] = (both, i)
        return both[1:]

    def finished(kind, count):
        own_rows = down_weight.shape[1] if kind == "down" else rows
        columns = wide if kind == "up" else width
        outs = [((layers, own_rows, columns), F32)] * count
        if kind == "four":
            outs += [(v.shape, F32) for v in order]
        return chain(
            functools.partial(write_out, kind=kind, sections=[last[layer, kind][1] for layer in range(layers)]), outs,
            smem=[tab], vmem=[v for layer in range(layers) for v in last[layer, kind][0]],
        )

    d1, u1, f1, d0, u0, f0 = [(layer, kind) for layer in (1, 0) for kind in ("down", "up", "four")]
    back_feed(1)
    back_norm(1)
    fold(d1, u1)
    back_attend(1)
    back_last(1)
    fold(f1)
    back_feed(0)
    fold((d1, u1))
    fold(f1)
    back_norm(0)
    fold(d0, u0)
    back_attend(0)
    fan((d1, u1), f1)
    fold(f0)
    back_last(0)
    fold((d0, u0))
    done = total((d1, u1, f1))
    fan((d0, u0))
    fold(f0, after=done)
    total((d0, u0))
    fan(f0)
    (down_grad,) = finished("down", 1)
    total(f0)
    (up_grad,) = finished("up", 1)
    grads = finished("four", 4)
    q_b, v_b, o_b, g_one, s_one, d_b, g_two, s_two, u_b = grads[4:]
    return (
        xs[-1], flowing[0], *grads[:4],
        q_b, v_b, o_b, g_one, s_one, up_grad, u_b, down_grad, d_b, g_two, s_two,
    )


def shards(
    hidden, region_count, text_mask,
    q_weight, k_weight, v_weight, o_weight, q_bias, v_bias, o_bias, gain_one, shift_one,
    up_weight, up_bias, down_weight, down_bias, gain_two, shift_two, cotangent,
):
    owners = lax.axis_size("dp")
    valid_keys = slot_valid(region_count, text_mask)
    weights = (q_weight, k_weight, v_weight, o_weight, up_weight, down_weight)
    small = (q_bias, v_bias, o_bias, gain_one, shift_one, up_bias, down_bias, gain_two, shift_two)
    seq = valid_keys.shape[1]
    width = hidden.shape[1]
    fits = (
        owners in (16, 32)
        and q_weight.shape[1] % 8 == 0
        and up_weight.shape[2] % (2 * width) == 0
        and seq <= ITEM
        and q_weight.shape[0] == 2
    )
    if not fits:
        return plain(weights, small, valid_keys, hidden, cotangent)
    mask = (valid_keys - 1.0) * 10000.0
    mask = jnp.pad(mask, ((0, 0), (0, ITEM - seq)), constant_values=PAD)[:, None, :]
    return blocks(weights, small, mask, hidden, cotangent, seq)


def solution(mesh):
    rows = P("dp", None)
    matrix = P(None, "dp", None)
    vector = P(None, "dp")
    four = (matrix,) * 4
    return jax.shard_map(
        shards,
        mesh=mesh,
        in_specs=(rows, P("dp"), rows) + four + (vector,) * 5
        + (matrix, vector, matrix, vector, vector, vector, rows),
        out_specs=(rows, rows) + four + (vector,) * 5
        + (matrix, vector, matrix, vector, vector, vector),
        check_vma=False,
    )
```
